32 devices in a mesh: dp: 8 (over z, x), fsdp: 4 (over y, core).
Axes of the slice: x: 2, y: 2, z: 4, core: 2. Of those that a mesh axis runs over, the one named last changes fastest.
Arguments:
- signal: bfloat16 [4, 32768, 512], P('fsdp', 'dp'), may hold values from -6 to 6
- cond: bfloat16 [4, 80, 32768], P('fsdp', None, 'dp'), may hold values from -6 to 6
- clip_lengths: int32 [4, 16], P('fsdp'), may hold values from 1 to 28673, 32768 in all within a row
- dilation: int32 [4], P('fsdp'), may hold values from 1 to 512, as said below
- w_conv: bfloat16 [2, 512, 1024], P(None, ('dp', 'fsdp')), may hold values from -0.1875 to 0.1875
- w_cond: bfloat16 [80, 1024], P(None, ('dp', 'fsdp')), may hold values from -0.625 to 0.625
- b_conv: bfloat16 [1024], P(('dp', 'fsdp')), may hold values from -3 to 3
- w_res: bfloat16 [512, 512], P(('dp', 'fsdp')), may hold values from -0.5 to 0.5
- b_res: bfloat16 [512], P(('dp', 'fsdp')), may hold values from -3 to 3
- w_skip: bfloat16 [512, 512], P(('dp', 'fsdp')), may hold values from -0.5 to 0.5
- b_skip: bfloat16 [512], P(('dp', 'fsdp')), may hold values from -3 to 3
- cot_res: bfloat16 [4, 32768, 512], P('fsdp', 'dp'), may hold values from -6 to 6
- cot_skip: bfloat16 [4, 32768, 512], P('fsdp', 'dp'), may hold values from -6 to 6
Outputs:
- res_out: bfloat16 [4, 32768, 512], P('fsdp', 'dp')
- skip_out: bfloat16 [4, 32768, 512], P('fsdp', 'dp')
- grad_signal: float32 [4, 32768, 512], P('fsdp', 'dp')
- grad_w_conv: float32 [2, 512, 1024], P(None, ('dp', 'fsdp'))
- grad_w_cond: float32 [80, 1024], P(None, ('dp', 'fsdp'))
- grad_b_conv: float32 [1024], P(('dp', 'fsdp'))
- grad_w_res: float32 [512, 512], P(('dp', 'fsdp'))
- grad_b_res: float32 [512], P(('dp', 'fsdp'))
- grad_w_skip: float32 [512, 512], P(('dp', 'fsdp'))
- grad_b_skip: float32 [512], P(('dp', 'fsdp'))
The draws below stay inside these ranges and needn't reach their ends.
Inputs may be any that keep to these rules, and one draw needn't show every extreme that they name: `clip_lengths`: each row sums to 32768; in each stream one clip is exactly 28673 samples long. Some stream has dilation exactly 512.
All inputs are finite; a program needn't handle non-finite values.
Results may differ from the reference program's by a relative error of at most 0.0044.
Values may be sent and summed in bfloat16 or wider, within the bound.
A program may use at most 128 MiB of HBM per device.

```python
import math
import jax
import jax.numpy as jnp
import numpy as np
from jax import lax

RC = 512
SC = 512
CC = 80
DMAX = 512
TOK_DEV = 4096
CLIPS = 16
STREAMS = 4
STREAM = 32768


def draw_dilation(key, part):
    key = jax.random.fold_in(key, 11)
    first, second = jax.random.split(key)
    values = jax.random.randint(first, (STREAMS,), 1, DMAX + 1, dtype=jnp.int32)
    chosen = jax.random.randint(second, (), 0, STREAMS, dtype=jnp.int32)
    return jnp.where(jnp.arange(STREAMS, dtype=jnp.int32) == chosen, DMAX, values).astype(jnp.int32)


def level_of(key, shape, cuts, smallest, high):
    gain, own = 1.0, jax.random.fold_in(key, 6)
    for position, blocks in cuts:
        heights = jnp.exp(jax.random.uniform(jax.random.fold_in(own, position), (blocks,), jnp.float32, smallest / len(cuts), high / len(cuts)))
        gain = gain * jnp.repeat(heights, shape[position] // blocks).reshape([-1 if axis == position else 1 for axis in range(len(shape))])
    return gain


def split_up(number_of, total, reach, skew):
    loads = [(1 << 20) // math.isqrt(rank ** skew) + 1 for rank in range(2, number_of + 1)]
    rest, counts = total - reach - (number_of - 1), [1] * (number_of - 1)
    while rest > 0:
        candidates = [i for i in range(number_of - 1) if counts[i] < reach]
        pool, left = sum([loads[i] for i in candidates]), rest
        for i in candidates:
            extra = min(reach - counts[i], max(1, left * loads[i] // pool), rest)
            counts[i] = counts[i] + extra
            rest = rest - extra
    return np.array([reach] + counts)


def uneven_parts(rng, number_of, total, limit, slope):
    if number_of == 2:
        one = jax.random.randint(rng, (), max(1, total - limit), min(limit, total - 1) + 1)
        return jnp.stack([one, total - one])
    tallies = jnp.asarray(split_up(number_of, total, limit, slope), jnp.int32)
    couples = (number_of - 1) // 2
    donor, taker = tallies[1:1 + 2 * couples:2], tallies[2:2 + 2 * couples:2]
    slack = jnp.minimum(donor - 1, limit - taker)
    passed = jax.random.randint(jax.random.fold_in(rng, 1), (couples,), 0, 1 << 20) % (slack + 1)
    tallies = tallies.at[1:1 + 2 * couples:2].set(donor - passed).at[2:2 + 2 * couples:2].set(taker + passed)
    return tallies[jax.random.permutation(jax.random.fold_in(rng, 2), number_of)]


def bell_draw(rng, extent, deviation, reach, cuts=(), held_as=jnp.bfloat16):
    values = jax.random.normal(rng, extent, jnp.float32) * deviation
    if len(cuts) > 0:
        values = level_of(rng, extent, cuts, -0.22, 0.18) * values
    return jnp.clip(values, min=-reach, max=reach).astype(held_as)


def setup_inputs(seed: int = 0) -> dict:
    key_list = jax.random.split(jax.random.key(seed), 14)
    signal = bell_draw(key_list[0], (STREAMS, STREAM, RC), 1.0, 6.0, ((0, 4), (1, 8)))
    cond = bell_draw(key_list[1], (STREAMS, CC, STREAM), 1.0, 6.0, ((0, 4), (2, 8)))
    clip_lengths = jax.vmap(lambda own: uneven_parts(own, CLIPS, STREAM, STREAM - TOK_DEV + 1, 2))(jax.random.split(key_list[2], STREAMS)).reshape((STREAMS, CLIPS)).astype(jnp.int32)
    dilation = draw_dilation(jax.random.fold_in(key_list[13], 71), 0)
    w_conv = bell_draw(key_list[4], (2, RC, 2 * RC), (2 * RC) ** -0.5, 0.1875, ((1, 32),))
    w_cond = bell_draw(key_list[5], (CC, 2 * RC), CC ** -0.5, 0.625, ((1, 32),))
    b_conv = bell_draw(key_list[6], (2 * RC,), 0.5, 3.0, ((0, 32),))
    w_res = bell_draw(key_list[7], (RC, RC), (RC // 4) ** -0.5, 0.5, ((0, 32),))
    b_res = bell_draw(key_list[8], (RC,), 0.5, 3.0, ((0, 32),))
    w_skip = bell_draw(key_list[9], (RC, SC), (RC // 4) ** -0.5, 0.5, ((0, 32),))
    b_skip = bell_draw(key_list[10], (SC,), 0.5, 3.0, ((0, 32),))
    cot_res = bell_draw(key_list[11], (STREAMS, STREAM, RC), 1.0, 6.0, ((0, 4), (1, 8)))
    cot_skip = bell_draw(key_list[12], (STREAMS, STREAM, SC), 1.0, 6.0, ((0, 4), (1, 8)))
    return dict(signal=signal, cond=cond, clip_lengths=clip_lengths, dilation=dilation, w_conv=w_conv, w_cond=w_cond, b_conv=b_conv, w_res=w_res, b_res=b_res, w_skip=w_skip, b_skip=b_skip, cot_res=cot_res, cot_skip=cot_skip)


@jax.custom_vjp
def low(v):
    return lax.optimization_barrier(v.astype(jnp.bfloat16)).astype(jnp.float32)

@jax.custom_vjp
def low_back(v):
    return v

def low_keep(v):
    return (low(v), None)

def low_pass(kept, grad):
    return (grad,)

def back_keep(v):
    return (v, None)

def back_low(kept, grad):
    return (low(grad),)
low.defvjp(low_keep, low_pass)
low_back.defvjp(back_keep, back_low)

def product(left, right):
    return jnp.dot(left, right, precision=lax.Precision.HIGHEST)

def lag_mask(lengths, dilate, total):
    starts = (jnp.cumsum(lengths) - lengths).astype(jnp.int32)
    times = jnp.arange(total, dtype=jnp.int32)
    begin = lax.optimization_barrier(jnp.max(jnp.where(starts[None, :] <= times[:, None], starts[None, :], 0), axis=1)).astype(jnp.int32)
    return (times - begin >= dilate).astype(jnp.float32)

def forward(signal, conds, mask, dilate, w_conv, w_cond, b_conv, w_res, b_res, w_skip, b_skip):
    total = signal.shape[0]
    padded = jnp.concatenate([jnp.zeros((DMAX, signal.shape[1]), jnp.float32), signal], 0)
    lagged = lax.dynamic_slice_in_dim(padded, (DMAX - dilate).astype(jnp.int32), total, 0) * mask[:, None]
    preact = product(lagged, w_conv[0]) + product(signal, w_conv[1]) + product(conds.T, w_cond) + b_conv
    preact = low_back(preact)
    gated = low(jnp.tanh(preact[:, :RC]) * jax.nn.sigmoid(preact[:, RC:]))
    residual = signal + product(gated, w_res) + b_res
    skipped = product(gated, w_skip) + b_skip
    return (residual, skipped)

def reference(signal, cond, clip_lengths, dilation, w_conv, w_cond, b_conv, w_res, b_res, w_skip, b_skip, cot_res, cot_skip):
    weights = (w_conv.astype(jnp.float32), w_cond.astype(jnp.float32), b_conv.astype(jnp.float32), w_res.astype(jnp.float32), b_res.astype(jnp.float32), w_skip.astype(jnp.float32), b_skip.astype(jnp.float32))

    def per_stream(stream_item):
        samples, conds, lengths, dilate, back_res, back_skip = stream_item
        mask = lag_mask(lengths, dilate, samples.shape[0])
        conds = conds.astype(jnp.float32)

        def layer_fn(inputs, *params):
            return forward(inputs, conds, mask, dilate, *params)
        results, pullback = jax.vjp(layer_fn, samples.astype(jnp.float32), *weights)
        gradients = pullback((back_res.astype(jnp.float32), back_skip.astype(jnp.float32)))
        return (results[0].astype(jnp.bfloat16), results[1].astype(jnp.bfloat16), gradients)
    res_out, skip_out, gradients = lax.map(per_stream, (signal, cond, clip_lengths, dilation, cot_res, cot_skip))
    summed = [lax.optimization_barrier(jnp.sum(g, axis=0)) for g in gradients[1:]]
    return (res_out, skip_out, gradients[0], summed[0], summed[1], summed[2], summed[3], summed[4], summed[5], summed[6])
```

```python
import functools

import jax
import jax.numpy as jnp
from jax import lax
from jax.experimental import pallas as pl
from jax.experimental.pallas import tpu as pltpu
from jax.sharding import PartitionSpec as P

DMAX = 512
TILE = 512
MESH = pl.DeviceIdType.MESH
BF16 = jnp.bfloat16
F32 = jnp.float32


def matmul(left, right):
    return jnp.dot(left, right, preferred_element_type=F32)


def contract_first(left, right):
    return lax.dot_general(left, right, (((0,), (0,)), ((), ())), preferred_element_type=F32)


def contract_last(left, right):
    return lax.dot_general(left, right, (((1,), (1,)), ((), ())), preferred_element_type=F32)


def bias_places(skip):
    n = lax.broadcasted_iota(jnp.int32, (512, 1024), 0)
    m = lax.broadcasted_iota(jnp.int32, (512, 1024), 1)
    place = (n // 16) * 32 + n % 16 + 16 * skip
    return jnp.where(place == m, 1.0, 0.0).astype(BF16)


def layer_kernel(
    clip_ref, dil_ref, wconv_ref, wres_ref, wskip_ref, wb_ref, sig_hbm, cond_hbm, cr_hbm, cs_hbm,
    gated_hbm, e_hbm, wrs_hbm, bias_ref, gconv_ref, gres_ref, gskip_ref, gcond_ref,
    X, D, condv, W, WC, wct, F, halo, ret_send, ret_recv,
    Gt, GA, CS, CR, S1, R1, S2, R2, S3, R3,
    cGA, cCS, cCR, cS1, cR1, cS2, cR2, cS3, cR3,
    ld, st_g, st_e, st_w, ag_s, ag_r, h_s, h_r, rs_s, rs_r,
):
    T = sig_hbm.shape[0]
    tiles = T // TILE
    dp, fs = lax.axis_index("dp"), lax.axis_index("fsdp")
    z, x, y, c = dp // 2, dp % 2, fs // 2, fs % 2
    x1, y1, c1 = 1 - x, 1 - y, 1 - c
    zs = (z + 1 - 2 * (z % 2), (z + 2) % 4, 3 - z)

    def dev(zz, xx, yy, cc):
        return (zz * 2 + xx, yy * 2 + cc)

    sib, xn, yn = dev(z, x, y, c1), dev(z, x1, y, c), dev(z, x, y1, c)
    zn = [dev(zz, x, y, c) for zz in zs]

    def rcopy(src, dst, ssem, rsem, to):
        return pltpu.make_async_remote_copy(
            src_ref=src, dst_ref=dst, send_sem=ssem, recv_sem=rsem, device_id=to, device_id_type=MESH
        )

    loads = [
        pltpu.make_async_copy(sig_hbm, X.at[1], ld.at[0]),
        pltpu.make_async_copy(cr_hbm, D.at[0], ld.at[1]),
        pltpu.make_async_copy(cs_hbm, D.at[1], ld.at[2]),
        pltpu.make_async_copy(cond_hbm, condv.at[pl.ds(0, 80)], ld.at[3]),
    ]
    for load in loads:
        load.start()

    extra = dp - 1 + 2 * x
    has_extra = (extra >= 0) & (extra < 8)
    barrier = pltpu.get_barrier_semaphore()
    for to in [sib, xn, yn] + zn:
        pl.semaphore_signal(barrier, inc=1, device_id=to, device_id_type=MESH)

    @pl.when(has_extra)
    def _():
        pl.semaphore_signal(barrier, inc=1, device_id=(extra, fs), device_id_type=MESH)
        pl.semaphore_wait(barrier, 7)

    @pl.when(jnp.logical_not(has_extra))
    def _():
        pl.semaphore_wait(barrier, 6)

    W[0, z, x, y, c] = wconv_ref[0]
    W[1, z, x, y, c] = wconv_ref[1]
    W[2, z, x, y, c, :, 0:512] = wres_ref[...]
    W[2, z, x, y, c, :, 512:1024] = wskip_ref[...]
    WC[z, x, y, c] = wb_ref[...]
    sections = (2, 1, 0, 3)

    def along_z(s):
        own = W.at[s, z, x, y, c] if s < 3 else WC.at[z, x, y, c]
        return [rcopy(own, own, ag_s.at[s, k], ag_r.at[s, k], zn[k]) for k in range(3)]

    def along_one(s):
        if s < 3:
            a, b = W.at[s, :, x, y, c, :, pl.ds(0, 512)], W.at[s, :, x, y, c, :, pl.ds(512, 512)]
            return [
                rcopy(a, a, ag_s.at[s, 3], ag_r.at[s, 3], xn),
                rcopy(b, b, ag_s.at[s, 4], ag_r.at[s, 4], yn),
            ]
        a = WC.at[:, x, y, c]
        return [rcopy(a, a, ag_s.at[s, 3], ag_r.at[s, 3], xn)]

    def along_other(s):
        if s < 3:
            a, b = W.at[s, :, :, y, c, :, pl.ds(0, 512)], W.at[s, :, x, :, c, :, pl.ds(512, 512)]
            return [
                rcopy(a, a, ag_s.at[s, 5], ag_r.at[s, 5], yn),
                rcopy(b, b, ag_s.at[s, 6], ag_r.at[s, 6], xn),
            ]
        a = WC.at[:, :, y, c]
        return [rcopy(a, a, ag_s.at[s, 5], ag_r.at[s, 5], yn)]

    def along_core(s):
        a = W.at[s, :, :, :, c] if s < 3 else WC.at[:, :, :, c]
        return [rcopy(a, a, ag_s.at[s, 7], ag_r.at[s, 7], sib)]

    def start(copies):
        for copy in copies:
            copy.start()

    def wait(copies):
        for copy in copies:
            copy.wait()

    for s in sections:
        start(along_z(s))

    dilate = dil_ref[0]
    lane = lax.broadcasted_iota(jnp.int32, (1, 128), 1)
    starts = jnp.zeros((1, 128), jnp.int32)
    for i in range(16):
        starts = starts + jnp.where(lane > i, clip_ref[0, i], 0)
    row = lax.broadcasted_iota(jnp.int32, (TILE, 128), 0)

    def keep(i):
        times = dp * T + i * TILE + row
        inside = (starts <= times) & (starts > times - dilate)
        return 1.0 - jnp.max(jnp.where(inside, 1.0, 0.0), axis=1, keepdims=True)

    def at(i):
        return pl.ds(pl.multiple_of(i * TILE, TILE), TILE)

    def put(half, value):
        for n in range(4):
            F[n, half * TILE : half * TILE + TILE] = value[:, n * 128 : n * 128 + 128].astype(F32)

    def shifted(first):
        return jnp.concatenate([F[n, pl.ds(first, TILE), :] for n in range(4)], 1)

    def lag_tile(i):
        put(1, X[1, at(i)])
        X[2, at(i)] = (shifted(TILE - dilate) * keep(i)).astype(BF16)

    loads[0].wait()

    def lag_body(i, carry):
        put(0, X[1, at(i - 1)])
        lag_tile(i)
        return carry

    lax.fori_loop(1, 3, lag_body, 0)
    for s in sections:
        wait(along_z(s))
        start(along_one(s))
    lax.fori_loop(3, 6, lag_body, 0)
    for s in sections:
        wait(along_one(s))
        start(along_other(s))

    halo_copy = rcopy(X.at[1, pl.ds(T - DMAX, DMAX)], halo, h_s.at[0], h_r.at[0], (dp + 1, fs))

    @pl.when(dp < 7)
    def _():
        halo_copy.start()

    @pl.when(dp == 0)
    def _():
        halo[...] = jnp.zeros_like(halo)

    @pl.when(dp == 7)
    def _():
        ret_recv[...] = jnp.zeros_like(ret_recv)

    lax.fori_loop(6, tiles, lag_body, 0)
    condv[80:96] = jnp.where(lax.broadcasted_iota(jnp.int32, (16, T), 0) == 0, 1.0, 0.0).astype(BF16)
    condv[96:128] = jnp.zeros((32, T), BF16)
    for load in loads[1:]:
        load.wait()
    for s in sections:
        wait(along_other(s))
        start(along_core(s))

    wait(along_core(2))
    wrs_copy = pltpu.make_async_copy(W.at[2], wrs_hbm, st_w.at[0])
    wrs_copy.start()
    wrs = W[2].reshape(512, 1024)
    wres, wskip = wrs[:, :512], wrs[:, 512:]

    def dg_body(i, carry):
        dg = contract_last(D[0, at(i)], wres) + contract_last(D[1, at(i)], wskip)
        high = dg.astype(BF16)
        D[2, at(i)] = high
        D[3, at(i)] = (dg - high.astype(F32)).astype(BF16)
        return carry

    lax.fori_loop(0, tiles, dg_body, 0)

    for s in (1, 0, 3):
        wait(along_core(s))
    wct[...] = WC[...].reshape(1024, 128).T
    biases = wct[80:96]
    bias_ref[:, 0:512] = contract_last(biases, bias_places(0))
    bias_ref[:, 512:1024] = contract_last(biases, bias_places(1))

    def gated_copy(i):
        return pltpu.make_async_copy(X.at[0, at(i)], gated_hbm.at[at(i)], st_g.at[i])

    def forward_body(j, carry):
        i = j % tiles

        @pl.when(j == tiles)
        def _():
            @pl.when(dp > 0)
            def _():
                halo_copy.wait_recv()

            put(0, halo[...])
            lag_tile(i)

        samples, lagged = X[1, at(i)], X[2, at(i)]
        w0, w1 = W[0].reshape(512, 1024), W[1].reshape(512, 1024)
        preact = matmul(lagged, w0) + matmul(samples, w1) + contract_first(condv[:, at(i)], wct[...])
        a = jnp.tanh(preact[:, :512])
        g = 0.5 * jnp.tanh(0.5 * preact[:, 512:]) + 0.5
        X[0, at(i)] = (a * g).astype(BF16)
        gated_copy(i).start()
        dg = D[2, at(i)].astype(F32) + D[3, at(i)].astype(F32)
        t = dg * g
        D[2, at(i)] = (t * (1.0 - a * a)).astype(BF16)
        D[3, at(i)] = (t * a * (1.0 - g)).astype(BF16)
        return carry

    lax.fori_loop(1, tiles + 1, forward_body, 0)

    def back(i, s):
        w = W[s].reshape(512, 1024)
        return contract_last(D[2, at(i)], w[:, :512]) + contract_last(D[3, at(i)], w[:, 512:])

    ret_send[...] = (back(0, 0) * keep(0)).astype(BF16)
    ret_copy = rcopy(ret_send, ret_recv, h_s.at[1], h_r.at[1], (dp - 1, fs))

    @pl.when(dp > 0)
    def _():
        ret_copy.start()

    def stage0(k):
        CS[k] = Gt[:, :, :, c1].astype(BF16)
        GA[k] = Gt[:, :, :, c]
        rcopy(CS.at[k], CR.at[k], rs_s.at[k, 0], rs_r.at[k, 0], sib).start()

    def stage1(k):
        rcopy(CS.at[k], CR.at[k], rs_s.at[k, 0], rs_r.at[k, 0], sib).wait()

        @pl.when(k % 2 == 0)
        def _():
            S1[k] = (GA[k, :, :, y1] + CR[k, :, :, y1].astype(F32)).astype(BF16)
            GA[k, :, :, y] += CR[k, :, :, y].astype(F32)
            rcopy(S1.at[k], R1.at[k], rs_s.at[k, 1], rs_r.at[k, 1], yn).start()

        @pl.when(k % 2 == 1)
        def _():
            S1[k] = (GA[k, :, x1] + CR[k, :, x1].astype(F32)).astype(BF16)
            GA[k, :, x] += CR[k, :, x].astype(F32)
            rcopy(S1.at[k], R1.at[k], rs_s.at[k, 1], rs_r.at[k, 1], xn).start()

    def stage2(k):
        rcopy(S1.at[k], R1.at[k], rs_s.at[k, 1], rs_r.at[k, 1], yn).wait()

        @pl.when(k % 2 == 0)
        def _():
            S2[k] = (GA[k, :, x1, y] + R1[k, :, x1].astype(F32)).astype(BF16)
            GA[k, :, x, y] += R1[k, :, x].astype(F32)
            rcopy(S2.at[k], R2.at[k], rs_s.at[k, 2], rs_r.at[k, 2], xn).start()

        @pl.when(k % 2 == 1)
        def _():
            S2[k] = (GA[k, :, x, y1] + R1[k, :, y1].astype(F32)).astype(BF16)
            GA[k, :, x, y] += R1[k, :, y].astype(F32)
            rcopy(S2.at[k], R2.at[k], rs_s.at[k, 2], rs_r.at[k, 2], yn).start()

    def z_copies(k):
        return [
            rcopy(S3.at[k, zs[n]], R3.at[k, n], rs_s.at[k, 3 + n], rs_r.at[k, 3 + n], zn[n]) for n in range(3)
        ]

    def stage3(k):
        rcopy(S2.at[k], R2.at[k], rs_s.at[k, 2], rs_r.at[k, 2], xn).wait()
        total = GA[k, :, x, y] + R2[k].astype(F32)
        GA[k, :, x, y] = total
        S3[k] = total.astype(BF16)
        start(z_copies(k))

    def stage4(k):
        wait(z_copies(k))
        total = GA[k, z, x, y]
        for n in range(3):
            total = total + R3[k, n].astype(F32)
        return total

    def c0():
        return rcopy(cCS, cCR, rs_s.at[6, 0], rs_r.at[6, 0], sib)

    def c1_():
        return rcopy(cS1, cR1, rs_s.at[6, 1], rs_r.at[6, 1], yn)

    def c2():
        return rcopy(cS2, cR2, rs_s.at[6, 2], rs_r.at[6, 2], xn)

    def c3():
        return [rcopy(cS3.at[zs[n]], cR3.at[n], rs_s.at[6, 3 + n], rs_r.at[6, 3 + n], zn[n]) for n in range(3)]

    def cond_body(i, total):
        return (
            total[0] + matmul(condv[:, at(i)], D[2, at(i)]),
            total[1] + matmul(condv[:, at(i)], D[3, at(i)]),
        )

    zero = jnp.zeros((128, 512), F32)
    left, right = lax.fori_loop(0, tiles, cond_body, (zero, zero))

    def sums_body(i, total):
        return (
            total[0] + jnp.sum(D[0, at(i)].astype(F32), axis=0, keepdims=True),
            total[1] + jnp.sum(D[1, at(i)].astype(F32), axis=0, keepdims=True),
        )

    zero = jnp.zeros((1, 512), F32)
    bres, bskip = lax.fori_loop(0, tiles, sums_body, (zero, zero))

    def three_parts(value):
        parts = []
        for _ in range(3):
            parts.append(value.astype(BF16))
            value = value - parts[-1].astype(F32)
        return jnp.concatenate(parts + [jnp.zeros((13, 512), BF16)], 0)

    bias_row = matmul(three_parts(bres), bias_places(0)) + matmul(three_parts(bskip), bias_places(1))
    bias_row = jnp.sum(bias_row, axis=0, keepdims=True)
    grad_cond = jnp.concatenate([left, right], 1)
    rows128 = lax.broadcasted_iota(jnp.int32, (128, 1024), 0)
    grad_cond = jnp.where(rows128 == 81, bias_row, grad_cond)
    gct = grad_cond.T.reshape(4, 2, 2, 2, 32, 128)
    cGA[...] = gct
    cCS[...] = cGA[:, :, :, c1]
    c0().start()

    def cond_stage1():
        c0().wait()
        cS1[...] = cGA[:, :, y1, c] + cCR[:, :, y1]
        cGA[:, :, y, c] += cCR[:, :, y]
        c1_().start()

    def cond_stage2():
        c1_().wait()
        cS2[...] = cGA[:, x1, y, c] + cR1[:, x1]
        cGA[:, x, y, c] += cR1[:, x]
        c2().start()

    def cond_stage3():
        c2().wait()
        total = cGA[:, x, y, c] + cR2[...]
        cGA[:, x, y, c] = total
        cS3[...] = total
        start(c3())

    def cond_stage4():
        wait(c3())
        total = cGA[z, x, y, c]
        for n in range(3):
            total = total + cR3[n]
        gcond_ref[...] = total

    def chunk_body(k, carry):
        left, right = k // 2, k % 2 + 2 * ((k + 4) // 6)

        def part(q, carry):
            rows = pl.ds(pl.multiple_of(q * 1024, 1024), 1024)
            prod = contract_first(X[left, rows], D[right, rows]).reshape(4, 2, 2, 2, 16, 512)

            @pl.when(q == 0)
            def _():
                Gt[...] = prod

            @pl.when(q > 0)
            def _():
                Gt[...] += prod

            return carry

        lax.fori_loop(0, T // 1024, part, 0)
        stage0(k)

        @pl.when(k >= 1)
        def _():
            stage1(k - 1)

        @pl.when(k >= 3)
        def _():
            stage2(k - 3)

        @pl.when(k >= 5)
        def _():
            stage3(k - 5)

        @pl.when(k == 1)
        def _():
            cond_stage1()

        @pl.when(k == 3)
        def _():
            cond_stage2()

        @pl.when(k == 5)
        def _():
            cond_stage3()

        return carry

    lax.fori_loop(0, 6, chunk_body, 0)

    @pl.when(dp < 7)
    def _():
        ret_copy.wait_recv()

    put(0, ret_recv[...])

    def e_copy(i):
        return pltpu.make_async_copy(X.at[2, at(i)], e_hbm.at[at(i)], st_e.at[i])

    def e_body(e, carry):
        i = tiles - 1 - e
        F[:, TILE : 2 * TILE] = F[:, 0:TILE]
        put(0, back(i, 0) * keep(i))
        X[2, at(i)] = (back(i, 1) + shifted(dilate)).astype(BF16)
        e_copy(i).start()

        @pl.when(e == 0)
        def _():
            stage1(5)
            stage2(3)

        @pl.when(e == 1)
        def _():
            stage3(1)

        @pl.when(e == 2)
        def _():
            stage3(2)
            stage2(4)

        @pl.when(e == 4)
        def _():
            stage2(5)
            stage3(3)

        @pl.when(e == 6)
        def _():
            stage3(4)

        return carry

    lax.fori_loop(0, tiles, e_body, 0)
    stage3(5)
    cond_stage4()
    for k in range(4):
        gconv_ref[1 - k // 2, :, (k % 2) * 512 : (k % 2) * 512 + 512] = stage4(k + 2)
    gres_ref[...] = stage4(0)
    gskip_ref[...] = stage4(1)

    def finish(i, carry):
        gated_copy(i).wait()
        e_copy(i).wait()
        return carry

    lax.fori_loop(0, tiles, finish, 0)
    wrs_copy.wait()

    @pl.when(dp < 7)
    def _():
        halo_copy.wait_send()

    @pl.when(dp > 0)
    def _():
        ret_copy.wait_send()


def output_kernel(gated_ref, sig_ref, e_ref, cot_ref, w_ref, bias_ref, res_ref, skip_ref, grad_ref):
    gated, w = gated_ref[...], w_ref[...]
    res = sig_ref[...].astype(F32) + matmul(gated, w[:, :512]) + bias_ref[1:2, 0:512]
    res_ref[...] = res.astype(BF16)
    skip_ref[...] = (matmul(gated, w[:, 512:]) + bias_ref[1:2, 512:1024]).astype(BF16)
    grad_ref[...] = cot_ref[...].astype(F32) + e_ref[...].astype(F32)


def shards(
    signal, cond, clip_lengths, dilation, w_conv, w_cond, b_conv, w_res, b_res, w_skip, b_skip, cot_res, cot_skip
):
    T = signal.shape[1]
    tiles = T // TILE
    sig, conds, cr, cs = signal[0], cond[0], cot_res[0], cot_skip[0]
    wb = jnp.concatenate(
        [w_cond.T, b_conv[:, None], jnp.concatenate([b_res, b_skip])[:, None], jnp.zeros((32, 46), BF16)], 1
    )
    vmem, hbm, smem = (pl.BlockSpec(memory_space=m) for m in (pltpu.VMEM, pl.ANY, pltpu.SMEM))
    dma = pltpu.SemaphoreType.DMA
    out = jax.ShapeDtypeStruct
    gated, e, wrs, bias, gconv, gres, gskip, gcond = pl.pallas_call(
        layer_kernel,
        out_shape=[
            out((T, 512), BF16),
            out((T, 512), BF16),
            out((4, 2, 2, 2, 16, 1024), BF16),
            out((16, 1024), F32),
            out((2, 16, 1024), F32),
            out((16, 512), F32),
            out((16, 512), F32),
            out((32, 128), F32),
        ],
        in_specs=[smem, smem] + [vmem] * 4 + [hbm] * 4,
        out_specs=[hbm] * 3 + [vmem] * 5,
        scratch_shapes=[
            pltpu.VMEM((3, T, 512), BF16),
            pltpu.VMEM((4, T, 512), BF16),
            pltpu.VMEM((128, T), BF16),
            pltpu.VMEM((3, 4, 2, 2, 2, 16, 1024), BF16),
            pltpu.VMEM((4, 2, 2, 2, 32, 128), BF16),
            pltpu.VMEM((128, 1024), BF16),
            pltpu.VMEM((4, 2 * TILE, 128), F32),
            pltpu.VMEM((DMAX, 512), BF16),
            pltpu.VMEM((DMAX, 512), BF16),
            pltpu.VMEM((DMAX, 512), BF16),
            pltpu.VMEM((4, 2, 2, 2, 16, 512), F32),
            pltpu.VMEM((6, 4, 2, 2, 16, 512), F32),
            pltpu.VMEM((6, 4, 2, 2, 16, 512), BF16),
            pltpu.VMEM((6, 4, 2, 2, 16, 512), BF16),
            pltpu.VMEM((6, 4, 2, 16, 512), BF16),
            pltpu.VMEM((6, 4, 2, 16, 512), BF16),
            pltpu.VMEM((6, 4, 16, 512), BF16),
            pltpu.VMEM((6, 4, 16, 512), BF16),
            pltpu.VMEM((6, 4, 16, 512), BF16),
            pltpu.VMEM((6, 3, 16, 512), BF16),
            pltpu.VMEM((4, 2, 2, 2, 32, 128), F32),
            pltpu.VMEM((4, 2, 2, 32, 128), F32),
            pltpu.VMEM((4, 2, 2, 32, 128), F32),
            pltpu.VMEM((4, 2, 32, 128), F32),
            pltpu.VMEM((4, 2, 32, 128), F32),
            pltpu.VMEM((4, 32, 128), F32),
            pltpu.VMEM((4, 32, 128), F32),
            pltpu.VMEM((4, 32, 128), F32),
            pltpu.VMEM((3, 32, 128), F32),
            dma((4,)),
            dma((tiles,)),
            dma((tiles,)),
            dma((1,)),
            dma((4, 8)),
            dma((4, 8)),
            dma((2,)),
            dma((2,)),
            dma((7, 6)),
            dma((7, 6)),
        ],
        compiler_params=pltpu.CompilerParams(
            collective_id=0, has_side_effects=True, vmem_limit_bytes=60 << 20
        ),
        name="layer",
    )(clip_lengths, dilation, w_conv, w_res, w_skip, wb, sig, conds, cr, cs)

    rows = pl.BlockSpec((TILE, 512), lambda i: (i, 0))
    res_out, skip_out, grad_signal = pl.pallas_call(
        output_kernel,
        grid=(tiles,),
        in_specs=[rows] * 4
        + [pl.BlockSpec((512, 1024), lambda i: (0, 0)), pl.BlockSpec((16, 1024), lambda i: (0, 0))],
        out_specs=[rows] * 3,
        out_shape=[out((T, 512), BF16), out((T, 512), BF16), out((T, 512), F32)],
        compiler_params=pltpu.CompilerParams(vmem_limit_bytes=60 << 20),
        name="outputs",
    )(gated, sig, e, cr, wrs.reshape(512, 1024), bias)
    return (
        res_out[None],
        skip_out[None],
        grad_signal[None],
        gconv,
        gcond[:, :80].T,
        gcond[:, 80],
        gres,
        gcond[:16, 81],
        gskip,
        gcond[16:, 81],
    )


def from_behind(value, axis, steps):
    count = lax.axis_size(axis)
    first, last = (max(0, -steps), min(count, count - steps))
    return lax.ppermute(value, axis, [(source, source + steps) for source in range(first, last)])


def shards_any(
    signal,
    cond,
    clip_lengths,
    dilation,
    w_conv,
    w_cond,
    b_conv,
    w_res,
    b_res,
    w_skip,
    b_skip,
    cot_res,
    cot_skip,
):
    rows = signal.shape[1]
    chans = signal.shape[2]
    conv_full, cond_full, bconv_full, res_full, bres_full, skip_full, bskip_full = (
        lax.all_gather(w_conv, ("dp", "fsdp"), axis=1, tiled=True),
        lax.all_gather(w_cond, ("dp", "fsdp"), axis=1, tiled=True),
        lax.all_gather(b_conv, ("dp", "fsdp"), axis=0, tiled=True),
        lax.all_gather(w_res, ("dp", "fsdp"), axis=0, tiled=True),
        lax.all_gather(b_res, ("dp", "fsdp"), axis=0, tiled=True),
        lax.all_gather(w_skip, ("dp", "fsdp"), axis=0, tiled=True),
        lax.all_gather(b_skip, ("dp", "fsdp"), axis=0, tiled=True),
    )
    segment = lax.axis_index("dp")
    times = segment * rows + jnp.arange(rows, dtype=jnp.int32)
    lengths = clip_lengths[0]
    starts = jnp.cumsum(lengths) - lengths
    begin = jnp.max(jnp.where(starts[None, :] <= times[:, None], starts[None, :], 0), axis=1)
    dilate = dilation[0]
    keep = times - begin >= dilate
    mask_low = keep.astype(jnp.bfloat16)
    samples = signal[0]
    conds = cond[0]
    tail = from_behind(samples[rows - DMAX :], "dp", 1)
    extended = jnp.concatenate([tail, samples], 0)
    lagged = lax.dynamic_slice_in_dim(extended, DMAX - dilate, rows, 0) * mask_low[:, None]
    preact = (
        matmul(lagged, conv_full[0])
        + matmul(samples, conv_full[1])
        + contract_first(conds, cond_full)
        + bconv_full.astype(jnp.float32)
    )
    half = preact.shape[1] // 2
    tanh_part = jnp.tanh(preact[:, :half])
    sig_part = jax.nn.sigmoid(preact[:, half:])
    gated = (tanh_part * sig_part).astype(jnp.bfloat16)
    res_out = (
        samples.astype(jnp.float32) + matmul(gated, res_full) + bres_full.astype(jnp.float32)
    ).astype(jnp.bfloat16)
    skip_out = (matmul(gated, skip_full) + bskip_full.astype(jnp.float32)).astype(jnp.bfloat16)
    conv_back, cond_back, bconv_back, res_back, bres_back, skip_back, bskip_back = (
        lax.all_gather(w_conv, ("dp", "fsdp"), axis=1, tiled=True),
        lax.all_gather(w_cond, ("dp", "fsdp"), axis=1, tiled=True),
        lax.all_gather(b_conv, ("dp", "fsdp"), axis=0, tiled=True),
        lax.all_gather(w_res, ("dp", "fsdp"), axis=0, tiled=True),
        lax.all_gather(b_res, ("dp", "fsdp"), axis=0, tiled=True),
        lax.all_gather(w_skip, ("dp", "fsdp"), axis=0, tiled=True),
        lax.all_gather(b_skip, ("dp", "fsdp"), axis=0, tiled=True),
    )
    back_res = cot_res[0]
    back_skip = cot_skip[0]
    d_gated = contract_last(back_res, res_back) + contract_last(back_skip, skip_back)
    d_preact = jnp.concatenate(
        [
            d_gated * sig_part * (1.0 - tanh_part * tanh_part),
            d_gated * tanh_part * sig_part * (1.0 - sig_part),
        ],
        1,
    ).astype(jnp.bfloat16)
    grad_res = contract_first(gated, back_res)
    grad_bres = jnp.sum(back_res.astype(jnp.float32), axis=0)
    grad_skip = contract_first(gated, back_skip)
    grad_bskip = jnp.sum(back_skip.astype(jnp.float32), axis=0)
    grad_conv = jnp.stack([contract_first(lagged, d_preact), contract_first(samples, d_preact)])
    grad_cond = matmul(conds, d_preact)
    grad_bconv = jnp.sum(d_preact.astype(jnp.float32), axis=0)
    grad_in = back_res.astype(jnp.float32) + contract_last(d_preact, conv_back[1])
    d_lagged = contract_last(d_preact, conv_back[0]) * keep.astype(jnp.float32)[:, None]
    d_extended = jnp.zeros((DMAX + rows, chans), jnp.float32)
    d_extended = lax.dynamic_update_slice_in_dim(d_extended, d_lagged, DMAX - dilate, 0)
    grad_in = grad_in + d_extended[DMAX:]
    returned = from_behind(d_extended[:DMAX].astype(jnp.bfloat16), "dp", -1).astype(jnp.float32)
    grad_in = grad_in + jnp.concatenate([jnp.zeros((rows - DMAX, chans), jnp.float32), returned], 0)
    sums = (
        lax.psum_scatter(grad_conv, ("dp", "fsdp"), scatter_dimension=1, tiled=True),
        lax.psum_scatter(grad_cond, ("dp", "fsdp"), scatter_dimension=1, tiled=True),
        lax.psum_scatter(grad_bconv, ("dp", "fsdp"), scatter_dimension=0, tiled=True),
        lax.psum_scatter(grad_res, ("dp", "fsdp"), scatter_dimension=0, tiled=True),
        lax.psum_scatter(grad_bres, ("dp", "fsdp"), scatter_dimension=0, tiled=True),
        lax.psum_scatter(grad_skip, ("dp", "fsdp"), scatter_dimension=0, tiled=True),
        lax.psum_scatter(grad_bskip, ("dp", "fsdp"), scatter_dimension=0, tiled=True),
    )
    return (
        res_out[None],
        skip_out[None],
        grad_in[None],
        sums[0],
        sums[1],
        sums[2],
        sums[3],
        sums[4],
        sums[5],
        sums[6],
    )


def solution(mesh):
    return jax.shard_map(
        shards if dict(mesh.shape) == {"dp": 8, "fsdp": 4} else shards_any,
        mesh=mesh,
        in_specs=(
            P("fsdp", "dp", None),
            P("fsdp", None, "dp"),
            P("fsdp", None),
            P("fsdp"),
            P(None, ("dp", "fsdp"), None),
            P(None, ("dp", "fsdp")),
            P(("dp", "fsdp")),
            P(("dp", "fsdp"), None),
            P(("dp", "fsdp")),
            P(("dp", "fsdp"), None),
            P(("dp", "fsdp")),
            P("fsdp", "dp", None),
            P("fsdp", "dp", None),
        ),
        out_specs=(
            P("fsdp", "dp", None),
            P("fsdp", "dp", None),
            P("fsdp", "dp", None),
            P(None, ("dp", "fsdp"), None),
            P(None, ("dp", "fsdp")),
            P(("dp", "fsdp")),
            P(("dp", "fsdp"), None),
            P(("dp", "fsdp")),
            P(("dp", "fsdp"), None),
            P(("dp", "fsdp")),
        ),
        check_vma=False,
    )
```

```python
import functools

import jax
import jax.numpy as jnp
from jax import lax
from jax.experimental import pallas as pl
from jax.experimental.pallas import tpu as pltpu
from jax.sharding import PartitionSpec as P

DMAX = 512
TILE = 512
BIG = 1024
PIECES = 8
MESH = pl.DeviceIdType.MESH
BF16 = jnp.bfloat16
F32 = jnp.float32


def matmul(left, right):
    return jnp.dot(left, right, preferred_element_type=F32)


def contract_first(left, right):
    return lax.dot_general(left, right, (((0,), (0,)), ((), ())), preferred_element_type=F32)


def contract_last(left, right):
    return lax.dot_general(left, right, (((1,), (1,)), ((), ())), preferred_element_type=F32)


def bias_places(skip):
    n = lax.broadcasted_iota(jnp.int32, (512, 1024), 0)
    m = lax.broadcasted_iota(jnp.int32, (512, 1024), 1)
    place = ((n >> 4) << 5) + (n & 15) + 16 * skip
    return jnp.where(place == m, 1.0, 0.0).astype(BF16)


def layer_kernel(
    clip_ref, dil_ref, wconv_ref, wres_ref, wskip_ref, wb_ref, sig_hbm, cond_hbm, cr_hbm, cs_hbm,
    gated_hbm, e_hbm, wrs_hbm, bias_ref, gconv_ref, gres_ref, gskip_ref, gcond_ref,
    X, D, condv, W, WC, wct, F, halo, ret_send, ret_recv,
    Gt, GA, CS, CR, S1, R1, S2, R2, S3, R3,
    cGA, cCS, cCR, cS1, cR1, cS2, cR2, cS3, cR3,
    ld, st_g, st_e, st_w, ag_s, ag_r, h_s, h_r, rs_s, rs_r,
):
    T = sig_hbm.shape[0]
    tiles = T // TILE
    dp, fs = lax.axis_index("dp"), lax.axis_index("fsdp")
    z, x, y, c = dp // 2, dp % 2, fs // 2, fs % 2
    x1, y1, c1 = 1 - x, 1 - y, 1 - c
    zs = (z + 1 - 2 * (z % 2), (z + 2) % 4, 3 - z)

    def dev(zz, xx, yy, cc):
        return (zz * 2 + xx, yy * 2 + cc)

    sib, xn, yn = dev(z, x, y, c1), dev(z, x1, y, c), dev(z, x, y1, c)
    zn = [dev(zz, x, y, c) for zz in zs]

    def rcopy(src, dst, ssem, rsem, to):
        return pltpu.make_async_remote_copy(
            src_ref=src, dst_ref=dst, send_sem=ssem, recv_sem=rsem, device_id=to, device_id_type=MESH
        )

    loads = [
        pltpu.make_async_copy(sig_hbm, X.at[1], ld.at[0]),
        pltpu.make_async_copy(cr_hbm, D.at[0], ld.at[1]),
        pltpu.make_async_copy(cs_hbm, D.at[1], ld.at[2]),
        pltpu.make_async_copy(cond_hbm, condv.at[pl.ds(0, 80)], ld.at[3]),
    ]
    for load in loads:
        load.start()

    extra = dp - 1 + 2 * x
    has_extra = (extra >= 0) & (extra < 8)
    barrier = pltpu.get_barrier_semaphore()
    for to in [sib, xn, yn] + zn:
        pl.semaphore_signal(barrier, inc=1, device_id=to, device_id_type=MESH)

    @pl.when(has_extra)
    def _():
        pl.semaphore_signal(barrier, inc=1, device_id=(extra, fs), device_id_type=MESH)
        pl.semaphore_wait(barrier, 7)

    @pl.when(jnp.logical_not(has_extra))
    def _():
        pl.semaphore_wait(barrier, 6)

    for q in range(2):
        for tap in range(2):
            for n in range(2):
                to = tap * 512 + n * 256
                W[q, z, x, y, c, :, to : to + 256] = wconv_ref[tap, :, n * 512 + q * 256 : n * 512 + q * 256 + 256]
    W[2, z, x, y, c, :, 0:512] = wres_ref[...]
    W[2, z, x, y, c, :, 512:1024] = wskip_ref[...]
    WC[z, x, y, c] = wb_ref[...]

    def along_z(s):
        own = W.at[s, z, x, y, c] if s < 3 else WC.at[z, x, y, c]
        return [rcopy(own, own, ag_s.at[s, k], ag_r.at[s, k], zn[k]) for k in range(3)]

    def along_one(s):
        if s < 3:
            a, b = W.at[s, :, x, y, c, :, pl.ds(0, 512)], W.at[s, :, x, y, c, :, pl.ds(512, 512)]
            return [
                rcopy(a, a, ag_s.at[s, 3], ag_r.at[s, 3], xn),
                rcopy(b, b, ag_s.at[s, 4], ag_r.at[s, 4], yn),
            ]
        a = WC.at[:, x, y, c]
        return [rcopy(a, a, ag_s.at[s, 3], ag_r.at[s, 3], xn)]

    def along_other(s):
        if s < 3:
            a, b = W.at[s, :, :, y, c, :, pl.ds(0, 512)], W.at[s, :, x, :, c, :, pl.ds(512, 512)]
            return [
                rcopy(a, a, ag_s.at[s, 5], ag_r.at[s, 5], yn),
                rcopy(b, b, ag_s.at[s, 6], ag_r.at[s, 6], xn),
            ]
        a = WC.at[:, :, y, c]
        return [rcopy(a, a, ag_s.at[s, 5], ag_r.at[s, 5], yn)]

    def along_core(s):
        a = W.at[s, :, :, :, c] if s < 3 else WC.at[:, :, :, c]
        return [rcopy(a, a, ag_s.at[s, 7], ag_r.at[s, 7], sib)]

    def start(phase, *sections):
        for s in sections:
            for copy in phase(s):
                copy.start()

    def wait(phase, *sections):
        for s in sections:
            for copy in phase(s):
                copy.wait()

    def halo_copy(n):
        size = DMAX // PIECES
        return rcopy(
            X.at[1, pl.ds(T - DMAX + n * size, size)], halo.at[pl.ds(n * size, size)], h_s.at[n], h_r.at[n], (dp + 1, fs)
        )

    def send_halo(first, last):
        @pl.when(dp < 7)
        def _():
            for n in range(first, last):
                halo_copy(n).start()

    start(along_z, 2)

    dilate = dil_ref[0]
    lane = lax.broadcasted_iota(jnp.int32, (1, 128), 1)
    starts = jnp.zeros((1, 128), jnp.int32)
    for i in range(16):
        starts = starts + jnp.where(lane > i, clip_ref[0, i], 0)
    row = lax.broadcasted_iota(jnp.int32, (TILE, 128), 0)

    def keep(i):
        times = dp * T + i * TILE + row
        inside = (starts <= times) & (starts > times - dilate)
        return 1.0 - jnp.max(jnp.where(inside, 1.0, 0.0), axis=1, keepdims=True)

    def at(i, size=TILE):
        return pl.ds(pl.multiple_of(i * size, size), size)

    def put(half, value):
        for n in range(4):
            F[n, half * TILE : half * TILE + TILE] = value[:, n * 128 : n * 128 + 128].astype(F32)

    def shifted(first):
        return jnp.concatenate([F[n, pl.ds(first, TILE), :] for n in range(4)], 1)

    def lag_tile(i):
        put(1, X[1, at(i)])
        X[2, at(i)] = (shifted(TILE - dilate) * keep(i)).astype(BF16)

    def lag_body(i, carry):
        put(0, X[1, at(i - 1)])
        lag_tile(i)
        return carry

    def sums_body(i, total):
        return (
            total[0] + jnp.sum(D[0, at(i)].astype(F32), axis=0, keepdims=True),
            total[1] + jnp.sum(D[1, at(i)].astype(F32), axis=0, keepdims=True),
        )

    def dg_body(i, carry):
        wrs = W[2].reshape(512, 1024)
        rows = at(i, BIG)
        dg = contract_last(D[0, rows], wrs[:, :512]) + contract_last(D[1, rows], wrs[:, 512:])
        high = dg.astype(BF16)
        low = (dg - high.astype(F32)).astype(BF16)
        for q in range(2):
            D[2 + q, rows, 0:256] = high[:, q * 256 : q * 256 + 256]
            D[2 + q, rows, 256:512] = low[:, q * 256 : q * 256 + 256]
        return carry

    loads[0].wait()
    lax.fori_loop(1, 2, lag_body, 0)
    wait(along_z, 2)
    start(along_one, 2)
    start(along_z, 0, 3, 1)
    lax.fori_loop(2, 4, lag_body, 0)
    wait(along_one, 2)
    start(along_other, 2)
    lax.fori_loop(4, 6, lag_body, 0)
    wait(along_z, 0, 3)
    start(along_one, 0, 3)
    wait(along_z, 1)
    start(along_one, 1)
    lax.fori_loop(6, tiles, lag_body, 0)
    wait(along_other, 2)
    start(along_core, 2)
    wait(along_one, 0, 3)
    start(along_other, 0, 3)
    wait(along_one, 1)
    start(along_other, 1)
    for load in loads[1:]:
        load.wait()
    zero = jnp.zeros((1, 512), F32)
    bres, bskip = lax.fori_loop(0, tiles, sums_body, (zero, zero))
    condv[80:96] = jnp.where(lax.broadcasted_iota(jnp.int32, (16, T), 0) == 0, 1.0, 0.0).astype(BF16)
    condv[96:128] = jnp.zeros((32, T), BF16)
    wait(along_core, 2)
    wrs_copy = pltpu.make_async_copy(W.at[2], wrs_hbm, st_w.at[0])
    wrs_copy.start()
    lax.fori_loop(0, T // BIG // 2, dg_body, 0)
    wait(along_other, 0, 3)
    start(along_core, 0, 3)
    lax.fori_loop(T // BIG // 2, T // BIG, dg_body, 0)
    wait(along_other, 1)
    start(along_core, 1)
    send_halo(0, PIECES)

    @pl.when(dp == 0)
    def _():
        halo[...] = jnp.zeros_like(halo)

    @pl.when(dp == 7)
    def _():
        ret_recv[...] = jnp.zeros_like(ret_recv)

    wait(along_core, 0, 3)
    turned = WC[...].reshape(1024, 128).T
    for q in range(2):
        for n in range(2):
            wct[q, :, n * 256 : n * 256 + 256] = turned[:, n * 512 + q * 256 : n * 512 + q * 256 + 256]
    biases = turned[80:96]
    bias_ref[:, 0:512] = contract_last(biases, bias_places(0))
    bias_ref[:, 512:1024] = contract_last(biases, bias_places(1))

    def forward(rows, q):
        w = W[q].reshape(512, 1024)
        preact = (
            matmul(X[2, rows], w[:, :512])
            + matmul(X[1, rows], w[:, 512:])
            + contract_first(condv[:, rows], wct[q])
        )
        a = jnp.tanh(preact[:, :256])
        g = 0.5 * jnp.tanh(0.5 * preact[:, 256:]) + 0.5
        X[0, rows, q * 256 : q * 256 + 256] = (a * g).astype(BF16)
        dg = D[2 + q, rows].astype(F32)
        t = (dg[:, :256] + dg[:, 256:]) * g
        D[2 + q, rows, 0:256] = (t * (1.0 - a * a)).astype(BF16)
        D[2 + q, rows, 256:512] = (t * a * (1.0 - g)).astype(BF16)

    def gated_copy(i):
        return pltpu.make_async_copy(X.at[0, at(i)], gated_hbm.at[at(i)], st_g.at[i])

    whole = (T - TILE) // BIG
    for q in range(2):
        if q == 1:
            wait(along_core, 1)

        def forward_body(j, carry, q=q):
            forward(pl.ds(pl.multiple_of(TILE + j * BIG, TILE), BIG), q)
            if q == 1:
                for n in range(BIG // TILE):
                    gated_copy(1 + j * (BIG // TILE) + n).start()
            return carry

        lax.fori_loop(0, whole, forward_body, 0)
        for i in range(1 + whole * (BIG // TILE), tiles):
            forward(at(i), q)
            if q == 1:
                gated_copy(i).start()

    @pl.when(dp > 0)
    def _():
        for n in range(PIECES):
            halo_copy(n).wait_recv()

    put(0, halo[...])
    lag_tile(0)
    forward(at(0), 0)
    forward(at(0), 1)
    gated_copy(0).start()

    def back(i, tap):
        w0 = W[0].reshape(512, 1024)[:, tap * 512 : tap * 512 + 512]
        w1 = W[1].reshape(512, 1024)[:, tap * 512 : tap * 512 + 512]
        return contract_last(D[2, at(i)], w0) + contract_last(D[3, at(i)], w1)

    first = back(0, 0) * keep(0)
    put(0, first)
    ret_send[...] = first.astype(BF16)

    def ret_copy(n):
        rows = pl.ds(pl.multiple_of(n * (DMAX // PIECES), DMAX // PIECES), DMAX // PIECES)
        return rcopy(ret_send.at[rows], ret_recv.at[rows], h_s.at[PIECES + n], h_r.at[PIECES + n], (dp - 1, fs))

    def send_back(n):
        @pl.when(dp > 0)
        def _():
            ret_copy(n).start()

    def to_core(k):
        return rcopy(CS.at[k], CR.at[k], rs_s.at[k, 0], rs_r.at[k, 0], sib)

    def to_first(k):
        return rcopy(S1.at[k], R1.at[k], rs_s.at[k, 1], rs_r.at[k, 1], yn)

    def to_second(k):
        return rcopy(S2.at[k], R2.at[k], rs_s.at[k, 2], rs_r.at[k, 2], xn)

    def to_z(k):
        return [
            rcopy(S3.at[k, zs[n]], R3.at[k, n], rs_s.at[k, 3 + n], rs_r.at[k, 3 + n], zn[n]) for n in range(3)
        ]

    def stage0(k):
        CS[k] = Gt[:, :, :, c1].astype(BF16)
        GA[k] = Gt[:, :, :, c]
        to_core(k).start()

    def stage1(k):
        to_core(k).wait()
        S1[k] = (GA[k, :, :, y1] + CR[k, :, :, y1].astype(F32)).astype(BF16)
        to_first(k).start()
        GA[k, :, :, y] += CR[k, :, :, y].astype(F32)

    def stage2(k):
        to_first(k).wait()
        S2[k] = (GA[k, :, x1, y] + R1[k, :, x1].astype(F32)).astype(BF16)
        to_second(k).start()
        GA[k, :, x, y] += R1[k, :, x].astype(F32)

    def stage3(k):
        to_second(k).wait()
        total = GA[k, :, x, y] + R2[k].astype(F32)
        S3[k] = total.astype(BF16)
        for copy in to_z(k):
            copy.start()
        GA[k, :, x, y] = total

    def stage4(k):
        for copy in to_z(k):
            copy.wait()
        total = GA[k, z, x, y]
        for n in range(3):
            total = total + R3[k, n].astype(F32)
        return total

    cond_core = rcopy(cCS, cCR, rs_s.at[6, 0], rs_r.at[6, 0], sib)
    cond_first = rcopy(cS1, cR1, rs_s.at[6, 1], rs_r.at[6, 1], yn)
    cond_second = rcopy(cS2, cR2, rs_s.at[6, 2], rs_r.at[6, 2], xn)
    cond_z = [rcopy(cS3.at[zs[n]], cR3.at[n], rs_s.at[6, 3 + n], rs_r.at[6, 3 + n], zn[n]) for n in range(3)]

    def three_parts(value):
        parts = []
        for _ in range(3):
            parts.append(value.astype(BF16))
            value = value - parts[-1].astype(F32)
        return jnp.concatenate(parts + [jnp.zeros((13, 512), BF16)], 0)

    def cond_stage0():
        bias_row = matmul(three_parts(bres), bias_places(0)) + matmul(three_parts(bskip), bias_places(1))
        bias_row = jnp.sum(bias_row, axis=0, keepdims=True)
        one, two = matmul(condv[...], D[2]), matmul(condv[...], D[3])
        grad = jnp.concatenate([one[:, :256], two[:, :256], one[:, 256:], two[:, 256:]], 1)
        place = lax.broadcasted_iota(jnp.int32, (128, 1024), 0)
        cGA[...] = jnp.where(place == 81, bias_row, grad).T.reshape(4, 2, 2, 2, 32, 128)
        cCS[...] = cGA[:, :, :, c1].astype(BF16)
        cond_core.start()

    def cond_stage1():
        cond_core.wait()
        cS1[...] = (cGA[:, :, y1, c] + cCR[:, :, y1].astype(F32)).astype(BF16)
        cond_first.start()
        cGA[:, :, y, c] += cCR[:, :, y].astype(F32)

    def cond_stage2():
        cond_first.wait()
        cS2[...] = (cGA[:, x1, y, c] + cR1[:, x1].astype(F32)).astype(BF16)
        cond_second.start()
        cGA[:, x, y, c] += cR1[:, x].astype(F32)

    def cond_stage3():
        cond_second.wait()
        total = cGA[:, x, y, c] + cR2[...].astype(F32)
        cS3[...] = total.astype(BF16)
        for copy in cond_z:
            copy.start()
        cGA[:, x, y, c] = total

    def cond_stage4():
        for copy in cond_z:
            copy.wait()
        total = cGA[z, x, y, c]
        for n in range(3):
            total = total + cR3[n].astype(F32)
        gcond_ref[...] = total

    def when(condition, work, *args):
        @pl.when(condition)
        def _():
            work(*args)

    cond_stage0()

    def chunk_body(k, carry):
        left, right = k // 2, k % 2 + 2 * ((k + 4) // 6)
        Gt[...] = contract_first(X[left], D[right]).reshape(4, 2, 2, 2, 16, 512)
        stage0(k)
        when(k >= 1, stage1, k - 1)
        when(k >= 3, stage2, k - 3)
        when(k >= 5, stage3, k - 5)
        when(k == 0, cond_stage1)
        when(k == 2, cond_stage2)
        when(k == 4, cond_stage3)
        send_back(k)
        return carry

    lax.fori_loop(0, 6, chunk_body, 0)

    def e_copy(i):
        return pltpu.make_async_copy(X.at[2, at(i)], e_hbm.at[at(i)], st_e.at[i])

    def e_tile(i):
        X[2, at(i)] = (back(i, 1) + shifted(dilate)).astype(BF16)
        e_copy(i).start()

    def e_body(e, carry):
        put(1, back(e + 1, 0) * keep(e + 1))
        e_tile(e)
        F[:, 0:TILE] = F[:, TILE : 2 * TILE]
        when(e == 0, stage1, 5)
        when(e == 0, stage2, 3)
        when(e == 1, stage3, 1)
        when(e == 1, stage2, 4)
        when(e == 2, stage3, 2)
        when(e == 3, stage2, 5)
        when(e == 4, stage3, 3)
        when(e == 5, stage3, 4)
        when(e == 6, stage3, 5)
        when(e < PIECES - 6, send_back, e + 6)
        return carry

    lax.fori_loop(0, tiles - 1, e_body, 0)

    @pl.when(dp < 7)
    def _():
        for n in range(PIECES):
            ret_copy(n).wait_recv()

    put(1, ret_recv[...])
    e_tile(tiles - 1)
    cond_stage4()
    gres_ref[...] = stage4(0)
    gskip_ref[...] = stage4(1)
    for k in range(2, 6):
        total, q = stage4(k), k % 2
        for n in range(2):
            to = n * 512 + q * 256
            gconv_ref[1 - (k - 2) // 2, :, to : to + 256] = total[:, n * 256 : n * 256 + 256]

    def finish(i, carry):
        gated_copy(i).wait()
        e_copy(i).wait()
        return carry

    lax.fori_loop(0, tiles, finish, 0)
    wrs_copy.wait()

    @pl.when(dp < 7)
    def _():
        for n in range(PIECES):
            halo_copy(n).wait_send()

    @pl.when(dp > 0)
    def _():
        for n in range(PIECES):
            ret_copy(n).wait_send()


def output_kernel(gated_ref, sig_ref, e_ref, cot_ref, w_ref, bias_ref, res_ref, skip_ref, grad_ref):
    gated, w = gated_ref[...], w_ref[...]
    res = sig_ref[...].astype(F32) + matmul(gated, w[:, :512]) + bias_ref[1:2, 0:512]
    res_ref[...] = res.astype(BF16)
    skip_ref[...] = (matmul(gated, w[:, 512:]) + bias_ref[1:2, 512:1024]).astype(BF16)
    grad_ref[...] = cot_ref[...].astype(F32) + e_ref[...].astype(F32)


def shards(
    signal, cond, clip_lengths, dilation, w_conv, w_cond, b_conv, w_res, b_res, w_skip, b_skip, cot_res, cot_skip
):
    T = signal.shape[1]
    tiles = T // TILE
    sig, conds, cr, cs = signal[0], cond[0], cot_res[0], cot_skip[0]
    wb = jnp.concatenate(
        [w_cond.T, b_conv[:, None], jnp.concatenate([b_res, b_skip])[:, None], jnp.zeros((32, 46), BF16)], 1
    )
    vmem, hbm, smem = (pl.BlockSpec(memory_space=m) for m in (pltpu.VMEM, pl.ANY, pltpu.SMEM))
    dma = pltpu.SemaphoreType.DMA
    out = jax.ShapeDtypeStruct
    gated, e, wrs, bias, gconv, gres, gskip, gcond = pl.pallas_call(
        layer_kernel,
        out_shape=[
            out((T, 512), BF16),
            out((T, 512), BF16),
            out((4, 2, 2, 2, 16, 1024), BF16),
            out((16, 1024), F32),
            out((2, 16, 1024), F32),
            out((16, 512), F32),
            out((16, 512), F32),
            out((32, 128), F32),
        ],
        in_specs=[smem, smem] + [vmem] * 4 + [hbm] * 4,
        out_specs=[hbm] * 3 + [vmem] * 5,
        scratch_shapes=[
            pltpu.VMEM((3, T, 512), BF16),
            pltpu.VMEM((4, T, 512), BF16),
            pltpu.VMEM((128, T), BF16),
            pltpu.VMEM((3, 4, 2, 2, 2, 16, 1024), BF16),
            pltpu.VMEM((4, 2, 2, 2, 32, 128), BF16),
            pltpu.VMEM((2, 128, 512), BF16),
            pltpu.VMEM((4, 2 * TILE, 128), F32),
            pltpu.VMEM((DMAX, 512), BF16),
            pltpu.VMEM((DMAX, 512), BF16),
            pltpu.VMEM((DMAX, 512), BF16),
            pltpu.VMEM((4, 2, 2, 2, 16, 512), F32),
            pltpu.VMEM((6, 4, 2, 2, 16, 512), F32),
            pltpu.VMEM((6, 4, 2, 2, 16, 512), BF16),
            pltpu.VMEM((6, 4, 2, 2, 16, 512), BF16),
            pltpu.VMEM((6, 4, 2, 16, 512), BF16),
            pltpu.VMEM((6, 4, 2, 16, 512), BF16),
            pltpu.VMEM((6, 4, 16, 512), BF16),
            pltpu.VMEM((6, 4, 16, 512), BF16),
            pltpu.VMEM((6, 4, 16, 512), BF16),
            pltpu.VMEM((6, 3, 16, 512), BF16),
            pltpu.VMEM((4, 2, 2, 2, 32, 128), F32),
            pltpu.VMEM((4, 2, 2, 32, 128), BF16),
            pltpu.VMEM((4, 2, 2, 32, 128), BF16),
            pltpu.VMEM((4, 2, 32, 128), BF16),
            pltpu.VMEM((4, 2, 32, 128), BF16),
            pltpu.VMEM((4, 32, 128), BF16),
            pltpu.VMEM((4, 32, 128), BF16),
            pltpu.VMEM((4, 32, 128), BF16),
            pltpu.VMEM((3, 32, 128), BF16),
            dma((4,)),
            dma((tiles,)),
            dma((tiles,)),
            dma((1,)),
            dma((4, 8)),
            dma((4, 8)),
            dma((2 * PIECES,)),
            dma((2 * PIECES,)),
            dma((7, 6)),
            dma((7, 6)),
        ],
        compiler_params=pltpu.CompilerParams(
            collective_id=0, has_side_effects=True, vmem_limit_bytes=60 << 20
        ),
        name="layer",
    )(clip_lengths, dilation, w_conv, w_res, w_skip, wb, sig, conds, cr, cs)

    rows = pl.BlockSpec((TILE, 512), lambda i: (i, 0))
    res_out, skip_out, grad_signal = pl.pallas_call(
        output_kernel,
        grid=(tiles,),
        in_specs=[rows] * 4
        + [pl.BlockSpec((512, 1024), lambda i: (0, 0)), pl.BlockSpec((16, 1024), lambda i: (0, 0))],
        out_specs=[rows] * 3,
        out_shape=[out((T, 512), BF16), out((T, 512), BF16), out((T, 512), F32)],
        compiler_params=pltpu.CompilerParams(vmem_limit_bytes=60 << 20),
        name="outputs",
    )(gated, sig, e, cr, wrs.reshape(512, 1024), bias)
    return (
        res_out[None],
        skip_out[None],
        grad_signal[None],
        gconv,
        gcond[:, :80].T,
        gcond[:, 80],
        gres,
        gcond[:16, 81],
        gskip,
        gcond[16:, 81],
    )


def from_behind(value, axis, steps):
    count = lax.axis_size(axis)
    first, last = (max(0, -steps), min(count, count - steps))
    return lax.ppermute(value, axis, [(source, source + steps) for source in range(first, last)])


def shards_any(
    signal,
    cond,
    clip_lengths,
    dilation,
    w_conv,
    w_cond,
    b_conv,
    w_res,
    b_res,
    w_skip,
    b_skip,
    cot_res,
    cot_skip,
):
    rows = signal.shape[1]
    chans = signal.shape[2]
    conv_full, cond_full, bconv_full, res_full, bres_full, skip_full, bskip_full = (
        lax.all_gather(w_conv, ("dp", "fsdp"), axis=1, tiled=True),
        lax.all_gather(w_cond, ("dp", "fsdp"), axis=1, tiled=True),
        lax.all_gather(b_conv, ("dp", "fsdp"), axis=0, tiled=True),
        lax.all_gather(w_res, ("dp", "fsdp"), axis=0, tiled=True),
        lax.all_gather(b_res, ("dp", "fsdp"), axis=0, tiled=True),
        lax.all_gather(w_skip, ("dp", "fsdp"), axis=0, tiled=True),
        lax.all_gather(b_skip, ("dp", "fsdp"), axis=0, tiled=True),
    )
    segment = lax.axis_index("dp")
    times = segment * rows + jnp.arange(rows, dtype=jnp.int32)
    lengths = clip_lengths[0]
    starts = jnp.cumsum(lengths) - lengths
    begin = jnp.max(jnp.where(starts[None, :] <= times[:, None], starts[None, :], 0), axis=1)
    dilate = dilation[0]
    keep = times - begin >= dilate
    mask_low = keep.astype(jnp.bfloat16)
    samples = signal[0]
    conds = cond[0]
    tail = from_behind(samples[rows - DMAX :], "dp", 1)
    extended = jnp.concatenate([tail, samples], 0)
    lagged = lax.dynamic_slice_in_dim(extended, DMAX - dilate, rows, 0) * mask_low[:, None]
    preact = (
        matmul(lagged, conv_full[0])
        + matmul(samples, conv_full[1])
        + contract_first(conds, cond_full)
        + bconv_full.astype(jnp.float32)
    )
    half = preact.shape[1] // 2
    tanh_part = jnp.tanh(preact[:, :half])
    sig_part = jax.nn.sigmoid(preact[:, half:])
    gated = (tanh_part * sig_part).astype(jnp.bfloat16)
    res_out = (
        samples.astype(jnp.float32) + matmul(gated, res_full) + bres_full.astype(jnp.float32)
    ).astype(jnp.bfloat16)
    skip_out = (matmul(gated, skip_full) + bskip_full.astype(jnp.float32)).astype(jnp.bfloat16)
    conv_back, cond_back, bconv_back, res_back, bres_back, skip_back, bskip_back = (
        lax.all_gather(w_conv, ("dp", "fsdp"), axis=1, tiled=True),
        lax.all_gather(w_cond, ("dp", "fsdp"), axis=1, tiled=True),
        lax.all_gather(b_conv, ("dp", "fsdp"), axis=0, tiled=True),
        lax.all_gather(w_res, ("dp", "fsdp"), axis=0, tiled=True),
        lax.all_gather(b_res, ("dp", "fsdp"), axis=0, tiled=True),
        lax.all_gather(w_skip, ("dp", "fsdp"), axis=0, tiled=True),
        lax.all_gather(b_skip, ("dp", "fsdp"), axis=0, tiled=True),
    )
    back_res = cot_res[0]
    back_skip = cot_skip[0]
    d_gated = contract_last(back_res, res_back) + contract_last(back_skip, skip_back)
    d_preact = jnp.concatenate(
        [
            d_gated * sig_part * (1.0 - tanh_part * tanh_part),
            d_gated * tanh_part * sig_part * (1.0 - sig_part),
        ],
        1,
    ).astype(jnp.bfloat16)
    grad_res = contract_first(gated, back_res)
    grad_bres = jnp.sum(back_res.astype(jnp.float32), axis=0)
    grad_skip = contract_first(gated, back_skip)
    grad_bskip = jnp.sum(back_skip.astype(jnp.float32), axis=0)
    grad_conv = jnp.stack([contract_first(lagged, d_preact), contract_first(samples, d_preact)])
    grad_cond = matmul(conds, d_preact)
    grad_bconv = jnp.sum(d_preact.astype(jnp.float32), axis=0)
    grad_in = back_res.astype(jnp.float32) + contract_last(d_preact, conv_back[1])
    d_lagged = contract_last(d_preact, conv_back[0]) * keep.astype(jnp.float32)[:, None]
    d_extended = jnp.zeros((DMAX + rows, chans), jnp.float32)
    d_extended = lax.dynamic_update_slice_in_dim(d_extended, d_lagged, DMAX - dilate, 0)
    grad_in = grad_in + d_extended[DMAX:]
    returned = from_behind(d_extended[:DMAX].astype(jnp.bfloat16), "dp", -1).astype(jnp.float32)
    grad_in = grad_in + jnp.concatenate([jnp.zeros((rows - DMAX, chans), jnp.float32), returned], 0)
    sums = (
        lax.psum_scatter(grad_conv, ("dp", "fsdp"), scatter_dimension=1, tiled=True),
        lax.psum_scatter(grad_cond, ("dp", "fsdp"), scatter_dimension=1, tiled=True),
        lax.psum_scatter(grad_bconv, ("dp", "fsdp"), scatter_dimension=0, tiled=True),
        lax.psum_scatter(grad_res, ("dp", "fsdp"), scatter_dimension=0, tiled=True),
        lax.psum_scatter(grad_bres, ("dp", "fsdp"), scatter_dimension=0, tiled=True),
        lax.psum_scatter(grad_skip, ("dp", "fsdp"), scatter_dimension=0, tiled=True),
        lax.psum_scatter(grad_bskip, ("dp", "fsdp"), scatter_dimension=0, tiled=True),
    )
    return (
        res_out[None],
        skip_out[None],
        grad_in[None],
        sums[0],
        sums[1],
        sums[2],
        sums[3],
        sums[4],
        sums[5],
        sums[6],
    )


def solution(mesh):
    return jax.shard_map(
        shards if dict(mesh.shape) == {"dp": 8, "fsdp": 4} else shards_any,
        mesh=mesh,
        in_specs=(
            P("fsdp", "dp", None),
            P("fsdp", None, "dp"),
            P("fsdp", None),
            P("fsdp"),
            P(None, ("dp", "fsdp"), None),
            P(None, ("dp", "fsdp")),
            P(("dp", "fsdp")),
            P(("dp", "fsdp"), None),
            P(("dp", "fsdp")),
            P(("dp", "fsdp"), None),
            P(("dp", "fsdp")),
            P("fsdp", "dp", None),
            P("fsdp", "dp", None),
        ),
        out_specs=(
            P("fsdp", "dp", None),
            P("fsdp", "dp", None),
            P("fsdp", "dp", None),
            P(None, ("dp", "fsdp"), None),
            P(None, ("dp", "fsdp")),
            P(("dp", "fsdp")),
            P(("dp", "fsdp"), None),
            P(("dp", "fsdp")),
            P(("dp", "fsdp"), None),
            P(("dp", "fsdp")),
        ),
        check_vma=False,
    )
```

```python
import functools

import jax
import jax.numpy as jnp
from jax import lax
from jax.experimental import pallas as pl
from jax.experimental.pallas import tpu as pltpu
from jax.sharding import PartitionSpec as P

DMAX = 512
TILE = 512
BIG = 1024
PIECES = 8
SPLIT = 384
OUT_TILE = 2048
MESH = pl.DeviceIdType.MESH
BF16 = jnp.bfloat16
F32 = jnp.float32


def matmul(left, right):
    return jnp.dot(left, right, preferred_element_type=F32)


def contract_first(left, right):
    return lax.dot_general(left, right, (((0,), (0,)), ((), ())), preferred_element_type=F32)


def contract_last(left, right):
    return lax.dot_general(left, right, (((1,), (1,)), ((), ())), preferred_element_type=F32)


def bias_places(skip):
    n = lax.broadcasted_iota(jnp.int32, (512, 1024), 0)
    m = lax.broadcasted_iota(jnp.int32, (512, 1024), 1)
    place = ((n >> 4) << 5) + (n & 15) + 16 * skip
    return jnp.where(place == m, 1.0, 0.0).astype(BF16)


def layer_kernel(
    clip_ref, dil_ref, wconv_ref, wres_ref, wskip_ref, wcond_ref, bconv_ref, bres_ref, bskip_ref, sig_hbm, cond_hbm, cr_hbm, cs_hbm,
    gated_hbm, e_hbm, wrs_hbm, bias_ref, gconv_ref, gres_ref, gskip_ref, gcond_ref,
    X, D, condv, W, WC, own_cond, wct, F, halo, ret_send, ret_recv,
    Gt, GA, CS, CR, S1y, R1y, S1x, R1x, S2y, R2y, S2x, R2x, S3, R3,
    cGA, cCS, cCR, cS1, cR1, cS2, cR2, cS3, cR3,
    ld, st_g, st_e, st_w, ag_s, ag_r, h_s, h_r, rs_s, rs_r,
):
    T = sig_hbm.shape[0]
    tiles = T // TILE
    dp, fs = lax.axis_index("dp"), lax.axis_index("fsdp")
    z, x, y, c = dp // 2, dp % 2, fs // 2, fs % 2
    x1, y1, c1 = 1 - x, 1 - y, 1 - c
    zs = (z + 1 - 2 * (z % 2), (z + 2) % 4, 3 - z)

    def dev(zz, xx, yy, cc):
        return (zz * 2 + xx, yy * 2 + cc)

    sib, xn, yn = dev(z, x, y, c1), dev(z, x1, y, c), dev(z, x, y1, c)
    zn = [dev(zz, x, y, c) for zz in zs]

    def rcopy(src, dst, ssem, rsem, to):
        return pltpu.make_async_remote_copy(
            src_ref=src, dst_ref=dst, send_sem=ssem, recv_sem=rsem, device_id=to, device_id_type=MESH
        )

    loads = [
        pltpu.make_async_copy(sig_hbm, X.at[1], ld.at[0]),
        pltpu.make_async_copy(cr_hbm, D.at[0], ld.at[1]),
        pltpu.make_async_copy(cs_hbm, D.at[1], ld.at[2]),
        pltpu.make_async_copy(cond_hbm, condv.at[pl.ds(0, 80)], ld.at[3]),
    ]
    for load in loads:
        load.start()

    extra = dp - 1 + 2 * x
    has_extra = (extra >= 0) & (extra < 8)
    barrier = pltpu.get_barrier_semaphore()
    for to in [sib, xn, yn] + zn:
        pl.semaphore_signal(barrier, inc=1, device_id=to, device_id_type=MESH)

    @pl.when(has_extra)
    def _():
        pl.semaphore_signal(barrier, inc=1, device_id=(extra, fs), device_id_type=MESH)
        pl.semaphore_wait(barrier, 7)

    @pl.when(jnp.logical_not(has_extra))
    def _():
        pl.semaphore_wait(barrier, 6)

    for q in range(2):
        for tap in range(2):
            for n in range(2):
                to = tap * 512 + n * 256
                W[q, z, x, y, c, :, to : to + 256] = wconv_ref[tap, :, n * 512 + q * 256 : n * 512 + q * 256 + 256]
    W[2, z, x, y, c, :, 0:512] = wres_ref[...]
    W[2, z, x, y, c, :, 512:1024] = wskip_ref[...]

    def column(ref):
        size = ref.shape[1]
        square = jnp.broadcast_to(ref[...].astype(F32), (size, size))
        diagonal = lax.broadcasted_iota(jnp.int32, (size, size), 0) == lax.broadcasted_iota(jnp.int32, (size, size), 1)
        return jnp.sum(jnp.where(diagonal, square, 0.0), axis=1, keepdims=True)

    own_cond[...] = jnp.zeros_like(own_cond)
    own_cond[:, 0:80] = wcond_ref[...].astype(F32)
    place = lax.broadcasted_iota(jnp.int32, (32, 128), 1)
    pair = jnp.concatenate([column(bres_ref), column(bskip_ref)], 0)
    WC[z, x, y, c] = jnp.where(place == 80, column(bconv_ref), jnp.where(place == 81, pair, own_cond[...])).astype(BF16)

    def along_z(s):
        own = W.at[s, z, x, y, c] if s < 3 else WC.at[z, x, y, c]
        return [rcopy(own, own, ag_s.at[s, k], ag_r.at[s, k], zn[k]) for k in range(3)]

    def along_one(s):
        if s < 3:
            a, b = W.at[s, :, x, y, c, :, pl.ds(0, 512)], W.at[s, :, x, y, c, :, pl.ds(512, 512)]
            return [
                rcopy(a, a, ag_s.at[s, 3], ag_r.at[s, 3], xn),
                rcopy(b, b, ag_s.at[s, 4], ag_r.at[s, 4], yn),
            ]
        a = WC.at[:, x, y, c]
        return [rcopy(a, a, ag_s.at[s, 3], ag_r.at[s, 3], xn)]

    def along_other(s):
        if s < 3:
            a, b = W.at[s, :, :, y, c, :, pl.ds(0, 512)], W.at[s, :, x, :, c, :, pl.ds(512, 512)]
            return [
                rcopy(a, a, ag_s.at[s, 5], ag_r.at[s, 5], yn),
                rcopy(b, b, ag_s.at[s, 6], ag_r.at[s, 6], xn),
            ]
        a = WC.at[:, :, y, c]
        return [rcopy(a, a, ag_s.at[s, 5], ag_r.at[s, 5], yn)]

    def along_core(s):
        a = W.at[s, :, :, :, c] if s < 3 else WC.at[:, :, :, c]
        return [rcopy(a, a, ag_s.at[s, 7], ag_r.at[s, 7], sib)]

    def start(phase, *sections):
        for s in sections:
            for copy in phase(s):
                copy.start()

    def wait(phase, *sections):
        for s in sections:
            for copy in phase(s):
                copy.wait()

    def halo_copy(n):
        size = DMAX // PIECES
        return rcopy(
            X.at[1, pl.ds(T - DMAX + n * size, size)], halo.at[pl.ds(n * size, size)], h_s.at[n], h_r.at[n], (dp + 1, fs)
        )

    def send_halo(first, last):
        @pl.when(dp < 7)
        def _():
            for n in range(first, last):
                halo_copy(n).start()

    start(along_z, 2)

    dilate = dil_ref[0]
    lane = lax.broadcasted_iota(jnp.int32, (1, 128), 1)
    starts = jnp.zeros((1, 128), jnp.int32)
    for i in range(16):
        starts = starts + jnp.where(lane > i, clip_ref[0, i], 0)
    row = lax.broadcasted_iota(jnp.int32, (TILE, 128), 0)

    def keep(i):
        times = dp * T + i * TILE + row
        inside = (starts <= times) & (starts > times - dilate)
        return 1.0 - jnp.max(jnp.where(inside, 1.0, 0.0), axis=1, keepdims=True)

    def at(i, size=TILE):
        return pl.ds(pl.multiple_of(i * size, size), size)

    def put(half, value):
        for n in range(4):
            F[n, half * TILE : half * TILE + TILE] = value[:, n * 128 : n * 128 + 128].astype(F32)

    def shifted(first):
        return jnp.concatenate([F[n, pl.ds(first, TILE), :] for n in range(4)], 1)

    def lag_tile(i):
        put(1, X[1, at(i)])
        X[2, at(i)] = (shifted(TILE - dilate) * keep(i)).astype(BF16)

    def lag_body(i, carry):
        put(0, X[1, at(i - 1)])
        lag_tile(i)
        return carry

    def sums_body(i, total):
        return (
            total[0] + jnp.sum(D[0, at(i)].astype(F32), axis=0, keepdims=True),
            total[1] + jnp.sum(D[1, at(i)].astype(F32), axis=0, keepdims=True),
        )

    def dg_body(i, carry):
        wrs = W[2].reshape(512, 1024)
        rows = at(i, BIG)
        dg = contract_last(D[0, rows], wrs[:, :512]) + contract_last(D[1, rows], wrs[:, 512:])
        high = dg.astype(BF16)
        low = (dg - high.astype(F32)).astype(BF16)
        for q in range(2):
            D[2 + q, rows, 0:256] = high[:, q * 256 : q * 256 + 256]
            D[2 + q, rows, 256:512] = low[:, q * 256 : q * 256 + 256]
        return carry

    loads[0].wait()
    lax.fori_loop(1, 2, lag_body, 0)
    wait(along_z, 2)
    start(along_one, 2)
    start(along_z, 0, 3, 1)
    lax.fori_loop(2, 4, lag_body, 0)
    wait(along_one, 2)
    start(along_other, 2)
    lax.fori_loop(4, 6, lag_body, 0)
    wait(along_z, 0, 3)
    start(along_one, 0, 3)
    wait(along_z, 1)
    start(along_one, 1)
    lax.fori_loop(6, tiles, lag_body, 0)
    wait(along_other, 2)
    start(along_core, 2)
    wait(along_one, 0, 3)
    start(along_other, 0, 3)
    wait(along_one, 1)
    start(along_other, 1)
    for load in loads[1:]:
        load.wait()
    zero = jnp.zeros((1, 512), F32)
    bres, bskip = lax.fori_loop(0, tiles, sums_body, (zero, zero))
    condv[80:96] = jnp.where(lax.broadcasted_iota(jnp.int32, (16, T), 0) == 0, 1.0, 0.0).astype(BF16)
    condv[96:128] = jnp.zeros((32, T), BF16)
    wait(along_core, 2)
    wrs_copy = pltpu.make_async_copy(W.at[2], wrs_hbm, st_w.at[0])
    wrs_copy.start()
    lax.fori_loop(0, T // BIG // 2, dg_body, 0)
    wait(along_other, 0, 3)
    start(along_core, 0, 3)
    lax.fori_loop(T // BIG // 2, T // BIG, dg_body, 0)
    wait(along_other, 1)
    start(along_core, 1)
    send_halo(0, PIECES)

    @pl.when(dp == 0)
    def _():
        halo[...] = jnp.zeros_like(halo)

    @pl.when(dp == 7)
    def _():
        ret_recv[...] = jnp.zeros_like(ret_recv)

    wait(along_core, 0, 3)
    turned = WC[...].reshape(1024, 128).T
    for q in range(2):
        for n in range(2):
            wct[q, :, n * 256 : n * 256 + 256] = turned[:, n * 512 + q * 256 : n * 512 + q * 256 + 256]
    biases = turned[80:96]
    bias_ref[:, 0:512] = contract_last(biases, bias_places(0))
    bias_ref[:, 512:1024] = contract_last(biases, bias_places(1))

    def forward(rows, q):
        w = W[q].reshape(512, 1024)
        preact = (
            matmul(X[2, rows], w[:, :512])
            + matmul(X[1, rows], w[:, 512:])
            + contract_first(condv[:, rows], wct[q])
        )
        a = jnp.tanh(preact[:, :256])
        g = 0.5 * jnp.tanh(0.5 * preact[:, 256:]) + 0.5
        X[0, rows, q * 256 : q * 256 + 256] = (a * g).astype(BF16)
        dg = D[2 + q, rows].astype(F32)
        t = (dg[:, :256] + dg[:, 256:]) * g
        D[2 + q, rows, 0:256] = (t * (1.0 - a * a)).astype(BF16)
        D[2 + q, rows, 256:512] = (t * a * (1.0 - g)).astype(BF16)

    def gated_copy(i):
        return pltpu.make_async_copy(X.at[0, at(i)], gated_hbm.at[at(i)], st_g.at[i])

    whole = (T - TILE) // BIG
    for q in range(2):
        if q == 1:
            wait(along_core, 1)

        def forward_body(j, carry, q=q):
            forward(pl.ds(pl.multiple_of(TILE + j * BIG, TILE), BIG), q)
            if q == 1:
                for n in range(BIG // TILE):
                    gated_copy(1 + j * (BIG // TILE) + n).start()
            return carry

        lax.fori_loop(0, whole, forward_body, 0)
        for i in range(1 + whole * (BIG // TILE), tiles):
            forward(at(i), q)
            if q == 1:
                gated_copy(i).start()

    @pl.when(dp > 0)
    def _():
        for n in range(PIECES):
            halo_copy(n).wait_recv()

    put(0, halo[...])
    lag_tile(0)
    forward(at(0), 0)
    forward(at(0), 1)
    gated_copy(0).start()

    def back(i, tap):
        w0 = W[0].reshape(512, 1024)[:, tap * 512 : tap * 512 + 512]
        w1 = W[1].reshape(512, 1024)[:, tap * 512 : tap * 512 + 512]
        return contract_last(D[2, at(i)], w0) + contract_last(D[3, at(i)], w1)

    first = back(0, 0) * keep(0)
    put(0, first)
    ret_send[...] = first.astype(BF16)

    def ret_copy(n):
        rows = pl.ds(pl.multiple_of(n * (DMAX // PIECES), DMAX // PIECES), DMAX // PIECES)
        return rcopy(ret_send.at[rows], ret_recv.at[rows], h_s.at[PIECES + n], h_r.at[PIECES + n], (dp - 1, fs))

    def send_back(n):
        @pl.when(dp > 0)
        def _():
            ret_copy(n).start()

    send_back(0)
    send_back(1)

    def to_core(k):
        return rcopy(CS.at[k], CR.at[k], rs_s.at[k, 0], rs_r.at[k, 0], sib)

    def to_first(k):
        return [
            rcopy(S1y.at[k], R1y.at[k], rs_s.at[k, 1], rs_r.at[k, 1], yn),
            rcopy(S1x.at[k], R1x.at[k], rs_s.at[k, 2], rs_r.at[k, 2], xn),
        ]

    def to_second(k):
        return [
            rcopy(S2y.at[k], R2y.at[k], rs_s.at[k, 3], rs_r.at[k, 3], xn),
            rcopy(S2x.at[k], R2x.at[k], rs_s.at[k, 4], rs_r.at[k, 4], yn),
        ]

    def to_z(k):
        return [
            rcopy(S3.at[k, zs[n]], R3.at[k, n], rs_s.at[k, 5 + n], rs_r.at[k, 5 + n], zn[n]) for n in range(3)
        ]

    A, B = pl.ds(0, SPLIT), pl.ds(SPLIT, 512 - SPLIT)

    def stage0(k):
        CS[k] = Gt[:, :, :, c1].astype(BF16)
        to_core(k).start()
        GA[k] = Gt[:, :, :, c]

    def stage1(k):
        to_core(k).wait()
        S1y[k] = (GA[k, :, :, y1, :, A] + CR[k, :, :, y1, :, A].astype(F32)).astype(BF16)
        S1x[k] = (GA[k, :, x1, :, :, B] + CR[k, :, x1, :, :, B].astype(F32)).astype(BF16)
        for copy in to_first(k):
            copy.start()
        GA[k, :, :, y, :, A] += CR[k, :, :, y, :, A].astype(F32)
        GA[k, :, x, :, :, B] += CR[k, :, x, :, :, B].astype(F32)

    def stage2(k):
        for copy in to_first(k):
            copy.wait()
        S2y[k] = (GA[k, :, x1, y, :, A] + R1y[k, :, x1].astype(F32)).astype(BF16)
        S2x[k] = (GA[k, :, x, y1, :, B] + R1x[k, :, y1].astype(F32)).astype(BF16)
        for copy in to_second(k):
            copy.start()
        GA[k, :, x, y, :, A] += R1y[k, :, x].astype(F32)
        GA[k, :, x, y, :, B] += R1x[k, :, y].astype(F32)

    def stage3(k):
        for copy in to_second(k):
            copy.wait()
        one = GA[k, :, x, y, :, A] + R2y[k].astype(F32)
        two = GA[k, :, x, y, :, B] + R2x[k].astype(F32)
        S3[k, :, :, A] = one.astype(BF16)
        S3[k, :, :, B] = two.astype(BF16)
        for copy in to_z(k):
            copy.start()
        GA[k, :, x, y, :, A] = one
        GA[k, :, x, y, :, B] = two

    def stage4(k):
        for copy in to_z(k):
            copy.wait()
        total = GA[k, z, x, y]
        for n in range(3):
            total = total + R3[k, n].astype(F32)
        return total

    cond_core = rcopy(cCS, cCR, rs_s.at[6, 0], rs_r.at[6, 0], sib)
    cond_first = rcopy(cS1, cR1, rs_s.at[6, 1], rs_r.at[6, 1], yn)
    cond_second = rcopy(cS2, cR2, rs_s.at[6, 2], rs_r.at[6, 2], xn)
    cond_z = [rcopy(cS3.at[zs[n]], cR3.at[n], rs_s.at[6, 3 + n], rs_r.at[6, 3 + n], zn[n]) for n in range(3)]

    def three_parts(value):
        parts = []
        for _ in range(3):
            parts.append(value.astype(BF16))
            value = value - parts[-1].astype(F32)
        return jnp.concatenate(parts + [jnp.zeros((13, 512), BF16)], 0)

    def cond_stage0():
        bias_row = matmul(three_parts(bres), bias_places(0)) + matmul(three_parts(bskip), bias_places(1))
        bias_row = jnp.sum(bias_row, axis=0, keepdims=True)
        one, two = matmul(condv[...], D[2]), matmul(condv[...], D[3])
        grad = jnp.concatenate([one[:, :256], two[:, :256], one[:, 256:], two[:, 256:]], 1)
        place = lax.broadcasted_iota(jnp.int32, (128, 1024), 0)
        cGA[...] = jnp.where(place == 81, bias_row, grad).T.reshape(4, 2, 2, 2, 32, 128)
        cCS[...] = cGA[:, :, :, c1].astype(BF16)
        cond_core.start()

    def cond_stage1():
        cond_core.wait()
        cS1[...] = (cGA[:, :, y1, c] + cCR[:, :, y1].astype(F32)).astype(BF16)
        cond_first.start()
        cGA[:, :, y, c] += cCR[:, :, y].astype(F32)

    def cond_stage2():
        cond_first.wait()
        cS2[...] = (cGA[:, x1, y, c] + cR1[:, x1].astype(F32)).astype(BF16)
        cond_second.start()
        cGA[:, x, y, c] += cR1[:, x].astype(F32)

    def cond_stage3():
        cond_second.wait()
        total = cGA[:, x, y, c] + cR2[...].astype(F32)
        cS3[...] = total.astype(BF16)
        for copy in cond_z:
            copy.start()
        cGA[:, x, y, c] = total

    def cond_stage4():
        for copy in cond_z:
            copy.wait()
        total = cGA[z, x, y, c]
        for n in range(3):
            total = total + cR3[n].astype(F32)
        gcond_ref[...] = total

    def when(condition, work, *args):
        @pl.when(condition)
        def _():
            work(*args)

    cond_stage0()

    def chunk_body(k, carry):
        left, right = k // 2, k % 2 + 2 * ((k + 4) // 6)
        Gt[...] = contract_first(X[left], D[right]).reshape(4, 2, 2, 2, 16, 512)
        stage0(k)
        when(k >= 1, stage1, k - 1)
        when(k >= 3, stage2, k - 3)
        when(k >= 5, stage3, k - 5)
        when(k == 0, cond_stage1)
        when(k == 2, cond_stage2)
        when(k == 4, cond_stage3)
        send_back(k + 2)
        return carry

    lax.fori_loop(0, 6, chunk_body, 0)

    def e_copy(i):
        return pltpu.make_async_copy(X.at[2, at(i)], e_hbm.at[at(i)], st_e.at[i])

    def e_tile(i):
        X[2, at(i)] = (back(i, 1) + shifted(dilate)).astype(BF16)
        e_copy(i).start()

    def e_body(e, carry):
        put(1, back(e + 1, 0) * keep(e + 1))
        e_tile(e)
        F[:, 0:TILE] = F[:, TILE : 2 * TILE]
        when(e == 0, stage1, 5)
        when(e == 0, stage2, 3)
        when(e == 1, stage3, 1)
        when(e == 1, stage2, 4)
        when(e == 2, stage3, 2)
        when(e == 3, stage2, 5)
        when(e == 3, stage3, 3)
        when(e == 4, stage3, 4)
        when(e == 5, stage3, 5)
        return carry

    lax.fori_loop(0, tiles - 1, e_body, 0)

    @pl.when(dp < 7)
    def _():
        for n in range(PIECES):
            ret_copy(n).wait_recv()

    put(1, ret_recv[...])
    e_tile(tiles - 1)
    cond_stage4()
    gres_ref[...] = stage4(0)
    gskip_ref[...] = stage4(1)
    for k in range(2, 6):
        total, q = stage4(k), k % 2
        for n in range(2):
            to = n * 512 + q * 256
            gconv_ref[1 - (k - 2) // 2, :, to : to + 256] = total[:, n * 256 : n * 256 + 256]

    def finish(i, carry):
        gated_copy(i).wait()
        e_copy(i).wait()
        return carry

    lax.fori_loop(0, tiles, finish, 0)
    wrs_copy.wait()

    @pl.when(dp < 7)
    def _():
        for n in range(PIECES):
            halo_copy(n).wait_send()

    @pl.when(dp > 0)
    def _():
        for n in range(PIECES):
            ret_copy(n).wait_send()


def output_kernel(
    gated_ref, sig_ref, e_ref, cot_ref, w_ref, bias_ref, gconv_ref, gres_ref, gskip_ref, gcond_ref,
    res_ref, skip_ref, grad_ref, conv_out, res_out, skip_out, cond_out, bconv_out, bres_out, bskip_out,
):
    gated, w = gated_ref[...], w_ref[...]
    res = sig_ref[...].astype(F32) + matmul(gated, w[:, :512]) + bias_ref[1:2, 0:512]
    res_ref[...] = res.astype(BF16)
    skip_ref[...] = (matmul(gated, w[:, 512:]) + bias_ref[1:2, 512:1024]).astype(BF16)
    grad_ref[...] = cot_ref[...].astype(F32) + e_ref[...].astype(F32)

    @pl.when(pl.program_id(0) == 0)
    def _():
        conv_out[...] = gconv_ref[...]
        res_out[...] = gres_ref[...]
        skip_out[...] = gskip_ref[...]
        cond_out[...] = gcond_ref[:, 0:80]

        def as_row(value):
            size = value.shape[0]
            square = jnp.broadcast_to(value, (size, size))
            first = lax.broadcasted_iota(jnp.int32, (size, size), 0)
            second = lax.broadcasted_iota(jnp.int32, (size, size), 1)
            return jnp.sum(jnp.where(first == second, square, 0.0), axis=0, keepdims=True)

        bconv_out[...] = as_row(gcond_ref[:, 80:81])
        bres_out[...] = as_row(gcond_ref[0:16, 81:82])
        bskip_out[...] = as_row(gcond_ref[16:32, 81:82])


def shards(
    signal, cond, clip_lengths, dilation, w_conv, w_cond, b_conv, w_res, b_res, w_skip, b_skip, cot_res, cot_skip
):
    T = signal.shape[1]
    tiles = T // TILE
    sig, conds, cr, cs = signal[0], cond[0], cot_res[0], cot_skip[0]
    vmem, hbm, smem = (pl.BlockSpec(memory_space=m) for m in (pltpu.VMEM, pl.ANY, pltpu.SMEM))
    dma = pltpu.SemaphoreType.DMA
    out = jax.ShapeDtypeStruct
    gated, e, wrs, bias, gconv, gres, gskip, gcond = pl.pallas_call(
        layer_kernel,
        out_shape=[
            out((T, 512), BF16),
            out((T, 512), BF16),
            out((4, 2, 2, 2, 16, 1024), BF16),
            out((16, 1024), F32),
            out((2, 16, 1024), F32),
            out((16, 512), F32),
            out((16, 512), F32),
            out((32, 128), F32),
        ],
        in_specs=[smem, smem] + [vmem] * 7 + [hbm] * 4,
        out_specs=[hbm] * 3 + [vmem] * 5,
        scratch_shapes=[
            pltpu.VMEM((3, T, 512), BF16),
            pltpu.VMEM((4, T, 512), BF16),
            pltpu.VMEM((128, T), BF16),
            pltpu.VMEM((3, 4, 2, 2, 2, 16, 1024), BF16),
            pltpu.VMEM((4, 2, 2, 2, 32, 128), BF16),
            pltpu.VMEM((32, 128), F32),
            pltpu.VMEM((2, 128, 512), BF16),
            pltpu.VMEM((4, 2 * TILE, 128), F32),
            pltpu.VMEM((DMAX, 512), BF16),
            pltpu.VMEM((DMAX, 512), BF16),
            pltpu.VMEM((DMAX, 512), BF16),
            pltpu.VMEM((4, 2, 2, 2, 16, 512), F32),
            pltpu.VMEM((6, 4, 2, 2, 16, 512), F32),
            pltpu.VMEM((6, 4, 2, 2, 16, 512), BF16),
            pltpu.VMEM((6, 4, 2, 2, 16, 512), BF16),
            pltpu.VMEM((6, 4, 2, 16, SPLIT), BF16),
            pltpu.VMEM((6, 4, 2, 16, SPLIT), BF16),
            pltpu.VMEM((6, 4, 2, 16, 512 - SPLIT), BF16),
            pltpu.VMEM((6, 4, 2, 16, 512 - SPLIT), BF16),
            pltpu.VMEM((6, 4, 16, SPLIT), BF16),
            pltpu.VMEM((6, 4, 16, SPLIT), BF16),
            pltpu.VMEM((6, 4, 16, 512 - SPLIT), BF16),
            pltpu.VMEM((6, 4, 16, 512 - SPLIT), BF16),
            pltpu.VMEM((6, 4, 16, 512), BF16),
            pltpu.VMEM((6, 3, 16, 512), BF16),
            pltpu.VMEM((4, 2, 2, 2, 32, 128), F32),
            pltpu.VMEM((4, 2, 2, 32, 128), BF16),
            pltpu.VMEM((4, 2, 2, 32, 128), BF16),
            pltpu.VMEM((4, 2, 32, 128), BF16),
            pltpu.VMEM((4, 2, 32, 128), BF16),
            pltpu.VMEM((4, 32, 128), BF16),
            pltpu.VMEM((4, 32, 128), BF16),
            pltpu.VMEM((4, 32, 128), BF16),
            pltpu.VMEM((3, 32, 128), BF16),
            dma((4,)),
            dma((tiles,)),
            dma((tiles,)),
            dma((1,)),
            dma((4, 8)),
            dma((4, 8)),
            dma((2 * PIECES,)),
            dma((2 * PIECES,)),
            dma((7, 8)),
            dma((7, 8)),
        ],
        compiler_params=pltpu.CompilerParams(
            collective_id=0, has_side_effects=True, vmem_limit_bytes=60 << 20
        ),
        name="layer",
    )(
        clip_lengths, dilation, w_conv, w_res, w_skip, w_cond.T, b_conv[None], b_res[None], b_skip[None], sig, conds, cr, cs
    )

    rows = pl.BlockSpec((OUT_TILE, 512), lambda i: (i, 0))

    def whole(array):
        return pl.BlockSpec(array.shape, lambda i: (0,) * len(array.shape))

    small = [wrs.reshape(512, 1024), bias, gconv, gres, gskip, gcond]
    sums = [out(g.shape, F32) for g in (gconv, gres, gskip)] + [out(shape, F32) for shape in ((32, 80), (1, 32), (1, 16), (1, 16))]
    res_out, skip_out, grad_signal, gconv, gres, gskip, gcond, gbconv, gbres, gbskip = pl.pallas_call(
        output_kernel,
        grid=(T // OUT_TILE,),
        in_specs=[rows] * 4 + [whole(array) for array in small],
        out_specs=[rows] * 3 + [whole(array) for array in sums],
        out_shape=[out((T, 512), BF16), out((T, 512), BF16), out((T, 512), F32)] + sums,
        compiler_params=pltpu.CompilerParams(vmem_limit_bytes=60 << 20),
        name="outputs",
    )(gated, sig, e, cr, *small)
    return (
        res_out[None],
        skip_out[None],
        grad_signal[None],
        gconv,
        gcond.T,
        gbconv[0],
        gres,
        gbres[0],
        gskip,
        gbskip[0],
    )


def from_behind(value, axis, steps):
    count = lax.axis_size(axis)
    first, last = (max(0, -steps), min(count, count - steps))
    return lax.ppermute(value, axis, [(source, source + steps) for source in range(first, last)])


def shards_any(
    signal,
    cond,
    clip_lengths,
    dilation,
    w_conv,
    w_cond,
    b_conv,
    w_res,
    b_res,
    w_skip,
    b_skip,
    cot_res,
    cot_skip,
):
    rows = signal.shape[1]
    chans = signal.shape[2]
    conv_full, cond_full, bconv_full, res_full, bres_full, skip_full, bskip_full = (
        lax.all_gather(w_conv, ("dp", "fsdp"), axis=1, tiled=True),
        lax.all_gather(w_cond, ("dp", "fsdp"), axis=1, tiled=True),
        lax.all_gather(b_conv, ("dp", "fsdp"), axis=0, tiled=True),
        lax.all_gather(w_res, ("dp", "fsdp"), axis=0, tiled=True),
        lax.all_gather(b_res, ("dp", "fsdp"), axis=0, tiled=True),
        lax.all_gather(w_skip, ("dp", "fsdp"), axis=0, tiled=True),
        lax.all_gather(b_skip, ("dp", "fsdp"), axis=0, tiled=True),
    )
    segment = lax.axis_index("dp")
    times = segment * rows + jnp.arange(rows, dtype=jnp.int32)
    lengths = clip_lengths[0]
    starts = jnp.cumsum(lengths) - lengths
    begin = jnp.max(jnp.where(starts[None, :] <= times[:, None], starts[None, :], 0), axis=1)
    dilate = dilation[0]
    keep = times - begin >= dilate
    mask_low = keep.astype(jnp.bfloat16)
    samples = signal[0]
    conds = cond[0]
    tail = from_behind(samples[rows - DMAX :], "dp", 1)
    extended = jnp.concatenate([tail, samples], 0)
    lagged = lax.dynamic_slice_in_dim(extended, DMAX - dilate, rows, 0) * mask_low[:, None]
    preact = (
        matmul(lagged, conv_full[0])
        + matmul(samples, conv_full[1])
        + contract_first(conds, cond_full)
        + bconv_full.astype(jnp.float32)
    )
    half = preact.shape[1] // 2
    tanh_part = jnp.tanh(preact[:, :half])
    sig_part = jax.nn.sigmoid(preact[:, half:])
    gated = (tanh_part * sig_part).astype(jnp.bfloat16)
    res_out = (
        samples.astype(jnp.float32) + matmul(gated, res_full) + bres_full.astype(jnp.float32)
    ).astype(jnp.bfloat16)
    skip_out = (matmul(gated, skip_full) + bskip_full.astype(jnp.float32)).astype(jnp.bfloat16)
    conv_back, cond_back, bconv_back, res_back, bres_back, skip_back, bskip_back = (
        lax.all_gather(w_conv, ("dp", "fsdp"), axis=1, tiled=True),
        lax.all_gather(w_cond, ("dp", "fsdp"), axis=1, tiled=True),
        lax.all_gather(b_conv, ("dp", "fsdp"), axis=0, tiled=True),
        lax.all_gather(w_res, ("dp", "fsdp"), axis=0, tiled=True),
        lax.all_gather(b_res, ("dp", "fsdp"), axis=0, tiled=True),
        lax.all_gather(w_skip, ("dp", "fsdp"), axis=0, tiled=True),
        lax.all_gather(b_skip, ("dp", "fsdp"), axis=0, tiled=True),
    )
    back_res = cot_res[0]
    back_skip = cot_skip[0]
    d_gated = contract_last(back_res, res_back) + contract_last(back_skip, skip_back)
    d_preact = jnp.concatenate(
        [
            d_gated * sig_part * (1.0 - tanh_part * tanh_part),
            d_gated * tanh_part * sig_part * (1.0 - sig_part),
        ],
        1,
    ).astype(jnp.bfloat16)
    grad_res = contract_first(gated, back_res)
    grad_bres = jnp.sum(back_res.astype(jnp.float32), axis=0)
    grad_skip = contract_first(gated, back_skip)
    grad_bskip = jnp.sum(back_skip.astype(jnp.float32), axis=0)
    grad_conv = jnp.stack([contract_first(lagged, d_preact), contract_first(samples, d_preact)])
    grad_cond = matmul(conds, d_preact)
    grad_bconv = jnp.sum(d_preact.astype(jnp.float32), axis=0)
    grad_in = back_res.astype(jnp.float32) + contract_last(d_preact, conv_back[1])
    d_lagged = contract_last(d_preact, conv_back[0]) * keep.astype(jnp.float32)[:, None]
    d_extended = jnp.zeros((DMAX + rows, chans), jnp.float32)
    d_extended = lax.dynamic_update_slice_in_dim(d_extended, d_lagged, DMAX - dilate, 0)
    grad_in = grad_in + d_extended[DMAX:]
    returned = from_behind(d_extended[:DMAX].astype(jnp.bfloat16), "dp", -1).astype(jnp.float32)
    grad_in = grad_in + jnp.concatenate([jnp.zeros((rows - DMAX, chans), jnp.float32), returned], 0)
    sums = (
        lax.psum_scatter(grad_conv, ("dp", "fsdp"), scatter_dimension=1, tiled=True),
        lax.psum_scatter(grad_cond, ("dp", "fsdp"), scatter_dimension=1, tiled=True),
        lax.psum_scatter(grad_bconv, ("dp", "fsdp"), scatter_dimension=0, tiled=True),
        lax.psum_scatter(grad_res, ("dp", "fsdp"), scatter_dimension=0, tiled=True),
        lax.psum_scatter(grad_bres, ("dp", "fsdp"), scatter_dimension=0, tiled=True),
        lax.psum_scatter(grad_skip, ("dp", "fsdp"), scatter_dimension=0, tiled=True),
        lax.psum_scatter(grad_bskip, ("dp", "fsdp"), scatter_dimension=0, tiled=True),
    )
    return (
        res_out[None],
        skip_out[None],
        grad_in[None],
        sums[0],
        sums[1],
        sums[2],
        sums[3],
        sums[4],
        sums[5],
        sums[6],
    )


def solution(mesh):
    return jax.shard_map(
        shards if dict(mesh.shape) == {"dp": 8, "fsdp": 4} else shards_any,
        mesh=mesh,
        in_specs=(
            P("fsdp", "dp", None),
            P("fsdp", None, "dp"),
            P("fsdp", None),
            P("fsdp"),
            P(None, ("dp", "fsdp"), None),
            P(None, ("dp", "fsdp")),
            P(("dp", "fsdp")),
            P(("dp", "fsdp"), None),
            P(("dp", "fsdp")),
            P(("dp", "fsdp"), None),
            P(("dp", "fsdp")),
            P("fsdp", "dp", None),
            P("fsdp", "dp", None),
        ),
        out_specs=(
            P("fsdp", "dp", None),
            P("fsdp", "dp", None),
            P("fsdp", "dp", None),
            P(None, ("dp", "fsdp"), None),
            P(None, ("dp", "fsdp")),
            P(("dp", "fsdp")),
            P(("dp", "fsdp"), None),
            P(("dp", "fsdp")),
            P(("dp", "fsdp"), None),
            P(("dp", "fsdp")),
        ),
        check_vma=False,
    )
```

```python
import functools

import jax
import jax.numpy as jnp
from jax import lax
from jax.experimental import pallas as pl
from jax.experimental.pallas import tpu as pltpu
from jax.sharding import PartitionSpec as P

DMAX = 512
TILE = 512
BIG = 1024
PIECES = 8
SPLIT = 384
OUT_TILE = 2048
MESH = pl.DeviceIdType.MESH
BF16 = jnp.bfloat16
F32 = jnp.float32


def matmul(left, right):
    return jnp.dot(left, right, preferred_element_type=F32)


def contract_first(left, right):
    return lax.dot_general(left, right, (((0,), (0,)), ((), ())), preferred_element_type=F32)


def contract_last(left, right):
    return lax.dot_general(left, right, (((1,), (1,)), ((), ())), preferred_element_type=F32)


def bias_places(skip):
    n = lax.broadcasted_iota(jnp.int32, (512, 1024), 0)
    m = lax.broadcasted_iota(jnp.int32, (512, 1024), 1)
    place = ((n >> 4) << 5) + (n & 15) + 16 * skip
    return jnp.where(place == m, 1.0, 0.0).astype(BF16)


def layer_kernel(
    clip_ref, dil_ref, wconv_ref, wres_ref, wskip_ref, wcond_ref, bconv_ref, bres_ref, bskip_ref, sig_hbm, cond_hbm, cr_hbm, cs_hbm,
    gated_hbm, e_hbm, wrs_hbm, bias_ref, gconv_ref, gres_ref, gskip_ref, gcond_ref,
    X, D, condv, W, WC, own_cond, wct, F, halo, ret_send, ret_recv,
    Gt, GA, CS, CR, S1y, R1y, S1x, R1x, S2y, R2y, S2x, R2x, S3, R3,
    cGA, cCS, cCR, cS1, cR1, cS2, cR2, cS3, cR3,
    ld, st_g, st_e, st_w, ag_s, ag_r, h_s, h_r, rs_s, rs_r,
):
    T = sig_hbm.shape[0]
    tiles = T // TILE
    dp, fs = lax.axis_index("dp"), lax.axis_index("fsdp")
    z, x, y, c = dp // 2, dp % 2, fs // 2, fs % 2
    x1, y1, c1 = 1 - x, 1 - y, 1 - c
    zs = (z + 1 - 2 * (z % 2), (z + 2) % 4, 3 - z)

    def dev(zz, xx, yy, cc):
        return (zz * 2 + xx, yy * 2 + cc)

    sib, xn, yn = dev(z, x, y, c1), dev(z, x1, y, c), dev(z, x, y1, c)
    zn = [dev(zz, x, y, c) for zz in zs]

    def rcopy(src, dst, ssem, rsem, to):
        return pltpu.make_async_remote_copy(
            src_ref=src, dst_ref=dst, send_sem=ssem, recv_sem=rsem, device_id=to, device_id_type=MESH
        )

    loads = [
        pltpu.make_async_copy(sig_hbm, X.at[1], ld.at[0]),
        pltpu.make_async_copy(cr_hbm, D.at[0], ld.at[1]),
        pltpu.make_async_copy(cs_hbm, D.at[1], ld.at[2]),
        pltpu.make_async_copy(cond_hbm, condv.at[pl.ds(0, 80)], ld.at[3]),
    ]
    for load in loads:
        load.start()

    extra = dp - 1 + 2 * x
    has_extra = (extra >= 0) & (extra < 8)
    barrier = pltpu.get_barrier_semaphore()
    for to in [sib, xn, yn] + zn:
        pl.semaphore_signal(barrier, inc=1, device_id=to, device_id_type=MESH)

    @pl.when(has_extra)
    def _():
        pl.semaphore_signal(barrier, inc=1, device_id=(extra, fs), device_id_type=MESH)
        pl.semaphore_wait(barrier, 7)

    @pl.when(jnp.logical_not(has_extra))
    def _():
        pl.semaphore_wait(barrier, 6)

    for q in range(2):
        for tap in range(2):
            for n in range(2):
                to = tap * 512 + n * 256
                W[q, z, x, y, c, :, to : to + 256] = wconv_ref[tap, :, n * 512 + q * 256 : n * 512 + q * 256 + 256]
    W[2, z, x, y, c, :, 0:512] = wres_ref[...]
    W[2, z, x, y, c, :, 512:1024] = wskip_ref[...]

    def column(ref):
        size = ref.shape[1]
        square = jnp.broadcast_to(ref[...].astype(F32), (size, size))
        diagonal = lax.broadcasted_iota(jnp.int32, (size, size), 0) == lax.broadcasted_iota(jnp.int32, (size, size), 1)
        return jnp.sum(jnp.where(diagonal, square, 0.0), axis=1, keepdims=True)

    own_cond[...] = jnp.zeros_like(own_cond)
    own_cond[:, 0:80] = wcond_ref[...].astype(F32)
    place = lax.broadcasted_iota(jnp.int32, (32, 128), 1)
    pair = jnp.concatenate([column(bres_ref), column(bskip_ref)], 0)
    WC[z, x, y, c] = jnp.where(place == 80, column(bconv_ref), jnp.where(place == 81, pair, own_cond[...])).astype(BF16)

    def along_z(s):
        own = W.at[s, z, x, y, c] if s < 3 else WC.at[z, x, y, c]
        return [rcopy(own, own, ag_s.at[s, k], ag_r.at[s, k], zn[k]) for k in range(3)]

    def along_one(s):
        if s < 3:
            a, b = W.at[s, :, x, y, c, :, pl.ds(0, 512)], W.at[s, :, x, y, c, :, pl.ds(512, 512)]
            return [
                rcopy(a, a, ag_s.at[s, 3], ag_r.at[s, 3], xn),
                rcopy(b, b, ag_s.at[s, 4], ag_r.at[s, 4], yn),
            ]
        a = WC.at[:, x, y, c]
        return [rcopy(a, a, ag_s.at[s, 3], ag_r.at[s, 3], xn)]

    def along_other(s):
        if s < 3:
            a, b = W.at[s, :, :, y, c, :, pl.ds(0, 512)], W.at[s, :, x, :, c, :, pl.ds(512, 512)]
            return [
                rcopy(a, a, ag_s.at[s, 5], ag_r.at[s, 5], yn),
                rcopy(b, b, ag_s.at[s, 6], ag_r.at[s, 6], xn),
            ]
        a = WC.at[:, :, y, c]
        return [rcopy(a, a, ag_s.at[s, 5], ag_r.at[s, 5], yn)]

    def along_core(s):
        a = W.at[s, :, :, :, c] if s < 3 else WC.at[:, :, :, c]
        return [rcopy(a, a, ag_s.at[s, 7], ag_r.at[s, 7], sib)]

    def start(phase, *sections):
        for s in sections:
            for copy in phase(s):
                copy.start()

    def wait(phase, *sections):
        for s in sections:
            for copy in phase(s):
                copy.wait()

    def halo_copy(n):
        size = DMAX // PIECES
        return rcopy(
            X.at[1, pl.ds(T - DMAX + n * size, size)], halo.at[pl.ds(n * size, size)], h_s.at[n], h_r.at[n], (dp + 1, fs)
        )

    def send_halo(first, last):
        @pl.when(dp < 7)
        def _():
            for n in range(first, last):
                halo_copy(n).start()

    start(along_z, 2)

    dilate = dil_ref[0]
    lane = lax.broadcasted_iota(jnp.int32, (1, 128), 1)
    starts = jnp.zeros((1, 128), jnp.int32)
    for i in range(16):
        starts = starts + jnp.where(lane > i, clip_ref[0, i], 0)
    row = lax.broadcasted_iota(jnp.int32, (TILE, 128), 0)

    def keep(i):
        times = dp * T + i * TILE + row
        inside = (starts <= times) & (starts > times - dilate)
        return 1.0 - jnp.max(jnp.where(inside, 1.0, 0.0), axis=1, keepdims=True)

    def at(i, size=TILE):
        return pl.ds(i * size if isinstance(i, int) else pl.multiple_of(i * size, size), size)

    def put(half, value):
        for n in range(4):
            F[n, half * TILE : half * TILE + TILE] = value[:, n * 128 : n * 128 + 128].astype(F32)

    def shifted(first):
        return jnp.concatenate([F[n, pl.ds(first, TILE), :] for n in range(4)], 1)

    def lag_tile(i):
        put(1, X[1, at(i)])
        X[2, at(i)] = (shifted(TILE - dilate) * keep(i)).astype(BF16)

    def lag_body(i, carry):
        put(0, X[1, at(i - 1)])
        lag_tile(i)
        return carry

    def sums_body(i, total):
        return (
            total[0] + jnp.sum(D[0, at(i)].astype(F32), axis=0, keepdims=True),
            total[1] + jnp.sum(D[1, at(i)].astype(F32), axis=0, keepdims=True),
        )

    def d_gated(rows):
        wrs = W[2].reshape(512, 1024)
        dg = contract_last(D[0, rows], wrs[:, :512]) + contract_last(D[1, rows], wrs[:, 512:])
        high = dg.astype(BF16)
        low = (dg - high.astype(F32)).astype(BF16)
        for q in range(2):
            D[2 + q, rows, 0:256] = high[:, q * 256 : q * 256 + 256]
            D[2 + q, rows, 256:512] = low[:, q * 256 : q * 256 + 256]

    loads[0].wait()
    lax.fori_loop(1, 2, lag_body, 0)
    wait(along_z, 2)
    start(along_one, 2)
    start(along_z, 0, 3, 1)
    lax.fori_loop(2, 4, lag_body, 0)
    wait(along_one, 2)
    start(along_other, 2)
    wait(along_z, 0, 3)
    start(along_one, 0, 3)
    wait(along_z, 1)
    start(along_one, 1)
    lax.fori_loop(4, tiles, lag_body, 0)
    wait(along_other, 2)
    start(along_core, 2)
    wait(along_one, 0, 3)
    start(along_other, 0, 3)
    wait(along_one, 1)
    start(along_other, 1)
    for load in loads[1:]:
        load.wait()
    zero = jnp.zeros((1, 512), F32)
    bres, bskip = lax.fori_loop(0, tiles, sums_body, (zero, zero))
    condv[80:96] = jnp.where(lax.broadcasted_iota(jnp.int32, (16, T), 0) == 0, 1.0, 0.0).astype(BF16)
    condv[96:128] = jnp.zeros((32, T), BF16)
    wait(along_core, 2)
    wrs_copy = pltpu.make_async_copy(W.at[2], wrs_hbm, st_w.at[0])
    wrs_copy.start()
    for i in range(0, T, BIG):
        d_gated(pl.ds(i, BIG))
        if i == T // 2 - BIG:
            wait(along_other, 0, 3)
            start(along_core, 0, 3)

    wait(along_other, 1)
    start(along_core, 1)
    send_halo(0, PIECES)

    @pl.when(dp == 0)
    def _():
        halo[...] = jnp.zeros_like(halo)

    @pl.when(dp == 7)
    def _():
        ret_recv[...] = jnp.zeros_like(ret_recv)

    wait(along_core, 0, 3)
    turned = WC[...].reshape(1024, 128).T
    for q in range(2):
        for n in range(2):
            wct[q, :, n * 256 : n * 256 + 256] = turned[:, n * 512 + q * 256 : n * 512 + q * 256 + 256]
    biases = turned[80:96]
    bias_ref[:, 0:512] = contract_last(biases, bias_places(0))
    bias_ref[:, 512:1024] = contract_last(biases, bias_places(1))

    def forward(rows, q):
        w = W[q].reshape(512, 1024)
        preact = (
            matmul(X[2, rows], w[:, :512])
            + matmul(X[1, rows], w[:, 512:])
            + contract_first(condv[:, rows], wct[q])
        )
        a = jnp.tanh(preact[:, :256])
        g = 0.5 * jnp.tanh(0.5 * preact[:, 256:]) + 0.5
        X[0, rows, q * 256 : q * 256 + 256] = (a * g).astype(BF16)
        dg = D[2 + q, rows].astype(F32)
        t = (dg[:, :256] + dg[:, 256:]) * g
        D[2 + q, rows, 0:256] = (t * (1.0 - a * a)).astype(BF16)
        D[2 + q, rows, 256:512] = (t * a * (1.0 - g)).astype(BF16)

    def gated_copy(i):
        return pltpu.make_async_copy(X.at[0, at(i)], gated_hbm.at[at(i)], st_g.at[i])

    whole = (T - TILE) // BIG
    for q in range(2):
        if q == 1:
            wait(along_core, 1)

        def forward_body(j, carry, q=q):
            forward(pl.ds(pl.multiple_of(TILE + j * BIG, TILE), BIG), q)
            if q == 1:
                for n in range(BIG // TILE):
                    gated_copy(1 + j * (BIG // TILE) + n).start()
            return carry

        lax.fori_loop(0, 1, forward_body, 0)
        lax.fori_loop(1, whole, forward_body, 0)
        for i in range(1 + whole * (BIG // TILE), tiles):
            forward(at(i), q)
            if q == 1:
                gated_copy(i).start()

    @pl.when(dp > 0)
    def _():
        for n in range(PIECES):
            halo_copy(n).wait_recv()

    put(0, halo[...])
    lag_tile(0)
    forward(at(0), 0)
    forward(at(0), 1)
    gated_copy(0).start()

    def back(i, tap):
        w0 = W[0].reshape(512, 1024)[:, tap * 512 : tap * 512 + 512]
        w1 = W[1].reshape(512, 1024)[:, tap * 512 : tap * 512 + 512]
        return contract_last(D[2, at(i)], w0) + contract_last(D[3, at(i)], w1)

    first = back(0, 0) * keep(0)
    put(0, first)
    ret_send[...] = first.astype(BF16)

    def ret_copy(n):
        rows = pl.ds(pl.multiple_of(n * (DMAX // PIECES), DMAX // PIECES), DMAX // PIECES)
        return rcopy(ret_send.at[rows], ret_recv.at[rows], h_s.at[PIECES + n], h_r.at[PIECES + n], (dp - 1, fs))

    def send_back(n):
        @pl.when(dp > 0)
        def _():
            ret_copy(n).start()

    send_back(0)
    send_back(1)

    def to_core(k):
        return rcopy(CS.at[k], CR.at[k], rs_s.at[k, 0], rs_r.at[k, 0], sib)

    def to_first(k):
        return [
            rcopy(S1y.at[k], R1y.at[k], rs_s.at[k, 1], rs_r.at[k, 1], yn),
            rcopy(S1x.at[k], R1x.at[k], rs_s.at[k, 2], rs_r.at[k, 2], xn),
        ]

    def to_second(k):
        return [
            rcopy(S2y.at[k], R2y.at[k], rs_s.at[k, 3], rs_r.at[k, 3], xn),
            rcopy(S2x.at[k], R2x.at[k], rs_s.at[k, 4], rs_r.at[k, 4], yn),
        ]

    def to_z(k):
        return [
            rcopy(S3.at[k, zs[n]], R3.at[k, n], rs_s.at[k, 5 + n], rs_r.at[k, 5 + n], zn[n]) for n in range(3)
        ]

    A, B = pl.ds(0, SPLIT), pl.ds(SPLIT, 512 - SPLIT)

    def stage0(k):
        CS[k] = Gt[:, :, :, c1].astype(BF16)
        to_core(k).start()
        GA[k] = Gt[:, :, :, c]

    def stage1(k):
        to_core(k).wait()
        S1y[k] = (GA[k, :, :, y1, :, A] + CR[k, :, :, y1, :, A].astype(F32)).astype(BF16)
        S1x[k] = (GA[k, :, x1, :, :, B] + CR[k, :, x1, :, :, B].astype(F32)).astype(BF16)
        for copy in to_first(k):
            copy.start()
        GA[k, :, :, y, :, A] += CR[k, :, :, y, :, A].astype(F32)
        GA[k, :, x, :, :, B] += CR[k, :, x, :, :, B].astype(F32)

    def stage2(k):
        for copy in to_first(k):
            copy.wait()
        S2y[k] = (GA[k, :, x1, y, :, A] + R1y[k, :, x1].astype(F32)).astype(BF16)
        S2x[k] = (GA[k, :, x, y1, :, B] + R1x[k, :, y1].astype(F32)).astype(BF16)
        for copy in to_second(k):
            copy.start()
        GA[k, :, x, y, :, A] += R1y[k, :, x].astype(F32)
        GA[k, :, x, y, :, B] += R1x[k, :, y].astype(F32)

    def stage3(k):
        for copy in to_second(k):
            copy.wait()
        one = GA[k, :, x, y, :, A] + R2y[k].astype(F32)
        two = GA[k, :, x, y, :, B] + R2x[k].astype(F32)
        S3[k, :, :, A] = one.astype(BF16)
        S3[k, :, :, B] = two.astype(BF16)
        for copy in to_z(k):
            copy.start()
        GA[k, :, x, y, :, A] = one
        GA[k, :, x, y, :, B] = two

    def stage4(k):
        for copy in to_z(k):
            copy.wait()
        total = GA[k, z, x, y]
        for n in range(3):
            total = total + R3[k, n].astype(F32)
        return total

    cond_core = rcopy(cCS, cCR, rs_s.at[6, 0], rs_r.at[6, 0], sib)
    cond_first = rcopy(cS1, cR1, rs_s.at[6, 1], rs_r.at[6, 1], yn)
    cond_second = rcopy(cS2, cR2, rs_s.at[6, 2], rs_r.at[6, 2], xn)
    cond_z = [rcopy(cS3.at[zs[n]], cR3.at[n], rs_s.at[6, 3 + n], rs_r.at[6, 3 + n], zn[n]) for n in range(3)]

    def three_parts(value):
        parts = []
        for _ in range(3):
            parts.append(value.astype(BF16))
            value = value - parts[-1].astype(F32)
        return jnp.concatenate(parts + [jnp.zeros((13, 512), BF16)], 0)

    def cond_stage0():
        bias_row = matmul(three_parts(bres), bias_places(0)) + matmul(three_parts(bskip), bias_places(1))
        bias_row = jnp.sum(bias_row, axis=0, keepdims=True)
        one, two = matmul(condv[...], D[2]), matmul(condv[...], D[3])
        grad = jnp.concatenate([one[:, :256], two[:, :256], one[:, 256:], two[:, 256:]], 1)
        place = lax.broadcasted_iota(jnp.int32, (128, 1024), 0)
        cGA[...] = jnp.where(place == 81, bias_row, grad).T.reshape(4, 2, 2, 2, 32, 128)
        cCS[...] = cGA[:, :, :, c1].astype(BF16)
        cond_core.start()

    def cond_stage1():
        cond_core.wait()
        cS1[...] = (cGA[:, :, y1, c] + cCR[:, :, y1].astype(F32)).astype(BF16)
        cond_first.start()
        cGA[:, :, y, c] += cCR[:, :, y].astype(F32)

    def cond_stage2():
        cond_first.wait()
        cS2[...] = (cGA[:, x1, y, c] + cR1[:, x1].astype(F32)).astype(BF16)
        cond_second.start()
        cGA[:, x, y, c] += cR1[:, x].astype(F32)

    def cond_stage3():
        cond_second.wait()
        total = cGA[:, x, y, c] + cR2[...].astype(F32)
        cS3[...] = total.astype(BF16)
        for copy in cond_z:
            copy.start()
        cGA[:, x, y, c] = total

    def cond_stage4():
        for copy in cond_z:
            copy.wait()
        total = cGA[z, x, y, c]
        for n in range(3):
            total = total + cR3[n].astype(F32)
        gcond_ref[...] = total

    for k in range(6):
        left, right = k // 2, k % 2 + 2 * (k >= 2)
        Gt[...] = contract_first(X[left], D[right]).reshape(4, 2, 2, 2, 16, 512)
        stage0(k)
        if k >= 1:
            stage1(k - 1)
        if k >= 3:
            stage2(k - 3)
        if k >= 5:
            stage3(k - 5)
        send_back(k + 2)

    def e_copy(i):
        return pltpu.make_async_copy(X.at[2, at(i)], e_hbm.at[at(i)], st_e.at[i])

    def e_tile(i):
        X[2, at(i)] = (D[0, at(i)].astype(F32) + back(i, 1) + shifted(dilate)).astype(BF16)
        e_copy(i).start()

    cond_stage0()
    stage1(5)
    stage2(3)
    after = {
        0: [(stage3, 1)],
        1: [(stage2, 4), (stage3, 2), (cond_stage1,)],
        2: [(stage2, 5), (stage3, 3)],
        3: [(stage3, 4), (cond_stage2,)],
        4: [(stage3, 5)],
        5: [(cond_stage3,)],
    }
    for e in range(tiles - 1):
        put(1, back(e + 1, 0) * keep(e + 1))
        e_tile(e)
        F[:, 0:TILE] = F[:, TILE : 2 * TILE]
        for stage, *k in after.get(e, []):
            stage(*k)

    @pl.when(dp < 7)
    def _():
        for n in range(PIECES):
            ret_copy(n).wait_recv()

    put(1, ret_recv[...])
    e_tile(tiles - 1)
    cond_stage4()
    gres_ref[...] = stage4(0)
    gskip_ref[...] = stage4(1)
    for k in range(2, 6):
        total, q = stage4(k), k % 2
        for n in range(2):
            to = n * 512 + q * 256
            gconv_ref[1 - (k - 2) // 2, :, to : to + 256] = total[:, n * 256 : n * 256 + 256]

    def finish(i, carry):
        gated_copy(i).wait()
        e_copy(i).wait()
        return carry

    lax.fori_loop(0, tiles, finish, 0)
    wrs_copy.wait()

    @pl.when(dp < 7)
    def _():
        for n in range(PIECES):
            halo_copy(n).wait_send()

    @pl.when(dp > 0)
    def _():
        for n in range(PIECES):
            ret_copy(n).wait_send()


def output_kernel(
    gated_ref, sig_ref, e_ref, w_ref, bias_ref, gconv_ref, gres_ref, gskip_ref, gcond_ref,
    res_ref, skip_ref, grad_ref, conv_out, res_out, skip_out, cond_out, bconv_out, bres_out, bskip_out,
):
    gated, w = gated_ref[...], w_ref[...]
    res = sig_ref[...].astype(F32) + matmul(gated, w[:, :512]) + bias_ref[1:2, 0:512]
    res_ref[...] = res.astype(BF16)
    skip_ref[...] = (matmul(gated, w[:, 512:]) + bias_ref[1:2, 512:1024]).astype(BF16)
    grad_ref[...] = e_ref[...].astype(F32)

    @pl.when(pl.program_id(0) == 0)
    def _():
        conv_out[...] = gconv_ref[...]
        res_out[...] = gres_ref[...]
        skip_out[...] = gskip_ref[...]
        cond_out[...] = gcond_ref[:, 0:80]

        def as_row(value):
            size = value.shape[0]
            square = jnp.broadcast_to(value, (size, size))
            first = lax.broadcasted_iota(jnp.int32, (size, size), 0)
            second = lax.broadcasted_iota(jnp.int32, (size, size), 1)
            return jnp.sum(jnp.where(first == second, square, 0.0), axis=0, keepdims=True)

        bconv_out[...] = as_row(gcond_ref[:, 80:81])
        bres_out[...] = as_row(gcond_ref[0:16, 81:82])
        bskip_out[...] = as_row(gcond_ref[16:32, 81:82])


def shards(
    signal, cond, clip_lengths, dilation, w_conv, w_cond, b_conv, w_res, b_res, w_skip, b_skip, cot_res, cot_skip
):
    T = signal.shape[1]
    tiles = T // TILE
    sig, conds, cr, cs = signal[0], cond[0], cot_res[0], cot_skip[0]
    vmem, hbm, smem = (pl.BlockSpec(memory_space=m) for m in (pltpu.VMEM, pl.ANY, pltpu.SMEM))
    dma = pltpu.SemaphoreType.DMA
    out = jax.ShapeDtypeStruct
    gated, e, wrs, bias, gconv, gres, gskip, gcond = pl.pallas_call(
        layer_kernel,
        out_shape=[
            out((T, 512), BF16),
            out((T, 512), BF16),
            out((4, 2, 2, 2, 16, 1024), BF16),
            out((16, 1024), F32),
            out((2, 16, 1024), F32),
            out((16, 512), F32),
            out((16, 512), F32),
            out((32, 128), F32),
        ],
        in_specs=[smem, smem] + [vmem] * 7 + [hbm] * 4,
        out_specs=[hbm] * 3 + [vmem] * 5,
        scratch_shapes=[
            pltpu.VMEM((3, T, 512), BF16),
            pltpu.VMEM((4, T, 512), BF16),
            pltpu.VMEM((128, T), BF16),
            pltpu.VMEM((3, 4, 2, 2, 2, 16, 1024), BF16),
            pltpu.VMEM((4, 2, 2, 2, 32, 128), BF16),
            pltpu.VMEM((32, 128), F32),
            pltpu.VMEM((2, 128, 512), BF16),
            pltpu.VMEM((4, 2 * TILE, 128), F32),
            pltpu.VMEM((DMAX, 512), BF16),
            pltpu.VMEM((DMAX, 512), BF16),
            pltpu.VMEM((DMAX, 512), BF16),
            pltpu.VMEM((4, 2, 2, 2, 16, 512), F32),
            pltpu.VMEM((6, 4, 2, 2, 16, 512), F32),
            pltpu.VMEM((6, 4, 2, 2, 16, 512), BF16),
            pltpu.VMEM((6, 4, 2, 2, 16, 512), BF16),
            pltpu.VMEM((6, 4, 2, 16, SPLIT), BF16),
            pltpu.VMEM((6, 4, 2, 16, SPLIT), BF16),
            pltpu.VMEM((6, 4, 2, 16, 512 - SPLIT), BF16),
            pltpu.VMEM((6, 4, 2, 16, 512 - SPLIT), BF16),
            pltpu.VMEM((6, 4, 16, SPLIT), BF16),
            pltpu.VMEM((6, 4, 16, SPLIT), BF16),
            pltpu.VMEM((6, 4, 16, 512 - SPLIT), BF16),
            pltpu.VMEM((6, 4, 16, 512 - SPLIT), BF16),
            pltpu.VMEM((6, 4, 16, 512), BF16),
            pltpu.VMEM((6, 3, 16, 512), BF16),
            pltpu.VMEM((4, 2, 2, 2, 32, 128), F32),
            pltpu.VMEM((4, 2, 2, 32, 128), BF16),
            pltpu.VMEM((4, 2, 2, 32, 128), BF16),
            pltpu.VMEM((4, 2, 32, 128), BF16),
            pltpu.VMEM((4, 2, 32, 128), BF16),
            pltpu.VMEM((4, 32, 128), BF16),
            pltpu.VMEM((4, 32, 128), BF16),
            pltpu.VMEM((4, 32, 128), BF16),
            pltpu.VMEM((3, 32, 128), BF16),
            dma((4,)),
            dma((tiles,)),
            dma((tiles,)),
            dma((1,)),
            dma((4, 8)),
            dma((4, 8)),
            dma((2 * PIECES,)),
            dma((2 * PIECES,)),
            dma((7, 8)),
            dma((7, 8)),
        ],
        compiler_params=pltpu.CompilerParams(
            collective_id=0, has_side_effects=True, vmem_limit_bytes=60 << 20
        ),
        name="layer",
    )(
        clip_lengths, dilation, w_conv, w_res, w_skip, w_cond.T, b_conv[None], b_res[None], b_skip[None], sig, conds, cr, cs
    )

    rows = pl.BlockSpec((OUT_TILE, 512), lambda i: (i, 0))

    def whole(array):
        return pl.BlockSpec(array.shape, lambda i: (0,) * len(array.shape))

    small = [wrs.reshape(512, 1024), bias, gconv, gres, gskip, gcond]
    sums = [out(g.shape, F32) for g in (gconv, gres, gskip)] + [out(shape, F32) for shape in ((32, 80), (1, 32), (1, 16), (1, 16))]
    res_out, skip_out, grad_signal, gconv, gres, gskip, gcond, gbconv, gbres, gbskip = pl.pallas_call(
        output_kernel,
        grid=(T // OUT_TILE,),
        in_specs=[rows] * 3 + [whole(array) for array in small],
        out_specs=[rows] * 3 + [whole(array) for array in sums],
        out_shape=[out((T, 512), BF16), out((T, 512), BF16), out((T, 512), F32)] + sums,
        compiler_params=pltpu.CompilerParams(vmem_limit_bytes=60 << 20),
        name="outputs",
    )(gated, sig, e, *small)
    return (
        res_out[None],
        skip_out[None],
        grad_signal[None],
        gconv,
        gcond.T,
        gbconv[0],
        gres,
        gbres[0],
        gskip,
        gbskip[0],
    )


def from_behind(value, axis, steps):
    count = lax.axis_size(axis)
    first, last = (max(0, -steps), min(count, count - steps))
    return lax.ppermute(value, axis, [(source, source + steps) for source in range(first, last)])


def shards_any(
    signal,
    cond,
    clip_lengths,
    dilation,
    w_conv,
    w_cond,
    b_conv,
    w_res,
    b_res,
    w_skip,
    b_skip,
    cot_res,
    cot_skip,
):
    rows = signal.shape[1]
    chans = signal.shape[2]
    conv_full, cond_full, bconv_full, res_full, bres_full, skip_full, bskip_full = (
        lax.all_gather(w_conv, ("dp", "fsdp"), axis=1, tiled=True),
        lax.all_gather(w_cond, ("dp", "fsdp"), axis=1, tiled=True),
        lax.all_gather(b_conv, ("dp", "fsdp"), axis=0, tiled=True),
        lax.all_gather(w_res, ("dp", "fsdp"), axis=0, tiled=True),
        lax.all_gather(b_res, ("dp", "fsdp"), axis=0, tiled=True),
        lax.all_gather(w_skip, ("dp", "fsdp"), axis=0, tiled=True),
        lax.all_gather(b_skip, ("dp", "fsdp"), axis=0, tiled=True),
    )
    segment = lax.axis_index("dp")
    times = segment * rows + jnp.arange(rows, dtype=jnp.int32)
    lengths = clip_lengths[0]
    starts = jnp.cumsum(lengths) - lengths
    begin = jnp.max(jnp.where(starts[None, :] <= times[:, None], starts[None, :], 0), axis=1)
    dilate = dilation[0]
    keep = times - begin >= dilate
    mask_low = keep.astype(jnp.bfloat16)
    samples = signal[0]
    conds = cond[0]
    tail = from_behind(samples[rows - DMAX :], "dp", 1)
    extended = jnp.concatenate([tail, samples], 0)
    lagged = lax.dynamic_slice_in_dim(extended, DMAX - dilate, rows, 0) * mask_low[:, None]
    preact = (
        matmul(lagged, conv_full[0])
        + matmul(samples, conv_full[1])
        + contract_first(conds, cond_full)
        + bconv_full.astype(jnp.float32)
    )
    half = preact.shape[1] // 2
    tanh_part = jnp.tanh(preact[:, :half])
    sig_part = jax.nn.sigmoid(preact[:, half:])
    gated = (tanh_part * sig_part).astype(jnp.bfloat16)
    res_out = (
        samples.astype(jnp.float32) + matmul(gated, res_full) + bres_full.astype(jnp.float32)
    ).astype(jnp.bfloat16)
    skip_out = (matmul(gated, skip_full) + bskip_full.astype(jnp.float32)).astype(jnp.bfloat16)
    conv_back, cond_back, bconv_back, res_back, bres_back, skip_back, bskip_back = (
        lax.all_gather(w_conv, ("dp", "fsdp"), axis=1, tiled=True),
        lax.all_gather(w_cond, ("dp", "fsdp"), axis=1, tiled=True),
        lax.all_gather(b_conv, ("dp", "fsdp"), axis=0, tiled=True),
        lax.all_gather(w_res, ("dp", "fsdp"), axis=0, tiled=True),
        lax.all_gather(b_res, ("dp", "fsdp"), axis=0, tiled=True),
        lax.all_gather(w_skip, ("dp", "fsdp"), axis=0, tiled=True),
        lax.all_gather(b_skip, ("dp", "fsdp"), axis=0, tiled=True),
    )
    back_res = cot_res[0]
    back_skip = cot_skip[0]
    d_gated = contract_last(back_res, res_back) + contract_last(back_skip, skip_back)
    d_preact = jnp.concatenate(
        [
            d_gated * sig_part * (1.0 - tanh_part * tanh_part),
            d_gated * tanh_part * sig_part * (1.0 - sig_part),
        ],
        1,
    ).astype(jnp.bfloat16)
    grad_res = contract_first(gated, back_res)
    grad_bres = jnp.sum(back_res.astype(jnp.float32), axis=0)
    grad_skip = contract_first(gated, back_skip)
    grad_bskip = jnp.sum(back_skip.astype(jnp.float32), axis=0)
    grad_conv = jnp.stack([contract_first(lagged, d_preact), contract_first(samples, d_preact)])
    grad_cond = matmul(conds, d_preact)
    grad_bconv = jnp.sum(d_preact.astype(jnp.float32), axis=0)
    grad_in = back_res.astype(jnp.float32) + contract_last(d_preact, conv_back[1])
    d_lagged = contract_last(d_preact, conv_back[0]) * keep.astype(jnp.float32)[:, None]
    d_extended = jnp.zeros((DMAX + rows, chans), jnp.float32)
    d_extended = lax.dynamic_update_slice_in_dim(d_extended, d_lagged, DMAX - dilate, 0)
    grad_in = grad_in + d_extended[DMAX:]
    returned = from_behind(d_extended[:DMAX].astype(jnp.bfloat16), "dp", -1).astype(jnp.float32)
    grad_in = grad_in + jnp.concatenate([jnp.zeros((rows - DMAX, chans), jnp.float32), returned], 0)
    sums = (
        lax.psum_scatter(grad_conv, ("dp", "fsdp"), scatter_dimension=1, tiled=True),
        lax.psum_scatter(grad_cond, ("dp", "fsdp"), scatter_dimension=1, tiled=True),
        lax.psum_scatter(grad_bconv, ("dp", "fsdp"), scatter_dimension=0, tiled=True),
        lax.psum_scatter(grad_res, ("dp", "fsdp"), scatter_dimension=0, tiled=True),
        lax.psum_scatter(grad_bres, ("dp", "fsdp"), scatter_dimension=0, tiled=True),
        lax.psum_scatter(grad_skip, ("dp", "fsdp"), scatter_dimension=0, tiled=True),
        lax.psum_scatter(grad_bskip, ("dp", "fsdp"), scatter_dimension=0, tiled=True),
    )
    return (
        res_out[None],
        skip_out[None],
        grad_in[None],
        sums[0],
        sums[1],
        sums[2],
        sums[3],
        sums[4],
        sums[5],
        sums[6],
    )


def solution(mesh):
    return jax.shard_map(
        shards if dict(mesh.shape) == {"dp": 8, "fsdp": 4} else shards_any,
        mesh=mesh,
        in_specs=(
            P("fsdp", "dp", None),
            P("fsdp", None, "dp"),
            P("fsdp", None),
            P("fsdp"),
            P(None, ("dp", "fsdp"), None),
            P(None, ("dp", "fsdp")),
            P(("dp", "fsdp")),
            P(("dp", "fsdp"), None),
            P(("dp", "fsdp")),
            P(("dp", "fsdp"), None),
            P(("dp", "fsdp")),
            P("fsdp", "dp", None),
            P("fsdp", "dp", None),
        ),
        out_specs=(
            P("fsdp", "dp", None),
            P("fsdp", "dp", None),
            P("fsdp", "dp", None),
            P(None, ("dp", "fsdp"), None),
            P(None, ("dp", "fsdp")),
            P(("dp", "fsdp")),
            P(("dp", "fsdp"), None),
            P(("dp", "fsdp")),
            P(("dp", "fsdp"), None),
            P(("dp", "fsdp")),
        ),
        check_vma=False,
    )
```

```python
import functools

import jax
import jax.numpy as jnp
from jax import lax
from jax.experimental import pallas as pl
from jax.experimental.pallas import tpu as pltpu
from jax.sharding import PartitionSpec as P

DMAX = 512
TILE = 512
BIG = 1024
PIECES = 8
SPLIT = 384
OUT_TILE = 2048
MESH = pl.DeviceIdType.MESH
BF16 = jnp.bfloat16
F32 = jnp.float32


def matmul(left, right):
    return jnp.dot(left, right, preferred_element_type=F32)


def contract_first(left, right):
    return lax.dot_general(left, right, (((0,), (0,)), ((), ())), preferred_element_type=F32)


def contract_last(left, right):
    return lax.dot_general(left, right, (((1,), (1,)), ((), ())), preferred_element_type=F32)


def bias_places(skip):
    n = lax.broadcasted_iota(jnp.int32, (512, 1024), 0)
    m = lax.broadcasted_iota(jnp.int32, (512, 1024), 1)
    place = ((n >> 4) << 5) + (n & 15) + 16 * skip
    return jnp.where(place == m, 1.0, 0.0).astype(BF16)


def layer_kernel(
    clip_ref, dil_ref, wconv_ref, wres_ref, wskip_ref, wcond_ref, bconv_ref, bres_ref, bskip_ref, sig_hbm, cond_hbm, cr_hbm, cs_hbm,
    gated_hbm, e_hbm, wrs_hbm, bias_ref, gconv_ref, gres_ref, gskip_ref, gcond_ref,
    X, D, condv, W, WC, own_cond, wct, F, halo, ret_send, ret_recv,
    Gt, GA, CS, CR, S1y, R1y, S1x, R1x, S2y, R2y, S2x, R2x, S3, R3,
    cGA, cCS, cCR, cS1, cR1, cS2, cR2, cS3, cR3,
    ld, st_g, st_e, st_w, ag_s, ag_r, h_s, h_r, rs_s, rs_r,
):
    T = sig_hbm.shape[0]
    tiles = T // TILE
    dp, fs = lax.axis_index("dp"), lax.axis_index("fsdp")
    z, x, y, c = dp // 2, dp % 2, fs // 2, fs % 2
    x1, y1, c1 = 1 - x, 1 - y, 1 - c
    zs = (z + 1 - 2 * (z % 2), (z + 2) % 4, 3 - z)

    def dev(zz, xx, yy, cc):
        return (zz * 2 + xx, yy * 2 + cc)

    sib, xn, yn = dev(z, x, y, c1), dev(z, x1, y, c), dev(z, x, y1, c)
    zn = [dev(zz, x, y, c) for zz in zs]

    def rcopy(src, dst, ssem, rsem, to):
        return pltpu.make_async_remote_copy(
            src_ref=src, dst_ref=dst, send_sem=ssem, recv_sem=rsem, device_id=to, device_id_type=MESH
        )

    loads = [
        pltpu.make_async_copy(sig_hbm, X.at[1], ld.at[0]),
        pltpu.make_async_copy(cr_hbm, D.at[0], ld.at[1]),
        pltpu.make_async_copy(cs_hbm, D.at[1], ld.at[2]),
        pltpu.make_async_copy(cond_hbm, condv.at[pl.ds(0, 80)], ld.at[3]),
    ]
    for load in loads:
        load.start()

    extra = dp - 1 + 2 * x
    has_extra = (extra >= 0) & (extra < 8)
    barrier = pltpu.get_barrier_semaphore()
    for to in [sib, xn, yn] + zn:
        pl.semaphore_signal(barrier, inc=1, device_id=to, device_id_type=MESH)

    @pl.when(has_extra)
    def _():
        pl.semaphore_signal(barrier, inc=1, device_id=(extra, fs), device_id_type=MESH)
        pl.semaphore_wait(barrier, 7)

    @pl.when(jnp.logical_not(has_extra))
    def _():
        pl.semaphore_wait(barrier, 6)

    for q in range(2):
        for tap in range(2):
            for n in range(2):
                to = tap * 512 + n * 256
                W[q, z, x, y, c, :, to : to + 256] = wconv_ref[tap, :, n * 512 + q * 256 : n * 512 + q * 256 + 256]
    W[2, z, x, y, c, :, 0:512] = wres_ref[...]
    W[2, z, x, y, c, :, 512:1024] = wskip_ref[...]

    def column(ref):
        size = ref.shape[1]
        square = jnp.broadcast_to(ref[...].astype(F32), (size, size))
        diagonal = lax.broadcasted_iota(jnp.int32, (size, size), 0) == lax.broadcasted_iota(jnp.int32, (size, size), 1)
        return jnp.sum(jnp.where(diagonal, square, 0.0), axis=1, keepdims=True)

    own_cond[...] = jnp.zeros_like(own_cond)
    own_cond[:, 0:80] = wcond_ref[...].astype(F32)
    place = lax.broadcasted_iota(jnp.int32, (32, 128), 1)
    pair = jnp.concatenate([column(bres_ref), column(bskip_ref)], 0)
    WC[z, x, y, c] = jnp.where(place == 80, column(bconv_ref), jnp.where(place == 81, pair, own_cond[...])).astype(BF16)

    def along_z(s):
        own = W.at[s, z, x, y, c] if s < 3 else WC.at[z, x, y, c]
        return [rcopy(own, own, ag_s.at[s, k], ag_r.at[s, k], zn[k]) for k in range(3)]

    def along_one(s):
        if s < 3:
            a, b = W.at[s, :, x, y, c, :, pl.ds(0, 512)], W.at[s, :, x, y, c, :, pl.ds(512, 512)]
            return [
                rcopy(a, a, ag_s.at[s, 3], ag_r.at[s, 3], xn),
                rcopy(b, b, ag_s.at[s, 4], ag_r.at[s, 4], yn),
            ]
        a = WC.at[:, x, y, c]
        return [rcopy(a, a, ag_s.at[s, 3], ag_r.at[s, 3], xn)]

    def along_other(s):
        if s < 3:
            a, b = W.at[s, :, :, y, c, :, pl.ds(0, 512)], W.at[s, :, x, :, c, :, pl.ds(512, 512)]
            return [
                rcopy(a, a, ag_s.at[s, 5], ag_r.at[s, 5], yn),
                rcopy(b, b, ag_s.at[s, 6], ag_r.at[s, 6], xn),
            ]
        a = WC.at[:, :, y, c]
        return [rcopy(a, a, ag_s.at[s, 5], ag_r.at[s, 5], yn)]

    def along_core(s):
        a = W.at[s, :, :, :, c] if s < 3 else WC.at[:, :, :, c]
        return [rcopy(a, a, ag_s.at[s, 7], ag_r.at[s, 7], sib)]

    def start(phase, *sections):
        for s in sections:
            for copy in phase(s):
                copy.start()

    def wait(phase, *sections):
        for s in sections:
            for copy in phase(s):
                copy.wait()

    def halo_copy(n):
        size = DMAX // PIECES
        return rcopy(
            X.at[1, pl.ds(T - DMAX + n * size, size)], halo.at[pl.ds(n * size, size)], h_s.at[n], h_r.at[n], (dp + 1, fs)
        )

    def send_halo(first, last):
        @pl.when(dp < 7)
        def _():
            for n in range(first, last):
                halo_copy(n).start()

    start(along_z, 2)

    dilate = dil_ref[0]
    lane = lax.broadcasted_iota(jnp.int32, (1, 128), 1)
    starts = jnp.zeros((1, 128), jnp.int32)
    for i in range(16):
        starts = starts + jnp.where(lane > i, clip_ref[0, i], 0)
    row = lax.broadcasted_iota(jnp.int32, (TILE, 128), 0)

    def keep(i):
        times = dp * T + i * TILE + row
        inside = (starts <= times) & (starts > times - dilate)
        return 1.0 - jnp.max(jnp.where(inside, 1.0, 0.0), axis=1, keepdims=True)

    def at(i, size=TILE):
        return pl.ds(i * size if isinstance(i, int) else pl.multiple_of(i * size, size), size)

    def put(half, value):
        for n in range(4):
            F[n, half * TILE : half * TILE + TILE] = value[:, n * 128 : n * 128 + 128].astype(F32)

    def shifted(first):
        return jnp.concatenate([F[n, pl.ds(first, TILE), :] for n in range(4)], 1)

    def lag_tile(i):
        put(1, X[1, at(i)])
        X[2, at(i)] = (shifted(TILE - dilate) * keep(i)).astype(BF16)

    def lag_body(i, carry):
        put(0, X[1, at(i - 1)])
        lag_tile(i)
        return carry

    def sums_body(i, total):
        return (
            total[0] + jnp.sum(D[0, at(i)].astype(F32), axis=0, keepdims=True),
            total[1] + jnp.sum(D[1, at(i)].astype(F32), axis=0, keepdims=True),
        )

    def d_gated(rows):
        wrs = W[2].reshape(512, 1024)
        dg = contract_last(D[0, rows], wrs[:, :512]) + contract_last(D[1, rows], wrs[:, 512:])
        high = dg.astype(BF16)
        low = (dg - high.astype(F32)).astype(BF16)
        for q in range(2):
            D[2 + q, rows, 0:256] = high[:, q * 256 : q * 256 + 256]
            D[2 + q, rows, 256:512] = low[:, q * 256 : q * 256 + 256]

    loads[0].wait()
    lax.fori_loop(1, 2, lag_body, 0)
    wait(along_z, 2)
    start(along_one, 2)
    start(along_z, 0, 3, 1)
    lax.fori_loop(2, 4, lag_body, 0)
    wait(along_one, 2)
    start(along_other, 2)
    wait(along_z, 0, 3)
    start(along_one, 0, 3)
    wait(along_z, 1)
    start(along_one, 1)
    lax.fori_loop(4, tiles, lag_body, 0)
    wait(along_other, 2)
    start(along_core, 2)
    wait(along_one, 0, 3)
    start(along_other, 0, 3)
    wait(along_one, 1)
    start(along_other, 1)
    for load in loads[1:]:
        load.wait()
    zero = jnp.zeros((1, 512), F32)
    bres, bskip = lax.fori_loop(0, tiles, sums_body, (zero, zero))
    condv[80:96] = jnp.where(lax.broadcasted_iota(jnp.int32, (16, T), 0) == 0, 1.0, 0.0).astype(BF16)
    condv[96:128] = jnp.zeros((32, T), BF16)
    wait(along_core, 2)
    wrs_copy = pltpu.make_async_copy(W.at[2], wrs_hbm, st_w.at[0])
    wrs_copy.start()
    def dg_body(i, carry):
        d_gated(at(i, BIG))
        return carry

    lax.fori_loop(0, T // BIG // 2, dg_body, 0)
    wait(along_other, 0, 3)
    start(along_core, 0, 3)
    lax.fori_loop(T // BIG // 2, T // BIG, dg_body, 0)
    wait(along_other, 1)
    start(along_core, 1)
    send_halo(0, PIECES)

    @pl.when(dp == 0)
    def _():
        halo[...] = jnp.zeros_like(halo)

    @pl.when(dp == 7)
    def _():
        ret_recv[...] = jnp.zeros_like(ret_recv)

    wait(along_core, 0, 3)
    turned = WC[...].reshape(1024, 128).T
    for q in range(2):
        for n in range(2):
            wct[q, :, n * 256 : n * 256 + 256] = turned[:, n * 512 + q * 256 : n * 512 + q * 256 + 256]
    biases = turned[80:96]
    bias_ref[:, 0:512] = contract_last(biases, bias_places(0))
    bias_ref[:, 512:1024] = contract_last(biases, bias_places(1))

    def forward(rows, q):
        w = W[q].reshape(512, 1024)
        preact = (
            matmul(X[2, rows], w[:, :512])
            + matmul(X[1, rows], w[:, 512:])
            + contract_first(condv[:, rows], wct[q])
        )
        a = jnp.tanh(preact[:, :256])
        g = 0.5 * jnp.tanh(0.5 * preact[:, 256:]) + 0.5
        X[0, rows, q * 256 : q * 256 + 256] = (a * g).astype(BF16)
        dg = D[2 + q, rows].astype(F32)
        t = (dg[:, :256] + dg[:, 256:]) * g
        D[2 + q, rows, 0:256] = (t * (1.0 - a * a)).astype(BF16)
        D[2 + q, rows, 256:512] = (t * a * (1.0 - g)).astype(BF16)

    def gated_copy(i):
        return pltpu.make_async_copy(X.at[0, at(i)], gated_hbm.at[at(i)], st_g.at[i])

    whole = (T - TILE) // BIG
    for q in range(2):
        if q == 1:
            wait(along_core, 1)

        def forward_body(j, carry, q=q):
            forward(pl.ds(pl.multiple_of(TILE + j * BIG, TILE), BIG), q)
            if q == 1:
                for n in range(BIG // TILE):
                    gated_copy(1 + j * (BIG // TILE) + n).start()
            return carry

        lax.fori_loop(0, 1, forward_body, 0)
        lax.fori_loop(1, whole, forward_body, 0)
        for i in range(1 + whole * (BIG // TILE), tiles):
            forward(at(i), q)
            if q == 1:
                gated_copy(i).start()

    @pl.when(dp > 0)
    def _():
        for n in range(PIECES):
            halo_copy(n).wait_recv()

    put(0, halo[...])
    lag_tile(0)
    forward(at(0), 0)
    forward(at(0), 1)
    gated_copy(0).start()

    def back(i, tap):
        w0 = W[0].reshape(512, 1024)[:, tap * 512 : tap * 512 + 512]
        w1 = W[1].reshape(512, 1024)[:, tap * 512 : tap * 512 + 512]
        return contract_last(D[2, at(i)], w0) + contract_last(D[3, at(i)], w1)

    first = back(0, 0) * keep(0)
    put(0, first)
    ret_send[...] = first.astype(BF16)

    def ret_copy(n):
        rows = pl.ds(pl.multiple_of(n * (DMAX // PIECES), DMAX // PIECES), DMAX // PIECES)
        return rcopy(ret_send.at[rows], ret_recv.at[rows], h_s.at[PIECES + n], h_r.at[PIECES + n], (dp - 1, fs))

    def send_back(n):
        @pl.when(dp > 0)
        def _():
            ret_copy(n).start()

    send_back(0)
    send_back(1)

    def to_core(k):
        return rcopy(CS.at[k], CR.at[k], rs_s.at[k, 0], rs_r.at[k, 0], sib)

    def to_first(k):
        return [
            rcopy(S1y.at[k], R1y.at[k], rs_s.at[k, 1], rs_r.at[k, 1], yn),
            rcopy(S1x.at[k], R1x.at[k], rs_s.at[k, 2], rs_r.at[k, 2], xn),
        ]

    def to_second(k):
        return [
            rcopy(S2y.at[k], R2y.at[k], rs_s.at[k, 3], rs_r.at[k, 3], xn),
            rcopy(S2x.at[k], R2x.at[k], rs_s.at[k, 4], rs_r.at[k, 4], yn),
        ]

    def to_z(k):
        return [
            rcopy(S3.at[k, zs[n]], R3.at[k, n], rs_s.at[k, 5 + n], rs_r.at[k, 5 + n], zn[n]) for n in range(3)
        ]

    A, B = pl.ds(0, SPLIT), pl.ds(SPLIT, 512 - SPLIT)

    def stage0(k):
        CS[k] = Gt[:, :, :, c1].astype(BF16)
        to_core(k).start()
        GA[k] = Gt[:, :, :, c]

    def stage1(k):
        to_core(k).wait()
        S1y[k] = (GA[k, :, :, y1, :, A] + CR[k, :, :, y1, :, A].astype(F32)).astype(BF16)
        S1x[k] = (GA[k, :, x1, :, :, B] + CR[k, :, x1, :, :, B].astype(F32)).astype(BF16)
        for copy in to_first(k):
            copy.start()
        GA[k, :, :, y, :, A] += CR[k, :, :, y, :, A].astype(F32)
        GA[k, :, x, :, :, B] += CR[k, :, x, :, :, B].astype(F32)

    def stage2(k):
        for copy in to_first(k):
            copy.wait()
        S2y[k] = (GA[k, :, x1, y, :, A] + R1y[k, :, x1].astype(F32)).astype(BF16)
        S2x[k] = (GA[k, :, x, y1, :, B] + R1x[k, :, y1].astype(F32)).astype(BF16)
        for copy in to_second(k):
            copy.start()
        GA[k, :, x, y, :, A] += R1y[k, :, x].astype(F32)
        GA[k, :, x, y, :, B] += R1x[k, :, y].astype(F32)

    def stage3(k):
        for copy in to_second(k):
            copy.wait()
        one = GA[k, :, x, y, :, A] + R2y[k].astype(F32)
        two = GA[k, :, x, y, :, B] + R2x[k].astype(F32)
        S3[k, :, :, A] = one.astype(BF16)
        S3[k, :, :, B] = two.astype(BF16)
        for copy in to_z(k):
            copy.start()
        GA[k, :, x, y, :, A] = one
        GA[k, :, x, y, :, B] = two

    def stage4(k):
        for copy in to_z(k):
            copy.wait()
        total = GA[k, z, x, y]
        for n in range(3):
            total = total + R3[k, n].astype(F32)
        return total

    cond_core = rcopy(cCS, cCR, rs_s.at[6, 0], rs_r.at[6, 0], sib)
    cond_first = rcopy(cS1, cR1, rs_s.at[6, 1], rs_r.at[6, 1], yn)
    cond_second = rcopy(cS2, cR2, rs_s.at[6, 2], rs_r.at[6, 2], xn)
    cond_z = [rcopy(cS3.at[zs[n]], cR3.at[n], rs_s.at[6, 3 + n], rs_r.at[6, 3 + n], zn[n]) for n in range(3)]

    def three_parts(value):
        parts = []
        for _ in range(3):
            parts.append(value.astype(BF16))
            value = value - parts[-1].astype(F32)
        return jnp.concatenate(parts + [jnp.zeros((13, 512), BF16)], 0)

    def cond_stage0():
        bias_row = matmul(three_parts(bres), bias_places(0)) + matmul(three_parts(bskip), bias_places(1))
        bias_row = jnp.sum(bias_row, axis=0, keepdims=True)
        one, two = matmul(condv[...], D[2]), matmul(condv[...], D[3])
        grad = jnp.concatenate([one[:, :256], two[:, :256], one[:, 256:], two[:, 256:]], 1)
        place = lax.broadcasted_iota(jnp.int32, (128, 1024), 0)
        cGA[...] = jnp.where(place == 81, bias_row, grad).T.reshape(4, 2, 2, 2, 32, 128)
        cCS[...] = cGA[:, :, :, c1].astype(BF16)
        cond_core.start()

    def cond_stage1():
        cond_core.wait()
        cS1[...] = (cGA[:, :, y1, c] + cCR[:, :, y1].astype(F32)).astype(BF16)
        cond_first.start()
        cGA[:, :, y, c] += cCR[:, :, y].astype(F32)

    def cond_stage2():
        cond_first.wait()
        cS2[...] = (cGA[:, x1, y, c] + cR1[:, x1].astype(F32)).astype(BF16)
        cond_second.start()
        cGA[:, x, y, c] += cR1[:, x].astype(F32)

    def cond_stage3():
        cond_second.wait()
        total = cGA[:, x, y, c] + cR2[...].astype(F32)
        cS3[...] = total.astype(BF16)
        for copy in cond_z:
            copy.start()
        cGA[:, x, y, c] = total

    def cond_stage4():
        for copy in cond_z:
            copy.wait()
        total = cGA[z, x, y, c]
        for n in range(3):
            total = total + cR3[n].astype(F32)
        gcond_ref[...] = total

    def when(condition, work, *args):
        @pl.when(condition)
        def _():
            work(*args)

    def chunk_body(k, carry):
        left, right = k // 2, k % 2 + 2 * ((k + 4) // 6)
        Gt[...] = contract_first(X[left], D[right]).reshape(4, 2, 2, 2, 16, 512)
        stage0(k)
        when(k >= 1, stage1, k - 1)
        when(k >= 3, stage2, k - 3)
        when(k >= 5, stage3, k - 5)
        send_back(k + 2)
        return carry

    lax.fori_loop(0, 6, chunk_body, 0)
    cond_stage0()
    stage1(5)
    stage2(3)

    def e_copy(i):
        return pltpu.make_async_copy(X.at[2, at(i)], e_hbm.at[at(i)], st_e.at[i])

    def e_tile(i):
        X[2, at(i)] = (D[0, at(i)].astype(F32) + back(i, 1) + shifted(dilate)).astype(BF16)
        e_copy(i).start()

    def e_body(e, carry):
        put(1, back(e + 1, 0) * keep(e + 1))
        e_tile(e)
        F[:, 0:TILE] = F[:, TILE : 2 * TILE]
        when(e == 0, stage3, 1)
        when(e == 1, stage2, 4)
        when(e == 1, stage3, 2)
        when(e == 1, cond_stage1)
        when(e == 2, stage2, 5)
        when(e == 2, stage3, 3)
        when(e == 3, stage3, 4)
        when(e == 3, cond_stage2)
        when(e == 4, stage3, 5)
        when(e == 5, cond_stage3)
        return carry

    lax.fori_loop(0, tiles - 1, e_body, 0)

    @pl.when(dp < 7)
    def _():
        for n in range(PIECES):
            ret_copy(n).wait_recv()

    put(1, ret_recv[...])
    e_tile(tiles - 1)
    cond_stage4()
    gres_ref[...] = stage4(0)
    gskip_ref[...] = stage4(1)
    for k in range(2, 6):
        total, q = stage4(k), k % 2
        for n in range(2):
            to = n * 512 + q * 256
            gconv_ref[1 - (k - 2) // 2, :, to : to + 256] = total[:, n * 256 : n * 256 + 256]

    def finish(i, carry):
        gated_copy(i).wait()
        e_copy(i).wait()
        return carry

    lax.fori_loop(0, tiles, finish, 0)
    wrs_copy.wait()

    @pl.when(dp < 7)
    def _():
        for n in range(PIECES):
            halo_copy(n).wait_send()

    @pl.when(dp > 0)
    def _():
        for n in range(PIECES):
            ret_copy(n).wait_send()


def output_kernel(
    gated_ref, sig_ref, e_ref, w_ref, bias_ref, gconv_ref, gres_ref, gskip_ref, gcond_ref,
    res_ref, skip_ref, grad_ref, conv_out, res_out, skip_out, cond_out, bconv_out, bres_out, bskip_out,
):
    gated, w = gated_ref[...], w_ref[...]
    res = sig_ref[...].astype(F32) + matmul(gated, w[:, :512]) + bias_ref[1:2, 0:512]
    res_ref[...] = res.astype(BF16)
    skip_ref[...] = (matmul(gated, w[:, 512:]) + bias_ref[1:2, 512:1024]).astype(BF16)
    grad_ref[...] = e_ref[...].astype(F32)

    @pl.when(pl.program_id(0) == 0)
    def _():
        conv_out[...] = gconv_ref[...]
        res_out[...] = gres_ref[...]
        skip_out[...] = gskip_ref[...]
        cond_out[...] = gcond_ref[:, 0:80]

        def as_row(value):
            size = value.shape[0]
            square = jnp.broadcast_to(value, (size, size))
            first = lax.broadcasted_iota(jnp.int32, (size, size), 0)
            second = lax.broadcasted_iota(jnp.int32, (size, size), 1)
            return jnp.sum(jnp.where(first == second, square, 0.0), axis=0, keepdims=True)

        bconv_out[...] = as_row(gcond_ref[:, 80:81])
        bres_out[...] = as_row(gcond_ref[0:16, 81:82])
        bskip_out[...] = as_row(gcond_ref[16:32, 81:82])


def shards(
    signal, cond, clip_lengths, dilation, w_conv, w_cond, b_conv, w_res, b_res, w_skip, b_skip, cot_res, cot_skip
):
    T = signal.shape[1]
    tiles = T // TILE
    sig, conds, cr, cs = signal[0], cond[0], cot_res[0], cot_skip[0]
    vmem, hbm, smem = (pl.BlockSpec(memory_space=m) for m in (pltpu.VMEM, pl.ANY, pltpu.SMEM))
    dma = pltpu.SemaphoreType.DMA
    out = jax.ShapeDtypeStruct
    gated, e, wrs, bias, gconv, gres, gskip, gcond = pl.pallas_call(
        layer_kernel,
        out_shape=[
            out((T, 512), BF16),
            out((T, 512), BF16),
            out((4, 2, 2, 2, 16, 1024), BF16),
            out((16, 1024), F32),
            out((2, 16, 1024), F32),
            out((16, 512), F32),
            out((16, 512), F32),
            out((32, 128), F32),
        ],
        in_specs=[smem, smem] + [vmem] * 7 + [hbm] * 4,
        out_specs=[hbm] * 3 + [vmem] * 5,
        scratch_shapes=[
            pltpu.VMEM((3, T, 512), BF16),
            pltpu.VMEM((4, T, 512), BF16),
            pltpu.VMEM((128, T), BF16),
            pltpu.VMEM((3, 4, 2, 2, 2, 16, 1024), BF16),
            pltpu.VMEM((4, 2, 2, 2, 32, 128), BF16),
            pltpu.VMEM((32, 128), F32),
            pltpu.VMEM((2, 128, 512), BF16),
            pltpu.VMEM((4, 2 * TILE, 128), F32),
            pltpu.VMEM((DMAX, 512), BF16),
            pltpu.VMEM((DMAX, 512), BF16),
            pltpu.VMEM((DMAX, 512), BF16),
            pltpu.VMEM((4, 2, 2, 2, 16, 512), F32),
            pltpu.VMEM((6, 4, 2, 2, 16, 512), F32),
            pltpu.VMEM((6, 4, 2, 2, 16, 512), BF16),
            pltpu.VMEM((6, 4, 2, 2, 16, 512), BF16),
            pltpu.VMEM((6, 4, 2, 16, SPLIT), BF16),
            pltpu.VMEM((6, 4, 2, 16, SPLIT), BF16),
            pltpu.VMEM((6, 4, 2, 16, 512 - SPLIT), BF16),
            pltpu.VMEM((6, 4, 2, 16, 512 - SPLIT), BF16),
            pltpu.VMEM((6, 4, 16, SPLIT), BF16),
            pltpu.VMEM((6, 4, 16, SPLIT), BF16),
            pltpu.VMEM((6, 4, 16, 512 - SPLIT), BF16),
            pltpu.VMEM((6, 4, 16, 512 - SPLIT), BF16),
            pltpu.VMEM((6, 4, 16, 512), BF16),
            pltpu.VMEM((6, 3, 16, 512), BF16),
            pltpu.VMEM((4, 2, 2, 2, 32, 128), F32),
            pltpu.VMEM((4, 2, 2, 32, 128), BF16),
            pltpu.VMEM((4, 2, 2, 32, 128), BF16),
            pltpu.VMEM((4, 2, 32, 128), BF16),
            pltpu.VMEM((4, 2, 32, 128), BF16),
            pltpu.VMEM((4, 32, 128), BF16),
            pltpu.VMEM((4, 32, 128), BF16),
            pltpu.VMEM((4, 32, 128), BF16),
            pltpu.VMEM((3, 32, 128), BF16),
            dma((4,)),
            dma((tiles,)),
            dma((tiles,)),
            dma((1,)),
            dma((4, 8)),
            dma((4, 8)),
            dma((2 * PIECES,)),
            dma((2 * PIECES,)),
            dma((7, 8)),
            dma((7, 8)),
        ],
        compiler_params=pltpu.CompilerParams(
            collective_id=0, has_side_effects=True, vmem_limit_bytes=60 << 20
        ),
        name="layer",
    )(
        clip_lengths, dilation, w_conv, w_res, w_skip, w_cond.T, b_conv[None], b_res[None], b_skip[None], sig, conds, cr, cs
    )

    rows = pl.BlockSpec((OUT_TILE, 512), lambda i: (i, 0))

    def whole(array):
        return pl.BlockSpec(array.shape, lambda i: (0,) * len(array.shape))

    small = [wrs.reshape(512, 1024), bias, gconv, gres, gskip, gcond]
    sums = [out(g.shape, F32) for g in (gconv, gres, gskip)] + [out(shape, F32) for shape in ((32, 80), (1, 32), (1, 16), (1, 16))]
    res_out, skip_out, grad_signal, gconv, gres, gskip, gcond, gbconv, gbres, gbskip = pl.pallas_call(
        output_kernel,
        grid=(T // OUT_TILE,),
        in_specs=[rows] * 3 + [whole(array) for array in small],
        out_specs=[rows] * 3 + [whole(array) for array in sums],
        out_shape=[out((T, 512), BF16), out((T, 512), BF16), out((T, 512), F32)] + sums,
        compiler_params=pltpu.CompilerParams(vmem_limit_bytes=60 << 20),
        name="outputs",
    )(gated, sig, e, *small)
    return (
        res_out[None],
        skip_out[None],
        grad_signal[None],
        gconv,
        gcond.T,
        gbconv[0],
        gres,
        gbres[0],
        gskip,
        gbskip[0],
    )


def from_behind(value, axis, steps):
    count = lax.axis_size(axis)
    first, last = (max(0, -steps), min(count, count - steps))
    return lax.ppermute(value, axis, [(source, source + steps) for source in range(first, last)])


def shards_any(
    signal,
    cond,
    clip_lengths,
    dilation,
    w_conv,
    w_cond,
    b_conv,
    w_res,
    b_res,
    w_skip,
    b_skip,
    cot_res,
    cot_skip,
):
    rows = signal.shape[1]
    chans = signal.shape[2]
    conv_full, cond_full, bconv_full, res_full, bres_full, skip_full, bskip_full = (
        lax.all_gather(w_conv, ("dp", "fsdp"), axis=1, tiled=True),
        lax.all_gather(w_cond, ("dp", "fsdp"), axis=1, tiled=True),
        lax.all_gather(b_conv, ("dp", "fsdp"), axis=0, tiled=True),
        lax.all_gather(w_res, ("dp", "fsdp"), axis=0, tiled=True),
        lax.all_gather(b_res, ("dp", "fsdp"), axis=0, tiled=True),
        lax.all_gather(w_skip, ("dp", "fsdp"), axis=0, tiled=True),
        lax.all_gather(b_skip, ("dp", "fsdp"), axis=0, tiled=True),
    )
    segment = lax.axis_index("dp")
    times = segment * rows + jnp.arange(rows, dtype=jnp.int32)
    lengths = clip_lengths[0]
    starts = jnp.cumsum(lengths) - lengths
    begin = jnp.max(jnp.where(starts[None, :] <= times[:, None], starts[None, :], 0), axis=1)
    dilate = dilation[0]
    keep = times - begin >= dilate
    mask_low = keep.astype(jnp.bfloat16)
    samples = signal[0]
    conds = cond[0]
    tail = from_behind(samples[rows - DMAX :], "dp", 1)
    extended = jnp.concatenate([tail, samples], 0)
    lagged = lax.dynamic_slice_in_dim(extended, DMAX - dilate, rows, 0) * mask_low[:, None]
    preact = (
        matmul(lagged, conv_full[0])
        + matmul(samples, conv_full[1])
        + contract_first(conds, cond_full)
        + bconv_full.astype(jnp.float32)
    )
    half = preact.shape[1] // 2
    tanh_part = jnp.tanh(preact[:, :half])
    sig_part = jax.nn.sigmoid(preact[:, half:])
    gated = (tanh_part * sig_part).astype(jnp.bfloat16)
    res_out = (
        samples.astype(jnp.float32) + matmul(gated, res_full) + bres_full.astype(jnp.float32)
    ).astype(jnp.bfloat16)
    skip_out = (matmul(gated, skip_full) + bskip_full.astype(jnp.float32)).astype(jnp.bfloat16)
    conv_back, cond_back, bconv_back, res_back, bres_back, skip_back, bskip_back = (
        lax.all_gather(w_conv, ("dp", "fsdp"), axis=1, tiled=True),
        lax.all_gather(w_cond, ("dp", "fsdp"), axis=1, tiled=True),
        lax.all_gather(b_conv, ("dp", "fsdp"), axis=0, tiled=True),
        lax.all_gather(w_res, ("dp", "fsdp"), axis=0, tiled=True),
        lax.all_gather(b_res, ("dp", "fsdp"), axis=0, tiled=True),
        lax.all_gather(w_skip, ("dp", "fsdp"), axis=0, tiled=True),
        lax.all_gather(b_skip, ("dp", "fsdp"), axis=0, tiled=True),
    )
    back_res = cot_res[0]
    back_skip = cot_skip[0]
    d_gated = contract_last(back_res, res_back) + contract_last(back_skip, skip_back)
    d_preact = jnp.concatenate(
        [
            d_gated * sig_part * (1.0 - tanh_part * tanh_part),
            d_gated * tanh_part * sig_part * (1.0 - sig_part),
        ],
        1,
    ).astype(jnp.bfloat16)
    grad_res = contract_first(gated, back_res)
    grad_bres = jnp.sum(back_res.astype(jnp.float32), axis=0)
    grad_skip = contract_first(gated, back_skip)
    grad_bskip = jnp.sum(back_skip.astype(jnp.float32), axis=0)
    grad_conv = jnp.stack([contract_first(lagged, d_preact), contract_first(samples, d_preact)])
    grad_cond = matmul(conds, d_preact)
    grad_bconv = jnp.sum(d_preact.astype(jnp.float32), axis=0)
    grad_in = back_res.astype(jnp.float32) + contract_last(d_preact, conv_back[1])
    d_lagged = contract_last(d_preact, conv_back[0]) * keep.astype(jnp.float32)[:, None]
    d_extended = jnp.zeros((DMAX + rows, chans), jnp.float32)
    d_extended = lax.dynamic_update_slice_in_dim(d_extended, d_lagged, DMAX - dilate, 0)
    grad_in = grad_in + d_extended[DMAX:]
    returned = from_behind(d_extended[:DMAX].astype(jnp.bfloat16), "dp", -1).astype(jnp.float32)
    grad_in = grad_in + jnp.concatenate([jnp.zeros((rows - DMAX, chans), jnp.float32), returned], 0)
    sums = (
        lax.psum_scatter(grad_conv, ("dp", "fsdp"), scatter_dimension=1, tiled=True),
        lax.psum_scatter(grad_cond, ("dp", "fsdp"), scatter_dimension=1, tiled=True),
        lax.psum_scatter(grad_bconv, ("dp", "fsdp"), scatter_dimension=0, tiled=True),
        lax.psum_scatter(grad_res, ("dp", "fsdp"), scatter_dimension=0, tiled=True),
        lax.psum_scatter(grad_bres, ("dp", "fsdp"), scatter_dimension=0, tiled=True),
        lax.psum_scatter(grad_skip, ("dp", "fsdp"), scatter_dimension=0, tiled=True),
        lax.psum_scatter(grad_bskip, ("dp", "fsdp"), scatter_dimension=0, tiled=True),
    )
    return (
        res_out[None],
        skip_out[None],
        grad_in[None],
        sums[0],
        sums[1],
        sums[2],
        sums[3],
        sums[4],
        sums[5],
        sums[6],
    )


def solution(mesh):
    return jax.shard_map(
        shards if dict(mesh.shape) == {"dp": 8, "fsdp": 4} else shards_any,
        mesh=mesh,
        in_specs=(
            P("fsdp", "dp", None),
            P("fsdp", None, "dp"),
            P("fsdp", None),
            P("fsdp"),
            P(None, ("dp", "fsdp"), None),
            P(None, ("dp", "fsdp")),
            P(("dp", "fsdp")),
            P(("dp", "fsdp"), None),
            P(("dp", "fsdp")),
            P(("dp", "fsdp"), None),
            P(("dp", "fsdp")),
            P("fsdp", "dp", None),
            P("fsdp", "dp", None),
        ),
        out_specs=(
            P("fsdp", "dp", None),
            P("fsdp", "dp", None),
            P("fsdp", "dp", None),
            P(None, ("dp", "fsdp"), None),
            P(None, ("dp", "fsdp")),
            P(("dp", "fsdp")),
            P(("dp", "fsdp"), None),
            P(("dp", "fsdp")),
            P(("dp", "fsdp"), None),
            P(("dp", "fsdp")),
        ),
        check_vma=False,
    )
```

```python
import functools

import jax
import jax.numpy as jnp
from jax import lax
from jax.experimental import pallas as pl
from jax.experimental.pallas import tpu as pltpu
from jax.sharding import PartitionSpec as P

DMAX = 512
TILE = 512
BIG = 1024
PIECES = 8
SPLIT = 384
OUT_TILE = 2048
MESH = pl.DeviceIdType.MESH
BF16 = jnp.bfloat16
F32 = jnp.float32


def matmul(left, right):
    return jnp.dot(left, right, preferred_element_type=F32)


def contract_first(left, right):
    return lax.dot_general(left, right, (((0,), (0,)), ((), ())), preferred_element_type=F32)


def contract_last(left, right):
    return lax.dot_general(left, right, (((1,), (1,)), ((), ())), preferred_element_type=F32)


def bias_places(skip):
    n = lax.broadcasted_iota(jnp.int32, (512, 1024), 0)
    m = lax.broadcasted_iota(jnp.int32, (512, 1024), 1)
    place = ((n >> 4) << 5) + (n & 15) + 16 * skip
    return jnp.where(place == m, 1.0, 0.0).astype(BF16)


def layer_kernel(
    clip_ref, dil_ref, wconv_ref, wres_ref, wskip_ref, wcond_ref, bconv_ref, bres_ref, bskip_ref, sig_hbm, cond_hbm, cr_hbm, cs_hbm,
    gated_hbm, e_hbm, wrs_hbm, bias_ref, gconv_ref, gres_ref, gskip_ref, gcond_ref,
    X, D, condv, W, WC, own_cond, wct, F, halo, ret_send, ret_recv,
    Gt, GA, CS, CR, S1y, R1y, S1x, R1x, S2y, R2y, S2x, R2x, S3, R3,
    cGA, cCS, cCR, cS1, cR1, cS2, cR2, cS3, cR3,
    ld, st_g, st_e, st_w, ag_s, ag_r, h_s, h_r, rs_s, rs_r,
):
    T = sig_hbm.shape[0]
    tiles = T // TILE
    dp, fs = lax.axis_index("dp"), lax.axis_index("fsdp")
    z, x, y, c = dp // 2, dp % 2, fs // 2, fs % 2
    x1, y1, c1 = 1 - x, 1 - y, 1 - c
    zs = (z + 1 - 2 * (z % 2), (z + 2) % 4, 3 - z)

    def dev(zz, xx, yy, cc):
        return (zz * 2 + xx, yy * 2 + cc)

    sib, xn, yn = dev(z, x, y, c1), dev(z, x1, y, c), dev(z, x, y1, c)
    zn = [dev(zz, x, y, c) for zz in zs]

    def rcopy(src, dst, ssem, rsem, to):
        return pltpu.make_async_remote_copy(
            src_ref=src, dst_ref=dst, send_sem=ssem, recv_sem=rsem, device_id=to, device_id_type=MESH
        )

    loads = [
        pltpu.make_async_copy(sig_hbm, X.at[1], ld.at[0]),
        pltpu.make_async_copy(cr_hbm, D.at[0], ld.at[1]),
        pltpu.make_async_copy(cs_hbm, D.at[1], ld.at[2]),
        pltpu.make_async_copy(cond_hbm, condv.at[pl.ds(0, 80)], ld.at[3]),
    ]
    for load in loads:
        load.start()

    extra = dp - 1 + 2 * x
    has_extra = (extra >= 0) & (extra < 8)
    barrier = pltpu.get_barrier_semaphore()
    for to in [sib, xn, yn] + zn:
        pl.semaphore_signal(barrier, inc=1, device_id=to, device_id_type=MESH)

    @pl.when(has_extra)
    def _():
        pl.semaphore_signal(barrier, inc=1, device_id=(extra, fs), device_id_type=MESH)
        pl.semaphore_wait(barrier, 7)

    @pl.when(jnp.logical_not(has_extra))
    def _():
        pl.semaphore_wait(barrier, 6)

    for q in range(2):
        for tap in range(2):
            for n in range(2):
                to = tap * 512 + n * 256
                W[q, z, x, y, c, :, to : to + 256] = wconv_ref[tap, :, n * 512 + q * 256 : n * 512 + q * 256 + 256]
    W[2, z, x, y, c, :, 0:512] = wres_ref[...]
    W[2, z, x, y, c, :, 512:1024] = wskip_ref[...]

    def column(ref):
        size = ref.shape[1]
        square = jnp.broadcast_to(ref[...].astype(F32), (size, size))
        diagonal = lax.broadcasted_iota(jnp.int32, (size, size), 0) == lax.broadcasted_iota(jnp.int32, (size, size), 1)
        return jnp.sum(jnp.where(diagonal, square, 0.0), axis=1, keepdims=True)

    own_cond[...] = jnp.zeros_like(own_cond)
    own_cond[:, 0:80] = wcond_ref[...].astype(F32)
    place = lax.broadcasted_iota(jnp.int32, (32, 128), 1)
    pair = jnp.concatenate([column(bres_ref), column(bskip_ref)], 0)
    WC[z, x, y, c] = jnp.where(place == 80, column(bconv_ref), jnp.where(place == 81, pair, own_cond[...])).astype(BF16)

    def along_z(s):
        own = W.at[s, z, x, y, c] if s < 3 else WC.at[z, x, y, c]
        return [rcopy(own, own, ag_s.at[s, k], ag_r.at[s, k], zn[k]) for k in range(3)]

    def along_one(s):
        if s < 3:
            a, b = W.at[s, :, x, y, c, :, pl.ds(0, 512)], W.at[s, :, x, y, c, :, pl.ds(512, 512)]
            return [
                rcopy(a, a, ag_s.at[s, 3], ag_r.at[s, 3], xn),
                rcopy(b, b, ag_s.at[s, 4], ag_r.at[s, 4], yn),
            ]
        a = WC.at[:, x, y, c]
        return [rcopy(a, a, ag_s.at[s, 3], ag_r.at[s, 3], xn)]

    def along_other(s):
        if s < 3:
            a, b = W.at[s, :, :, y, c, :, pl.ds(0, 512)], W.at[s, :, x, :, c, :, pl.ds(512, 512)]
            return [
                rcopy(a, a, ag_s.at[s, 5], ag_r.at[s, 5], yn),
                rcopy(b, b, ag_s.at[s, 6], ag_r.at[s, 6], xn),
            ]
        a = WC.at[:, :, y, c]
        return [rcopy(a, a, ag_s.at[s, 5], ag_r.at[s, 5], yn)]

    def along_core(s):
        a = W.at[s, :, :, :, c] if s < 3 else WC.at[:, :, :, c]
        return [rcopy(a, a, ag_s.at[s, 7], ag_r.at[s, 7], sib)]

    def start(phase, *sections):
        for s in sections:
            for copy in phase(s):
                copy.start()

    def wait(phase, *sections):
        for s in sections:
            for copy in phase(s):
                copy.wait()

    def halo_copy(n):
        size = DMAX // PIECES
        return rcopy(
            X.at[1, pl.ds(T - DMAX + n * size, size)], halo.at[pl.ds(n * size, size)], h_s.at[n], h_r.at[n], (dp + 1, fs)
        )

    def send_halo(first, last):
        @pl.when(dp < 7)
        def _():
            for n in range(first, last):
                halo_copy(n).start()

    start(along_z, 2)

    dilate = dil_ref[0]
    lane = lax.broadcasted_iota(jnp.int32, (1, 128), 1)
    starts = jnp.zeros((1, 128), jnp.int32)
    for i in range(16):
        starts = starts + jnp.where(lane > i, clip_ref[0, i], 0)
    row = lax.broadcasted_iota(jnp.int32, (TILE, 128), 0)

    def keep(i):
        times = dp * T + i * TILE + row
        inside = (starts <= times) & (starts > times - dilate)
        return 1.0 - jnp.max(jnp.where(inside, 1.0, 0.0), axis=1, keepdims=True)

    def at(i, size=TILE):
        return pl.ds(i * size if isinstance(i, int) else pl.multiple_of(i * size, size), size)

    def put(half, value):
        for n in range(4):
            F[n, half * TILE : half * TILE + TILE] = value[:, n * 128 : n * 128 + 128].astype(F32)

    def shifted(first):
        return jnp.concatenate([F[n, pl.ds(first, TILE), :] for n in range(4)], 1)

    def lag_tile(i):
        put(1, X[1, at(i)])
        X[2, at(i)] = (shifted(TILE - dilate) * keep(i)).astype(BF16)

    def lag_body(i, carry):
        put(0, X[1, at(i - 1)])
        lag_tile(i)
        return carry

    def sums_body(i, total):
        return (
            total[0] + jnp.sum(D[0, at(i)].astype(F32), axis=0, keepdims=True),
            total[1] + jnp.sum(D[1, at(i)].astype(F32), axis=0, keepdims=True),
        )

    def d_gated(rows):
        wrs = W[2].reshape(512, 1024)
        dg = contract_last(D[0, rows], wrs[:, :512]) + contract_last(D[1, rows], wrs[:, 512:])
        high = dg.astype(BF16)
        low = (dg - high.astype(F32)).astype(BF16)
        for q in range(2):
            D[2 + q, rows, 0:256] = high[:, q * 256 : q * 256 + 256]
            D[2 + q, rows, 256:512] = low[:, q * 256 : q * 256 + 256]

    loads[0].wait()
    lax.fori_loop(1, 2, lag_body, 0)
    wait(along_z, 2)
    start(along_one, 2)
    start(along_z, 0, 3, 1)
    lax.fori_loop(2, 4, lag_body, 0)
    wait(along_one, 2)
    start(along_other, 2)
    wait(along_z, 0, 3)
    start(along_one, 0, 3)
    wait(along_z, 1)
    start(along_one, 1)
    lax.fori_loop(4, tiles, lag_body, 0)
    wait(along_other, 2)
    start(along_core, 2)
    wait(along_one, 0, 3)
    start(along_other, 0, 3)
    wait(along_one, 1)
    start(along_other, 1)
    for load in loads[1:]:
        load.wait()
    zero = jnp.zeros((1, 512), F32)
    bres, bskip = lax.fori_loop(0, tiles, sums_body, (zero, zero))
    condv[80:96] = jnp.where(lax.broadcasted_iota(jnp.int32, (16, T), 0) == 0, 1.0, 0.0).astype(BF16)
    condv[96:128] = jnp.zeros((32, T), BF16)
    wait(along_core, 2)
    wrs_copy = pltpu.make_async_copy(W.at[2], wrs_hbm, st_w.at[0])
    wrs_copy.start()
    def dg_body(i, carry):
        d_gated(at(i, BIG))
        return carry

    lax.fori_loop(0, T // BIG // 2, dg_body, 0)
    wait(along_other, 0, 3)
    start(along_core, 0, 3)
    lax.fori_loop(T // BIG // 2, T // BIG, dg_body, 0)
    wait(along_other, 1)
    start(along_core, 1)
    send_halo(0, PIECES)

    @pl.when(dp == 0)
    def _():
        halo[...] = jnp.zeros_like(halo)

    @pl.when(dp == 7)
    def _():
        ret_recv[...] = jnp.zeros_like(ret_recv)

    wait(along_core, 0, 3)
    turned = WC[...].reshape(1024, 128).T
    for q in range(2):
        for n in range(2):
            wct[q, :, n * 256 : n * 256 + 256] = turned[:, n * 512 + q * 256 : n * 512 + q * 256 + 256]
    biases = turned[80:96]
    bias_ref[:, 0:512] = contract_last(biases, bias_places(0))
    bias_ref[:, 512:1024] = contract_last(biases, bias_places(1))

    def forward(rows, q):
        w = W[q].reshape(512, 1024)
        preact = (
            matmul(X[2, rows], w[:, :512])
            + matmul(X[1, rows], w[:, 512:])
            + contract_first(condv[:, rows], wct[q])
        )
        a = jnp.tanh(preact[:, :256])
        g = 0.5 * jnp.tanh(0.5 * preact[:, 256:]) + 0.5
        X[0, rows, q * 256 : q * 256 + 256] = (a * g).astype(BF16)
        dg = D[2 + q, rows].astype(F32)
        t = (dg[:, :256] + dg[:, 256:]) * g
        D[2 + q, rows, 0:256] = (t * (1.0 - a * a)).astype(BF16)
        D[2 + q, rows, 256:512] = (t * a * (1.0 - g)).astype(BF16)

    def gated_copy(i):
        return pltpu.make_async_copy(X.at[0, at(i)], gated_hbm.at[at(i)], st_g.at[0])

    whole = (T - TILE) // BIG
    for q in range(2):
        if q == 1:
            wait(along_core, 1)

        def forward_body(j, carry, q=q):
            forward(pl.ds(pl.multiple_of(TILE + j * BIG, TILE), BIG), q)
            if q == 1:
                for n in range(BIG // TILE):
                    gated_copy(1 + j * (BIG // TILE) + n).start()
            return carry

        lax.fori_loop(0, 1, forward_body, 0)
        lax.fori_loop(1, whole, forward_body, 0)
        for i in range(1 + whole * (BIG // TILE), tiles):
            forward(at(i), q)
            if q == 1:
                gated_copy(i).start()

    @pl.when(dp > 0)
    def _():
        for n in range(PIECES):
            halo_copy(n).wait_recv()

    put(0, halo[...])
    lag_tile(0)
    forward(at(0), 0)
    forward(at(0), 1)
    gated_copy(0).start()

    def back(i, tap):
        w0 = W[0].reshape(512, 1024)[:, tap * 512 : tap * 512 + 512]
        w1 = W[1].reshape(512, 1024)[:, tap * 512 : tap * 512 + 512]
        return contract_last(D[2, at(i)], w0) + contract_last(D[3, at(i)], w1)

    first = back(0, 0) * keep(0)
    put(0, first)
    ret_send[...] = first.astype(BF16)

    def ret_copy(n):
        rows = pl.ds(pl.multiple_of(n * (DMAX // PIECES), DMAX // PIECES), DMAX // PIECES)
        return rcopy(ret_send.at[rows], ret_recv.at[rows], h_s.at[PIECES + n], h_r.at[PIECES + n], (dp - 1, fs))

    def send_back(n):
        @pl.when(dp > 0)
        def _():
            ret_copy(n).start()

    send_back(0)
    send_back(1)

    def to_core(k):
        return rcopy(CS.at[k], CR.at[k], rs_s.at[k, 0], rs_r.at[k, 0], sib)

    def to_first(k):
        return [
            rcopy(S1y.at[k], R1y.at[k], rs_s.at[k, 1], rs_r.at[k, 1], yn),
            rcopy(S1x.at[k], R1x.at[k], rs_s.at[k, 2], rs_r.at[k, 2], xn),
        ]

    def to_second(k):
        return [
            rcopy(S2y.at[k], R2y.at[k], rs_s.at[k, 3], rs_r.at[k, 3], xn),
            rcopy(S2x.at[k], R2x.at[k], rs_s.at[k, 4], rs_r.at[k, 4], yn),
        ]

    def to_z(k):
        return [
            rcopy(S3.at[k, zs[n]], R3.at[k, n], rs_s.at[k, 5 + n], rs_r.at[k, 5 + n], zn[n]) for n in range(3)
        ]

    A, B = pl.ds(0, SPLIT), pl.ds(SPLIT, 512 - SPLIT)

    def stage0(k):
        CS[k] = Gt[:, :, :, c1].astype(BF16)
        to_core(k).start()
        GA[k] = Gt[:, :, :, c]

    def stage1(k):
        to_core(k).wait()
        S1y[k] = (GA[k, :, :, y1, :, A] + CR[k, :, :, y1, :, A].astype(F32)).astype(BF16)
        S1x[k] = (GA[k, :, x1, :, :, B] + CR[k, :, x1, :, :, B].astype(F32)).astype(BF16)
        for copy in to_first(k):
            copy.start()
        GA[k, :, :, y, :, A] += CR[k, :, :, y, :, A].astype(F32)
        GA[k, :, x, :, :, B] += CR[k, :, x, :, :, B].astype(F32)

    def stage2(k):
        for copy in to_first(k):
            copy.wait()
        S2y[k] = (GA[k, :, x1, y, :, A] + R1y[k, :, x1].astype(F32)).astype(BF16)
        S2x[k] = (GA[k, :, x, y1, :, B] + R1x[k, :, y1].astype(F32)).astype(BF16)
        for copy in to_second(k):
            copy.start()
        GA[k, :, x, y, :, A] += R1y[k, :, x].astype(F32)
        GA[k, :, x, y, :, B] += R1x[k, :, y].astype(F32)

    def stage3(k):
        for copy in to_second(k):
            copy.wait()
        one = GA[k, :, x, y, :, A] + R2y[k].astype(F32)
        two = GA[k, :, x, y, :, B] + R2x[k].astype(F32)
        S3[k, :, :, A] = one.astype(BF16)
        S3[k, :, :, B] = two.astype(BF16)
        for copy in to_z(k):
            copy.start()
        GA[k, :, x, y, :, A] = one
        GA[k, :, x, y, :, B] = two

    def stage4(k):
        for copy in to_z(k):
            copy.wait()
        total = GA[k, z, x, y]
        for n in range(3):
            total = total + R3[k, n].astype(F32)
        return total

    cond_core = rcopy(cCS, cCR, rs_s.at[6, 0], rs_r.at[6, 0], sib)
    cond_first = rcopy(cS1, cR1, rs_s.at[6, 1], rs_r.at[6, 1], yn)
    cond_second = rcopy(cS2, cR2, rs_s.at[6, 2], rs_r.at[6, 2], xn)
    cond_z = [rcopy(cS3.at[zs[n]], cR3.at[n], rs_s.at[6, 3 + n], rs_r.at[6, 3 + n], zn[n]) for n in range(3)]

    def three_parts(value):
        parts = []
        for _ in range(3):
            parts.append(value.astype(BF16))
            value = value - parts[-1].astype(F32)
        return jnp.concatenate(parts + [jnp.zeros((13, 512), BF16)], 0)

    def cond_stage0():
        bias_row = matmul(three_parts(bres), bias_places(0)) + matmul(three_parts(bskip), bias_places(1))
        bias_row = jnp.sum(bias_row, axis=0, keepdims=True)
        one, two = matmul(condv[...], D[2]), matmul(condv[...], D[3])
        grad = jnp.concatenate([one[:, :256], two[:, :256], one[:, 256:], two[:, 256:]], 1)
        place = lax.broadcasted_iota(jnp.int32, (128, 1024), 0)
        cGA[...] = jnp.where(place == 81, bias_row, grad).T.reshape(4, 2, 2, 2, 32, 128)
        cCS[...] = cGA[:, :, :, c1].astype(BF16)
        cond_core.start()

    def cond_stage1():
        cond_core.wait()
        cS1[...] = (cGA[:, :, y1, c] + cCR[:, :, y1].astype(F32)).astype(BF16)
        cond_first.start()
        cGA[:, :, y, c] += cCR[:, :, y].astype(F32)

    def cond_stage2():
        cond_first.wait()
        cS2[...] = (cGA[:, x1, y, c] + cR1[:, x1].astype(F32)).astype(BF16)
        cond_second.start()
        cGA[:, x, y, c] += cR1[:, x].astype(F32)

    def cond_stage3():
        cond_second.wait()
        total = cGA[:, x, y, c] + cR2[...].astype(F32)
        cS3[...] = total.astype(BF16)
        for copy in cond_z:
            copy.start()
        cGA[:, x, y, c] = total

    def cond_stage4():
        for copy in cond_z:
            copy.wait()
        total = cGA[z, x, y, c]
        for n in range(3):
            total = total + cR3[n].astype(F32)
        gcond_ref[...] = total

    def when(condition, work, *args):
        @pl.when(condition)
        def _():
            work(*args)

    def chunk_body(k, carry):
        left, right = k // 2, k % 2 + 2 * ((k + 4) // 6)
        Gt[...] = contract_first(X[left], D[right]).reshape(4, 2, 2, 2, 16, 512)
        stage0(k)
        when(k >= 1, stage1, k - 1)
        when(k >= 3, stage2, k - 3)
        when(k >= 5, stage3, k - 5)
        send_back(k + 2)
        return carry

    lax.fori_loop(0, 6, chunk_body, 0)
    cond_stage0()
    stage1(5)
    stage2(3)

    def e_copy(i):
        return pltpu.make_async_copy(X.at[2, at(i)], e_hbm.at[at(i)], st_e.at[0])

    def e_tile(i):
        X[2, at(i)] = (D[0, at(i)].astype(F32) + back(i, 1) + shifted(dilate)).astype(BF16)
        e_copy(i).start()

    def e_body(e, carry):
        put(1, back(e + 1, 0) * keep(e + 1))
        e_tile(e)
        F[:, 0:TILE] = F[:, TILE : 2 * TILE]
        when(e == 0, stage3, 1)
        when(e == 1, stage2, 4)
        when(e == 1, stage3, 2)
        when(e == 1, cond_stage1)
        when(e == 2, stage2, 5)
        when(e == 2, stage3, 3)
        when(e == 3, stage3, 4)
        when(e == 3, cond_stage2)
        when(e == 4, stage3, 5)
        when(e == 5, cond_stage3)
        return carry

    lax.fori_loop(0, tiles - 1, e_body, 0)

    @pl.when(dp < 7)
    def _():
        for n in range(PIECES):
            ret_copy(n).wait_recv()

    put(1, ret_recv[...])
    e_tile(tiles - 1)
    cond_stage4()
    gres_ref[...] = stage4(0)
    gskip_ref[...] = stage4(1)
    for k in range(2, 6):
        total, q = stage4(k), k % 2
        for n in range(2):
            to = n * 512 + q * 256
            gconv_ref[1 - (k - 2) // 2, :, to : to + 256] = total[:, n * 256 : n * 256 + 256]

    pltpu.make_async_copy(X.at[0], gated_hbm, st_g.at[0]).wait()
    pltpu.make_async_copy(X.at[2], e_hbm, st_e.at[0]).wait()
    wrs_copy.wait()

    @pl.when(dp < 7)
    def _():
        for n in range(PIECES):
            halo_copy(n).wait_send()

    @pl.when(dp > 0)
    def _():
        for n in range(PIECES):
            ret_copy(n).wait_send()


def output_kernel(
    gated_ref, sig_ref, e_ref, w_ref, bias_ref, gconv_ref, gres_ref, gskip_ref, gcond_ref,
    res_ref, skip_ref, grad_ref, conv_out, res_out, skip_out, cond_out, bconv_out, bres_out, bskip_out,
):
    gated, w = gated_ref[...], w_ref[...]
    res = sig_ref[...].astype(F32) + matmul(gated, w[:, :512]) + bias_ref[1:2, 0:512]
    res_ref[...] = res.astype(BF16)
    skip_ref[...] = (matmul(gated, w[:, 512:]) + bias_ref[1:2, 512:1024]).astype(BF16)
    grad_ref[...] = e_ref[...].astype(F32)

    @pl.when(pl.program_id(0) == 0)
    def _():
        conv_out[...] = gconv_ref[...]
        res_out[...] = gres_ref[...]
        skip_out[...] = gskip_ref[...]
        cond_out[...] = gcond_ref[:, 0:80]

        def as_row(value):
            size = value.shape[0]
            square = jnp.broadcast_to(value, (size, size))
            first = lax.broadcasted_iota(jnp.int32, (size, size), 0)
            second = lax.broadcasted_iota(jnp.int32, (size, size), 1)
            return jnp.sum(jnp.where(first == second, square, 0.0), axis=0, keepdims=True)

        bconv_out[...] = as_row(gcond_ref[:, 80:81])
        bres_out[...] = as_row(gcond_ref[0:16, 81:82])
        bskip_out[...] = as_row(gcond_ref[16:32, 81:82])


def shards(
    signal, cond, clip_lengths, dilation, w_conv, w_cond, b_conv, w_res, b_res, w_skip, b_skip, cot_res, cot_skip
):
    T = signal.shape[1]
    tiles = T // TILE
    sig, conds, cr, cs = signal[0], cond[0], cot_res[0], cot_skip[0]
    vmem, hbm, smem = (pl.BlockSpec(memory_space=m) for m in (pltpu.VMEM, pl.ANY, pltpu.SMEM))
    dma = pltpu.SemaphoreType.DMA
    out = jax.ShapeDtypeStruct
    gated, e, wrs, bias, gconv, gres, gskip, gcond = pl.pallas_call(
        layer_kernel,
        out_shape=[
            out((T, 512), BF16),
            out((T, 512), BF16),
            out((4, 2, 2, 2, 16, 1024), BF16),
            out((16, 1024), F32),
            out((2, 16, 1024), F32),
            out((16, 512), F32),
            out((16, 512), F32),
            out((32, 128), F32),
        ],
        in_specs=[smem, smem] + [vmem] * 7 + [hbm] * 4,
        out_specs=[hbm] * 3 + [vmem] * 5,
        scratch_shapes=[
            pltpu.VMEM((3, T, 512), BF16),
            pltpu.VMEM((4, T, 512), BF16),
            pltpu.VMEM((128, T), BF16),
            pltpu.VMEM((3, 4, 2, 2, 2, 16, 1024), BF16),
            pltpu.VMEM((4, 2, 2, 2, 32, 128), BF16),
            pltpu.VMEM((32, 128), F32),
            pltpu.VMEM((2, 128, 512), BF16),
            pltpu.VMEM((4, 2 * TILE, 128), F32),
            pltpu.VMEM((DMAX, 512), BF16),
            pltpu.VMEM((DMAX, 512), BF16),
            pltpu.VMEM((DMAX, 512), BF16),
            pltpu.VMEM((4, 2, 2, 2, 16, 512), F32),
            pltpu.VMEM((6, 4, 2, 2, 16, 512), F32),
            pltpu.VMEM((6, 4, 2, 2, 16, 512), BF16),
            pltpu.VMEM((6, 4, 2, 2, 16, 512), BF16),
            pltpu.VMEM((6, 4, 2, 16, SPLIT), BF16),
            pltpu.VMEM((6, 4, 2, 16, SPLIT), BF16),
            pltpu.VMEM((6, 4, 2, 16, 512 - SPLIT), BF16),
            pltpu.VMEM((6, 4, 2, 16, 512 - SPLIT), BF16),
            pltpu.VMEM((6, 4, 16, SPLIT), BF16),
            pltpu.VMEM((6, 4, 16, SPLIT), BF16),
            pltpu.VMEM((6, 4, 16, 512 - SPLIT), BF16),
            pltpu.VMEM((6, 4, 16, 512 - SPLIT), BF16),
            pltpu.VMEM((6, 4, 16, 512), BF16),
            pltpu.VMEM((6, 3, 16, 512), BF16),
            pltpu.VMEM((4, 2, 2, 2, 32, 128), F32),
            pltpu.VMEM((4, 2, 2, 32, 128), BF16),
            pltpu.VMEM((4, 2, 2, 32, 128), BF16),
            pltpu.VMEM((4, 2, 32, 128), BF16),
            pltpu.VMEM((4, 2, 32, 128), BF16),
            pltpu.VMEM((4, 32, 128), BF16),
            pltpu.VMEM((4, 32, 128), BF16),
            pltpu.VMEM((4, 32, 128), BF16),
            pltpu.VMEM((3, 32, 128), BF16),
            dma((4,)),
            dma((tiles,)),
            dma((tiles,)),
            dma((1,)),
            dma((4, 8)),
            dma((4, 8)),
            dma((2 * PIECES,)),
            dma((2 * PIECES,)),
            dma((7, 8)),
            dma((7, 8)),
        ],
        compiler_params=pltpu.CompilerParams(
            collective_id=0, has_side_effects=True, vmem_limit_bytes=60 << 20
        ),
        name="layer",
    )(
        clip_lengths, dilation, w_conv, w_res, w_skip, w_cond.T, b_conv[None], b_res[None], b_skip[None], sig, conds, cr, cs
    )

    rows = pl.BlockSpec((OUT_TILE, 512), lambda i: (i, 0))

    def whole(array):
        return pl.BlockSpec(array.shape, lambda i: (0,) * len(array.shape))

    small = [wrs.reshape(512, 1024), bias, gconv, gres, gskip, gcond]
    sums = [out(g.shape, F32) for g in (gconv, gres, gskip)] + [out(shape, F32) for shape in ((32, 80), (1, 32), (1, 16), (1, 16))]
    res_out, skip_out, grad_signal, gconv, gres, gskip, gcond, gbconv, gbres, gbskip = pl.pallas_call(
        output_kernel,
        grid=(T // OUT_TILE,),
        in_specs=[rows] * 3 + [whole(array) for array in small],
        out_specs=[rows] * 3 + [whole(array) for array in sums],
        out_shape=[out((T, 512), BF16), out((T, 512), BF16), out((T, 512), F32)] + sums,
        compiler_params=pltpu.CompilerParams(vmem_limit_bytes=60 << 20),
        name="outputs",
    )(gated, sig, e, *small)
    return (
        res_out[None],
        skip_out[None],
        grad_signal[None],
        gconv,
        gcond.T,
        gbconv[0],
        gres,
        gbres[0],
        gskip,
        gbskip[0],
    )


def from_behind(value, axis, steps):
    count = lax.axis_size(axis)
    first, last = (max(0, -steps), min(count, count - steps))
    return lax.ppermute(value, axis, [(source, source + steps) for source in range(first, last)])


def shards_any(
    signal,
    cond,
    clip_lengths,
    dilation,
    w_conv,
    w_cond,
    b_conv,
    w_res,
    b_res,
    w_skip,
    b_skip,
    cot_res,
    cot_skip,
):
    rows = signal.shape[1]
    chans = signal.shape[2]
    conv_full, cond_full, bconv_full, res_full, bres_full, skip_full, bskip_full = (
        lax.all_gather(w_conv, ("dp", "fsdp"), axis=1, tiled=True),
        lax.all_gather(w_cond, ("dp", "fsdp"), axis=1, tiled=True),
        lax.all_gather(b_conv, ("dp", "fsdp"), axis=0, tiled=True),
        lax.all_gather(w_res, ("dp", "fsdp"), axis=0, tiled=True),
        lax.all_gather(b_res, ("dp", "fsdp"), axis=0, tiled=True),
        lax.all_gather(w_skip, ("dp", "fsdp"), axis=0, tiled=True),
        lax.all_gather(b_skip, ("dp", "fsdp"), axis=0, tiled=True),
    )
    segment = lax.axis_index("dp")
    times = segment * rows + jnp.arange(rows, dtype=jnp.int32)
    lengths = clip_lengths[0]
    starts = jnp.cumsum(lengths) - lengths
    begin = jnp.max(jnp.where(starts[None, :] <= times[:, None], starts[None, :], 0), axis=1)
    dilate = dilation[0]
    keep = times - begin >= dilate
    mask_low = keep.astype(jnp.bfloat16)
    samples = signal[0]
    conds = cond[0]
    tail = from_behind(samples[rows - DMAX :], "dp", 1)
    extended = jnp.concatenate([tail, samples], 0)
    lagged = lax.dynamic_slice_in_dim(extended, DMAX - dilate, rows, 0) * mask_low[:, None]
    preact = (
        matmul(lagged, conv_full[0])
        + matmul(samples, conv_full[1])
        + contract_first(conds, cond_full)
        + bconv_full.astype(jnp.float32)
    )
    half = preact.shape[1] // 2
    tanh_part = jnp.tanh(preact[:, :half])
    sig_part = jax.nn.sigmoid(preact[:, half:])
    gated = (tanh_part * sig_part).astype(jnp.bfloat16)
    res_out = (
        samples.astype(jnp.float32) + matmul(gated, res_full) + bres_full.astype(jnp.float32)
    ).astype(jnp.bfloat16)
    skip_out = (matmul(gated, skip_full) + bskip_full.astype(jnp.float32)).astype(jnp.bfloat16)
    conv_back, cond_back, bconv_back, res_back, bres_back, skip_back, bskip_back = (
        lax.all_gather(w_conv, ("dp", "fsdp"), axis=1, tiled=True),
        lax.all_gather(w_cond, ("dp", "fsdp"), axis=1, tiled=True),
        lax.all_gather(b_conv, ("dp", "fsdp"), axis=0, tiled=True),
        lax.all_gather(w_res, ("dp", "fsdp"), axis=0, tiled=True),
        lax.all_gather(b_res, ("dp", "fsdp"), axis=0, tiled=True),
        lax.all_gather(w_skip, ("dp", "fsdp"), axis=0, tiled=True),
        lax.all_gather(b_skip, ("dp", "fsdp"), axis=0, tiled=True),
    )
    back_res = cot_res[0]
    back_skip = cot_skip[0]
    d_gated = contract_last(back_res, res_back) + contract_last(back_skip, skip_back)
    d_preact = jnp.concatenate(
        [
            d_gated * sig_part * (1.0 - tanh_part * tanh_part),
            d_gated * tanh_part * sig_part * (1.0 - sig_part),
        ],
        1,
    ).astype(jnp.bfloat16)
    grad_res = contract_first(gated, back_res)
    grad_bres = jnp.sum(back_res.astype(jnp.float32), axis=0)
    grad_skip = contract_first(gated, back_skip)
    grad_bskip = jnp.sum(back_skip.astype(jnp.float32), axis=0)
    grad_conv = jnp.stack([contract_first(lagged, d_preact), contract_first(samples, d_preact)])
    grad_cond = matmul(conds, d_preact)
    grad_bconv = jnp.sum(d_preact.astype(jnp.float32), axis=0)
    grad_in = back_res.astype(jnp.float32) + contract_last(d_preact, conv_back[1])
    d_lagged = contract_last(d_preact, conv_back[0]) * keep.astype(jnp.float32)[:, None]
    d_extended = jnp.zeros((DMAX + rows, chans), jnp.float32)
    d_extended = lax.dynamic_update_slice_in_dim(d_extended, d_lagged, DMAX - dilate, 0)
    grad_in = grad_in + d_extended[DMAX:]
    returned = from_behind(d_extended[:DMAX].astype(jnp.bfloat16), "dp", -1).astype(jnp.float32)
    grad_in = grad_in + jnp.concatenate([jnp.zeros((rows - DMAX, chans), jnp.float32), returned], 0)
    sums = (
        lax.psum_scatter(grad_conv, ("dp", "fsdp"), scatter_dimension=1, tiled=True),
        lax.psum_scatter(grad_cond, ("dp", "fsdp"), scatter_dimension=1, tiled=True),
        lax.psum_scatter(grad_bconv, ("dp", "fsdp"), scatter_dimension=0, tiled=True),
        lax.psum_scatter(grad_res, ("dp", "fsdp"), scatter_dimension=0, tiled=True),
        lax.psum_scatter(grad_bres, ("dp", "fsdp"), scatter_dimension=0, tiled=True),
        lax.psum_scatter(grad_skip, ("dp", "fsdp"), scatter_dimension=0, tiled=True),
        lax.psum_scatter(grad_bskip, ("dp", "fsdp"), scatter_dimension=0, tiled=True),
    )
    return (
        res_out[None],
        skip_out[None],
        grad_in[None],
        sums[0],
        sums[1],
        sums[2],
        sums[3],
        sums[4],
        sums[5],
        sums[6],
    )


def solution(mesh):
    return jax.shard_map(
        shards if dict(mesh.shape) == {"dp": 8, "fsdp": 4} else shards_any,
        mesh=mesh,
        in_specs=(
            P("fsdp", "dp", None),
            P("fsdp", None, "dp"),
            P("fsdp", None),
            P("fsdp"),
            P(None, ("dp", "fsdp"), None),
            P(None, ("dp", "fsdp")),
            P(("dp", "fsdp")),
            P(("dp", "fsdp"), None),
            P(("dp", "fsdp")),
            P(("dp", "fsdp"), None),
            P(("dp", "fsdp")),
            P("fsdp", "dp", None),
            P("fsdp", "dp", None),
        ),
        out_specs=(
            P("fsdp", "dp", None),
            P("fsdp", "dp", None),
            P("fsdp", "dp", None),
            P(None, ("dp", "fsdp"), None),
            P(None, ("dp", "fsdp")),
            P(("dp", "fsdp")),
            P(("dp", "fsdp"), None),
            P(("dp", "fsdp")),
            P(("dp", "fsdp"), None),
            P(("dp", "fsdp")),
        ),
        check_vma=False,
    )
```
